32 devices in a mesh: dp: 4 (over x, core), expert: 8 (over z, y).
Axes of the slice: x: 2, y: 2, z: 4, core: 2. Of those that a mesh axis runs over, the one named last changes fastest.
Arguments:
- block_input: bfloat16 [16384, 768], P(('dp', 'expert')), may hold values from -6 to 6
- cotangent: bfloat16 [16384, 768], P(('dp', 'expert')), may hold values from -6 to 6
- attn_in: bfloat16 [768, 2304], P(None, ('dp', 'expert')), may hold values from -0.21875 to 0.21875
- attn_out: bfloat16 [768, 768], P(None, ('dp', 'expert')), may hold values from -0.875 to 0.875
- router: bfloat16 [768, 16], P(('dp', 'expert')), may hold values from -0.21875 to 0.21875
- ln1_gain: bfloat16 [768], P(('dp', 'expert')), may hold values from 0.099609375 to 1.8984375
- ln1_bias: bfloat16 [768], P(('dp', 'expert')), may hold values from -3 to 3
- ln2_gain: bfloat16 [768], P(('dp', 'expert')), may hold values from 0.099609375 to 1.8984375
- ln2_bias: bfloat16 [768], P(('dp', 'expert')), may hold values from -3 to 3
- new_w1: bfloat16 [8, 768, 3072], P('expert', 'dp'), may hold values from -0.21875 to 0.21875
- new_w2: bfloat16 [8, 3072, 768], P('expert', 'dp'), may hold values from -1.75 to 1.75
- old_w1: bfloat16 [8, 768, 3072], P('expert', 'dp'), may hold values from -0.21875 to 0.21875
- old_w2: bfloat16 [8, 3072, 768], P('expert', 'dp'), may hold values from -1.75 to 1.75
- expert_ids: int32 [16384, 2], P(('dp', 'expert')), may hold values from 0 to 15, as said below
- slots: int32 [16384, 2], P(('dp', 'expert')), may hold values from 0 to 111, as said below
- drops: int32 [16384, 2], P(('dp', 'expert')), may hold values from 0 to 1, as said below
Outputs:
- mixed: bfloat16 [16384, 768], P(('dp', 'expert'))
- input_grad: float32 [16384, 768], P(('dp', 'expert'))
- attn_in_grad: float32 [768, 2304], P(None, ('dp', 'expert'))
- attn_out_grad: float32 [768, 768], P(None, ('dp', 'expert'))
- router_grad: float32 [768, 16], P(('dp', 'expert'))
- ln1_gain_grad: float32 [768], P(('dp', 'expert'))
- ln1_bias_grad: float32 [768], P(('dp', 'expert'))
- ln2_gain_grad: float32 [768], P(('dp', 'expert'))
- ln2_bias_grad: float32 [768], P(('dp', 'expert'))
- new_w1_grad: float32 [8, 768, 3072], P('expert', 'dp')
- new_w2_grad: float32 [8, 3072, 768], P('expert', 'dp')
The draws below stay inside these ranges and needn't reach their ends.
Inputs may be any that keep to these rules, and one draw needn't show every extreme that they name: `expert_ids`: each row names two different experts. Within the 512 rows of one device, the choices of one expert are counted in order of rows, first choice before second; a choice's slot is its count, and it is dropped when its count reaches 112, in which case its slot is 0. Every device fills all 112 slots of some expert, and one expert is full from every device. 1 exactly for the choices whose count reaches 112, as stated for slots; every device drops some.
All inputs are finite; a program needn't handle non-finite values.
Results may differ from the reference program's by a relative error of at most 0.015.
Values may be sent and summed in bfloat16 or wider, within the bound.
No kernel may reach another device: no remote copies, remote signals or barrier semaphores. Data moves between devices by JAX's collectives and lax.ppermute only.
A program may use at most 192 MiB of HBM per device.

```python
import jax
import jax.numpy as jnp
from jax import lax

D = 768
HEADS = 12
HEAD_DIM = 64
FF = 3072
TOK_DEV = 512
EXPERTS = 16
CAP = 112
TOKENS = 16384
N_DP = 4
N_EXPERT = 8


def routing_tables(key):
    base_key = jax.random.fold_in(key, 1729)
    first_key, second_key, offset_key, order_key, hot_key = jax.random.split(base_key, 5)
    first_draw = jax.random.randint(first_key, (TOKENS,), 0, EXPERTS)
    second_draw = jax.random.randint(second_key, (TOKENS,), 0, EXPERTS)
    ordering = jax.random.permutation(order_key, EXPERTS)
    favourite = ordering[jnp.minimum(first_draw, second_draw)]
    hottest = jax.random.randint(hot_key, (), 0, EXPERTS)
    position = jnp.arange(TOKENS, dtype=jnp.int32) % TOK_DEV
    favourite = jnp.where(position < CAP + CAP // 2, hottest, favourite)
    offsets = jax.random.randint(offset_key, (TOKENS,), 1, EXPERTS)
    runner = (favourite + offsets) % EXPERTS
    chosen = jnp.stack([favourite, runner], axis=1).astype(jnp.int32)
    blocked = chosen.reshape(TOKENS // TOK_DEV, TOK_DEV * 2)
    onehot = (blocked[:, :, None] == jnp.arange(EXPERTS, dtype=jnp.int32)[None, None, :]).astype(jnp.int32)
    running = jnp.cumsum(onehot, axis=1)
    ranking = (jnp.sum(running * onehot, axis=2) - 1).reshape(TOKENS, 2)
    dropped = (ranking >= CAP).astype(jnp.int32)
    placed = jnp.where(dropped == 1, 0, ranking).astype(jnp.int32)
    return (chosen, placed, dropped)


def draw_expert_ids(key, part):
    return routing_tables(key)[0]


def draw_slots(key, part):
    return routing_tables(key)[1]


def draw_drops(key, part):
    return routing_tables(key)[2]


def block_scale(stream_key, shape, cuts, least, high):
    level = 1.0
    for axis_at, shards_of in cuts:
        heights = jax.random.uniform(jax.random.fold_in(jax.random.fold_in(stream_key, 6), axis_at), (shards_of,), jnp.float32, least / len(cuts), high / len(cuts))
        level = level * jnp.repeat(jnp.exp(heights), shape[axis_at] // shards_of).reshape((-1,) + (1,) * (len(shape) - 1 - axis_at))
    return level


def scatter_about(stream_key, shape, deviation, bound, cuts=(), kind=jnp.bfloat16):
    entries = deviation * jax.random.normal(stream_key, shape, jnp.float32)
    if cuts:
        entries = entries * block_scale(stream_key, shape, cuts, -0.22, 0.18)
    return jnp.clip(entries, -bound, bound).astype(kind)


def setup_inputs(seed: int = 0) -> dict:
    arg_keys = jax.random.split(jax.random.key(seed), 17)
    block_input = scatter_about(arg_keys[0], (TOKENS, D), 1.0, 6.0, ((0, 32),))
    cotangent = scatter_about(arg_keys[1], (TOKENS, D), 1.0, 6.0, ((0, 32),))
    attn_in = scatter_about(arg_keys[2], (D, 3 * D), D ** -0.5, 0.21875, ((1, 32),))
    attn_out = scatter_about(arg_keys[3], (D, D), (D * 32 // TOK_DEV) ** -0.5, 0.875, ((1, 32),))
    router = scatter_about(arg_keys[4], (D, EXPERTS), D ** -0.5, 0.21875, ((0, 32),))
    ln1_gain = jnp.clip(1.0 + 0.18 * jax.random.normal(arg_keys[5], (D,), jnp.float32), 0.099609375, 1.8984375).astype(jnp.bfloat16)
    ln1_bias = scatter_about(arg_keys[6], (D,), 0.5, 3.0, ((0, 32),))
    ln2_gain = jnp.clip(1.0 + 0.18 * jax.random.normal(arg_keys[7], (D,), jnp.float32), 0.099609375, 1.8984375).astype(jnp.bfloat16)
    ln2_bias = scatter_about(arg_keys[8], (D,), 0.5, 3.0, ((0, 32),))
    new_w1 = scatter_about(arg_keys[9], (N_EXPERT, D, FF), D ** -0.5, 0.21875, ((0, 8), (1, 4)))
    new_w2 = scatter_about(arg_keys[10], (N_EXPERT, FF, D), (max(FF // 256, 1)) ** -0.5, 1.75, ((0, 8), (1, 4)))
    old_w1 = scatter_about(arg_keys[11], (N_EXPERT, D, FF), D ** -0.5, 0.21875, ((0, 8), (1, 4)))
    old_w2 = scatter_about(arg_keys[12], (N_EXPERT, FF, D), (max(FF // 256, 1)) ** -0.5, 1.75, ((0, 8), (1, 4)))
    expert_ids = draw_expert_ids(jax.random.fold_in(arg_keys[16], 71), 0)
    slots = draw_slots(jax.random.fold_in(arg_keys[16], 71), 0)
    drops = draw_drops(jax.random.fold_in(arg_keys[16], 71), 0)
    return {"block_input": block_input, "cotangent": cotangent, "attn_in": attn_in, "attn_out": attn_out, "router": router, "ln1_gain": ln1_gain, "ln1_bias": ln1_bias, "ln2_gain": ln2_gain, "ln2_bias": ln2_bias, "new_w1": new_w1, "new_w2": new_w2, "old_w1": old_w1, "old_w2": old_w2, "expert_ids": expert_ids, "slots": slots, "drops": drops}


@jax.custom_vjp
def low(v):
    return lax.optimization_barrier(v.astype(jnp.bfloat16)).astype(jnp.float32)

@jax.custom_vjp
def low_back(v):
    return v

def low_keep(v):
    return (low(v), None)

def low_pass(kept, grad):
    return (grad,)

def back_keep(v):
    return (v, None)

def back_low(kept, grad):
    return (low(grad),)
low.defvjp(low_keep, low_pass)
low_back.defvjp(back_keep, back_low)

def layer_norm(values, scale_gain, shift_bias):
    centre = values - lax.optimization_barrier(jnp.mean(values, axis=-1, keepdims=True))
    spread = lax.optimization_barrier(jnp.mean(centre * centre, axis=-1, keepdims=True))
    return centre * lax.rsqrt(spread + 1e-05) * scale_gain + shift_bias

def matmul(left, right):
    return jnp.dot(left, right, precision=lax.Precision.HIGHEST)

def attend(sequence):
    length = sequence.shape[0]
    pieces = sequence.reshape(length, 3, HEADS, HEAD_DIM)
    queries, keys_all, values = (pieces[:, 0], pieces[:, 1], pieces[:, 2])
    scores = jnp.einsum('qhd,khd->hqk', queries, keys_all, precision=lax.Precision.HIGHEST) * HEAD_DIM ** (-0.5)
    scores = low_back(scores)
    rowpos = lax.broadcasted_iota(jnp.int32, (length, length), 0)
    colpos = lax.broadcasted_iota(jnp.int32, (length, length), 1)
    scores = jnp.where((rowpos >= colpos)[None], scores, -1e+30)
    weights = low(jax.nn.softmax(scores, axis=-1))
    context = jnp.einsum('hqk,khd->qhd', weights, values, precision=lax.Precision.HIGHEST)
    return context.reshape(length, HEADS * HEAD_DIM)

def expert_rows(items):
    block_rows, upward, downward = items
    preact = low_back(matmul(block_rows, upward))
    hidden = low(jax.nn.gelu(preact))
    return low_back(low(matmul(hidden, downward)))

def reference(block_input, cotangent, attn_in, attn_out, router, ln1_gain, ln1_bias, ln2_gain, ln2_bias, new_w1, new_w2, old_w1, old_w2, expert_ids, slots, drops):
    devices_all = N_DP * N_EXPERT
    kept_mask = (1 - drops).astype(jnp.float32)
    source = (jnp.arange(TOKENS, dtype=jnp.int32) // TOK_DEV)[:, None]
    target = ((source * EXPERTS + expert_ids) * CAP + slots).astype(jnp.int32)
    flat_target = target.reshape(-1)
    choose = (expert_ids[:, :, None] == jnp.arange(EXPERTS, dtype=jnp.int32)[None, None, :]).astype(jnp.float32)
    old_up = old_w1.astype(jnp.float32)
    old_down = old_w2.astype(jnp.float32)

    def forward(inputs, w_in, w_out, w_router, gain_one, bias_one, gain_two, bias_two, new_up, new_down):
        normed_one = low(layer_norm(inputs, gain_one, bias_one))
        projected = low_back(low(matmul(normed_one, w_in)))
        context = lax.map(jax.checkpoint(attend), projected.reshape(-1, TOK_DEV, 3 * D)).reshape(TOKENS, D)
        context = low_back(low(context))
        middle = inputs + low_back(matmul(context, w_out))
        normed_two = low(layer_norm(middle, gain_two, bias_two))
        route_probs = jax.nn.softmax(low_back(matmul(normed_two, w_router)), axis=-1)
        gate_values = lax.optimization_barrier(jnp.sum(choose * route_probs[:, None, :], axis=-1)) * kept_mask
        placed = (normed_two[:, None, :] * kept_mask[:, :, None]).reshape(-1, D)
        buffers = jnp.zeros((devices_all * EXPERTS * CAP, D), jnp.float32).at[flat_target].add(placed)
        buffers = low_back(buffers)
        grouped = buffers.reshape(devices_all, EXPERTS, CAP, D).transpose(1, 0, 2, 3).reshape(EXPERTS, devices_all * CAP, D)
        all_up = jnp.stack([old_up, new_up], axis=1).reshape(EXPERTS, D, FF)
        all_down = jnp.stack([old_down, new_down], axis=1).reshape(EXPERTS, FF, D)
        produced = lax.map(jax.checkpoint(expert_rows), (grouped, all_up, all_down))
        landed = produced.reshape(EXPERTS, devices_all, CAP, D).transpose(1, 0, 2, 3).reshape(-1, D)
        picked = landed[flat_target].reshape(TOKENS, 2, D)
        return middle + lax.optimization_barrier(jnp.sum(gate_values[:, :, None] * picked, axis=1))
    result, pullback = jax.vjp(forward, block_input.astype(jnp.float32), attn_in.astype(jnp.float32), attn_out.astype(jnp.float32), router.astype(jnp.float32), ln1_gain.astype(jnp.float32), ln1_bias.astype(jnp.float32), ln2_gain.astype(jnp.float32), ln2_bias.astype(jnp.float32), new_w1.astype(jnp.float32), new_w2.astype(jnp.float32))
    grads = pullback(cotangent.astype(jnp.float32))
    return (result.astype(jnp.bfloat16), grads[0], grads[1], grads[2], grads[3], grads[4], grads[5], grads[6], grads[7], grads[8], grads[9])
```

```python
import functools

import jax
import jax.numpy as jnp
from jax import lax
from jax.experimental import pallas as pl
from jax.experimental.pallas import tpu as pltpu
from jax.sharding import PartitionSpec as P

HEADS = 12
HEAD_DIM = 64
BF = jnp.bfloat16
F32 = jnp.float32


def mm(a, b, dims, out=F32):
    return lax.dot_general(a, b, (dims, ((), ())), preferred_element_type=F32).astype(out)


def powers(count):
    found = []
    bit = 1
    while bit < count:
        found.append(bit)
        bit *= 2
    return found


def swap(values, axis, bit):
    count = lax.axis_size(axis)
    return lax.ppermute(values, axis, [(i, i ^ bit) for i in range(count)])


def my_bit(axis, bit):
    return (lax.axis_index(axis) // bit) % 2


def canonical():
    return [("dp", b) for b in reversed(powers(lax.axis_size("dp")))] + [
        ("expert", b) for b in reversed(powers(lax.axis_size("expert")))
    ]


def orders():
    dp_bits = powers(lax.axis_size("dp"))
    expert_bits = powers(lax.axis_size("expert"))
    core = [("dp", dp_bits[0])]
    xs = [("dp", b) for b in reversed(dp_bits[1:])]
    ys = [("expert", expert_bits[0])]
    zs = [("expert", b) for b in reversed(expert_bits[1:])]
    return (zs + ys + xs + core, xs + zs + ys + core, ys + xs + zs + core)


def gather_blocks(block, order):
    lead = []
    current = block
    for axis, bit in order:
        other = swap(current, axis, bit)
        low = my_bit(axis, bit) == 0
        current = jnp.stack([jnp.where(low, current, other), jnp.where(low, other, current)])
        lead.insert(0, (axis, bit))
    want = canonical()
    tail = list(range(len(lead), len(lead) + block.ndim))
    current = current.transpose([lead.index(w) for w in want] + tail)
    return current.reshape((-1,) + block.shape[1:])


def scatter_blocks(values, order):
    lead = canonical()
    current = values.reshape([2] * len(lead) + [-1] + list(values.shape[1:]))
    for axis, bit in reversed(order):
        at = lead.index((axis, bit))
        mine = my_bit(axis, bit)
        keep = lax.dynamic_index_in_dim(current, mine, at, keepdims=False)
        send = lax.dynamic_index_in_dim(current, 1 - mine, at, keepdims=False)
        got = swap(send.astype(BF), axis, bit)
        current = keep.astype(F32) + got.astype(F32)
        lead.pop(at)
    return current


def gather_dp(shard):
    dp_bits = powers(lax.axis_size("dp"))
    current = shard
    order = [("dp", b) for b in reversed(dp_bits)]
    lead = []
    for axis, bit in order:
        other = swap(current, axis, bit)
        low = my_bit(axis, bit) == 0
        current = jnp.stack([jnp.where(low, current, other), jnp.where(low, other, current)])
        lead.insert(0, (axis, bit))
    tail = list(range(len(lead), len(lead) + shard.ndim))
    current = current.transpose([lead.index(w) for w in order] + tail)
    return current.reshape((-1,) + shard.shape[1:])


def scatter_dp(values):
    dp_bits = powers(lax.axis_size("dp"))
    lead = [("dp", b) for b in reversed(dp_bits)]
    current = values.reshape([2] * len(lead) + [-1] + list(values.shape[1:]))
    for axis, bit in [("dp", b) for b in dp_bits]:
        at = lead.index((axis, bit))
        mine = my_bit(axis, bit)
        keep = lax.dynamic_index_in_dim(current, mine, at, keepdims=False)
        send = lax.dynamic_index_in_dim(current, 1 - mine, at, keepdims=False)
        got = swap(send.astype(BF), axis, bit)
        current = keep.astype(F32) + got.astype(F32)
        lead.pop(at)
    return current


LIMIT = 56 * 1024 * 1024
QUERY_BLOCK = 128
SCALE = HEAD_DIM ** (-0.5)


def dot(a, b, over_a, over_b):
    return lax.dot_general(
        a, b, (((over_a,), (over_b,)), ((), ())), preferred_element_type=F32
    )


def whole(array):
    return jax.ShapeDtypeStruct(array[0], array[1])


def plain_call(body, outs, scratch, name, *args):
    space = pl.BlockSpec(memory_space=pltpu.VMEM)
    return pl.pallas_call(
        body,
        out_shape=[whole(o) for o in outs],
        in_specs=[space] * len(args),
        out_specs=[space] * len(outs),
        scratch_shapes=scratch,
        compiler_params=pltpu.CompilerParams(vmem_limit_bytes=LIMIT),
        name=name,
    )(*args)


def norm_parts(values):
    centre = values - jnp.mean(values, axis=-1, keepdims=True)
    spread = jnp.mean(centre * centre, axis=-1, keepdims=True)
    scale = lax.rsqrt(spread + 1e-05)
    return centre * scale, scale


def norm_back(values, gain, grad):
    normal, scale = norm_parts(values)
    scaled = grad * gain
    back = scale * (
        scaled
        - jnp.mean(scaled, axis=-1, keepdims=True)
        - normal * jnp.mean(scaled * normal, axis=-1, keepdims=True)
    )
    return back, jnp.sum(grad * normal, axis=0, keepdims=True), jnp.sum(grad, axis=0, keepdims=True)


def place_rows(target_ref, values, first, count):
    tokens = values.shape[0]
    at = lax.broadcasted_iota(jnp.int32, (count, tokens), 0) + first
    hit = (at == target_ref[0:1, :]) | (at == target_ref[1:2, :])
    return dot(hit.astype(F32).astype(BF), values, 1, 0).astype(BF)


def place_kernel(target_ref, values_ref, old_ref, new_ref):
    values = values_ref[...]
    count = old_ref.shape[0]
    half = count // 2
    for at, ref in ((0, old_ref), (count, new_ref)):
        for part in range(2):
            ref[part * half : (part + 1) * half, :] = place_rows(
                target_ref, values, at + part * half, half
            )


def take_rows(target_ref, slots_refs, tokens):
    total = None
    first = 0
    for ref in slots_refs:
        count = ref.shape[0]
        at = lax.broadcasted_iota(jnp.int32, (tokens, count), 1) + first
        hit = (at == target_ref[:, 0:1]) | (at == target_ref[:, 1:2])
        part = dot(hit.astype(F32).astype(BF), ref[...], 1, 0)
        total = part if total is None else total + part
        first += count
    return total


def causal(size):
    rowpos = lax.broadcasted_iota(jnp.int32, (size, size), 0)
    colpos = lax.broadcasted_iota(jnp.int32, (size, size), 1)
    return rowpos >= colpos


def head_lanes(block, which):
    lane = lax.broadcasted_iota(jnp.int32, block.shape, 1)
    keep = (lane < HEAD_DIM) if which == 0 else (lane >= HEAD_DIM)
    return jnp.where(keep, block, jnp.zeros_like(block))


def block_softmax(query, keys, seen):
    size = query.shape[0]
    before = keys.shape[0] - size
    own = dot(query, keys[before:], 1, 1)
    own = jnp.where(seen, own, -1e30)
    top = jnp.max(own, axis=-1, keepdims=True)
    if before:
        past = dot(query, keys[:before], 1, 1)
        top = jnp.maximum(top, jnp.max(past, axis=-1, keepdims=True))
        past = jnp.exp(past - top)
    own = jnp.exp(own - top)
    total = jnp.sum(own, axis=-1, keepdims=True)
    if before:
        total = total + jnp.sum(past, axis=-1, keepdims=True)
    inverse = 1.0 / total
    own = own * inverse
    return (past * inverse, own) if before else (own,)


def pair_columns(pair, part, width):
    return pl.ds(pl.multiple_of(part * width + pair * 2 * HEAD_DIM, 2 * HEAD_DIM), 2 * HEAD_DIM)


def forward_kernel(
    x_ref,
    in_ref,
    out_ref,
    vec_ref,
    target_ref,
    normed_ref,
    proj_ref,
    context_ref,
    middle_ref,
    old_ref,
    new_ref,
):
    length, width = x_ref.shape
    x = x_ref[...].astype(F32)
    normal, _ = norm_parts(x)
    normed = (normal * vec_ref[0:1, :] + vec_ref[1:2, :]).astype(BF)
    normed_ref[...] = normed
    for part in range(3):
        cols = slice(part * width, (part + 1) * width)
        proj_ref[:, cols] = dot(normed, in_ref[cols, :], 1, 1).astype(BF)
    size = min(QUERY_BLOCK, length)
    seen = causal(size)

    def one_pair(pair, carry):
        q_at, k_at, v_at = (pair_columns(pair, part, width) for part in range(3))
        for block in range(length // size):
            rows = slice(block * size, (block + 1) * size)
            upto = (block + 1) * size
            query = proj_ref[rows, q_at] * BF(SCALE)
            keys = proj_ref[0:upto, k_at]
            values = proj_ref[0:upto, v_at]
            outs = []
            for which in range(2):
                probs = block_softmax(head_lanes(query, which), keys, seen)
                probs = [p.astype(BF) for p in probs]
                out = dot(probs[-1], values[upto - size :], 1, 0)
                if len(probs) > 1:
                    out = out + dot(probs[0], values[: upto - size], 1, 0)
                outs.append(out)
            lane = lax.broadcasted_iota(jnp.int32, outs[0].shape, 1)
            context_ref[rows, pair_columns(pair, 0, width)] = jnp.where(
                lane < HEAD_DIM, outs[0], outs[1]
            ).astype(BF)
        return carry

    lax.fori_loop(0, HEADS // 2, one_pair, 0)
    middle = x + dot(context_ref[...], out_ref[...], 1, 1)
    middle_ref[...] = middle
    normal, _ = norm_parts(middle)
    normed_two = (normal * vec_ref[2:3, :] + vec_ref[3:4, :]).astype(BF)
    count = old_ref.shape[0]
    half = count // 2
    for at, ref in ((0, old_ref), (count, new_ref)):
        for part in range(2):
            ref[part * half : (part + 1) * half, :] = place_rows(
                target_ref, normed_two, at + part * half, half
            )


def branch_kernel(
    old_ref,
    new_ref,
    target_ref,
    cot_ref,
    middle_ref,
    context_ref,
    out_ref,
    vec_ref,
    gmid_ref,
    gctx_ref,
    og0_ref,
    og1_ref,
    og2_ref,
    sums_ref,
):
    length, width = cot_ref.shape
    grad = take_rows(target_ref, (old_ref, new_ref), length)
    back, gain_sum, bias_sum = norm_back(middle_ref[...], vec_ref[2:3, :], grad)
    gmid = back + cot_ref[...].astype(F32)
    gmid_ref[...] = gmid
    sums_ref[...] = jnp.concatenate([gain_sum, bias_sum, jnp.zeros((6, width), F32)], axis=0)
    branch = gmid.astype(BF)
    gctx_ref[...] = dot(branch, out_ref[...], 1, 0).astype(BF)
    third = width // 3
    for part, ref in enumerate((og0_ref, og1_ref, og2_ref)):
        ref[...] = dot(branch, context_ref[:, part * third : (part + 1) * third], 0, 0).astype(BF)


def attention_back_kernel(
    proj_ref, gctx_ref, normed_ref, gproj_ref, ig0_ref, ig1_ref, ig2_ref, gk_acc, gv_acc
):
    length, width = gctx_ref.shape
    size = min(QUERY_BLOCK, length)
    seen = causal(size)

    def one_pair(pair, carry):
        q_at, k_at, v_at = (pair_columns(pair, part, width) for part in range(3))
        gk_acc[...] = jnp.zeros_like(gk_acc)
        gv_acc[...] = jnp.zeros_like(gv_acc)
        for block in range(length // size):
            rows = slice(block * size, (block + 1) * size)
            upto = (block + 1) * size
            query = proj_ref[rows, q_at] * BF(SCALE)
            keys = proj_ref[0:upto, k_at]
            values = proj_ref[0:upto, v_at]
            gout = gctx_ref[rows, pair_columns(pair, 0, width)]
            grads = []
            for which in range(2):
                mine = head_lanes(query, which)
                gmine = head_lanes(gout, which)
                probs = block_softmax(mine, keys, seen)
                spans = [slice(upto - size, upto)]
                if len(probs) > 1:
                    spans = [slice(0, upto - size)] + spans
                gprobs = [dot(gmine, values[s], 1, 1) for s in spans]
                row = sum(jnp.sum(p * g, axis=-1, keepdims=True) for p, g in zip(probs, gprobs))
                gquery = None
                for p, g, s in zip(probs, gprobs, spans):
                    gscore = (p * (g - row)).astype(BF)
                    part = dot(gscore, keys[s], 1, 0)
                    gquery = part if gquery is None else gquery + part
                    gk_acc[s, :] += dot(gscore, mine, 0, 0)
                    gv_acc[s, :] += dot(p.astype(BF), gmine, 0, 0)
                grads.append(gquery * SCALE)
            lane = lax.broadcasted_iota(jnp.int32, grads[0].shape, 1)
            gproj_ref[rows, q_at] = jnp.where(lane < HEAD_DIM, grads[0], grads[1]).astype(BF)
        gproj_ref[:, k_at] = gk_acc[...].astype(BF)
        gproj_ref[:, v_at] = gv_acc[...].astype(BF)
        return carry

    lax.fori_loop(0, HEADS // 2, one_pair, 0)
    third = width // 3
    for part, ref in enumerate((ig0_ref, ig1_ref, ig2_ref)):
        ref[...] = dot(
            gproj_ref[...], normed_ref[:, part * third : (part + 1) * third], 0, 0
        ).astype(BF)


def input_kernel(gproj_ref, in_ref, x_ref, vec_ref, gmid_ref, grad_ref, sums_ref):
    grad = dot(gproj_ref[...], in_ref[...], 1, 0)
    back, gain_sum, bias_sum = norm_back(x_ref[...].astype(F32), vec_ref[0:1, :], grad)
    grad_ref[...] = gmid_ref[...] + back
    width = x_ref.shape[1]
    sums_ref[...] = jnp.concatenate([gain_sum, bias_sum, jnp.zeros((6, width), F32)], axis=0)


def mixed_kernel(old_ref, new_ref, target_ref, middle_ref, mixed_ref):
    total = take_rows(target_ref, (old_ref, new_ref), middle_ref.shape[0])
    mixed_ref[...] = (middle_ref[...] + total).astype(BF)


def gelu_pair(x):
    c = 0.7978845608028654
    sq = x * x
    t = jnp.tanh(c * x * (1.0 + 0.044715 * sq))
    half = 0.5 * (1.0 + t)
    slope = half + 0.5 * x * (1.0 - t * t) * (c * (1.0 + 3 * 0.044715 * sq))
    return x * half, slope

def expert_kernel(train, steps, mine_ref, rows_ref, grads_ref, router_ref, up_ref, down_ref, *rest):
    if train:
        gated_ref, gin_ref, rgrad_ref, dup_ref, ddown_ref, out_acc, gin_acc, scaled, gate_s, probs_s = rest
    else:
        gated_ref, gin_ref, rgrad_ref, out_acc, gin_acc, scaled, gate_s, probs_s = rest
    j = pl.program_id(0)
    mine = mine_ref[0:1, :]

    @pl.when(j == 0)
    def _():
        logits = dot(rows_ref[...], router_ref[...], 1, 0)
        live = lax.broadcasted_iota(jnp.int32, logits.shape, 1) < mine_ref[1, 0].astype(jnp.int32)
        logits = jnp.where(live, logits, -1e30)
        e = jnp.exp(logits - jnp.max(logits, axis=1, keepdims=True))
        probs = e / jnp.sum(e, axis=1, keepdims=True)
        probs_s[...] = probs
        gate = jnp.sum(probs * mine, axis=1, keepdims=True)
        gate_s[...] = jnp.broadcast_to(gate, gate_s.shape)
        scaled[...] = (grads_ref[...].astype(F32) * gate).astype(BF)

    rows = rows_ref[...]
    up = up_ref[...]
    down = down_ref[...]
    pre = dot(rows, up, 1, 0)
    hid, slope = gelu_pair(pre)
    hid = hid.astype(BF)
    gh = dot(scaled[...], down, 1, 1)
    gpre = (gh * slope).astype(BF)
    o = dot(hid, down, 1, 0)
    gi = dot(gpre, up, 1, 1)

    @pl.when(j == 0)
    def _():
        out_acc[...] = o
        gin_acc[...] = gi

    @pl.when(j > 0)
    def _():
        out_acc[...] += o
        gin_acc[...] += gi

    if train:
        dup_ref[...] = dot(rows, gpre, 0, 0).astype(BF)
        ddown_ref[...] = dot(hid, scaled[...], 0, 0).astype(BF)

    @pl.when(j == steps - 1)
    def _():
        produced = out_acc[...].astype(BF).astype(F32)
        gate = gate_s[:, 0:1]
        gated_ref[...] = (produced * gate).astype(BF)
        grad_gate = jnp.sum(produced * grads_ref[...].astype(F32), axis=1, keepdims=True)
        gl = (grad_gate * gate * (mine - probs_s[...])).astype(BF)
        gin_ref[...] = (gin_acc[...] + dot(gl, router_ref[...], 1, 1)).astype(BF)
        rgrad_ref[...] = dot(gl, rows_ref[...], 0, 0)

def expert_call(mine, rows, grads, router_pad, up, down, train, ft=768, limit=LIMIT):
    n, d = rows.shape
    f = up.shape[1]
    steps = f // ft
    one = pl.Buffered(buffer_count=1)
    whole = lambda s: pl.BlockSpec(s, lambda j: (0, 0), pipeline_mode=one)
    outs = [jax.ShapeDtypeStruct((n, d), BF), jax.ShapeDtypeStruct((n, d), BF), jax.ShapeDtypeStruct((128, d), F32)]
    out_specs = [whole((n, d)), whole((n, d)), whole((128, d))]
    if train:
        outs += [jax.ShapeDtypeStruct((d, f), BF), jax.ShapeDtypeStruct((f, d), BF)]
        out_specs += [pl.BlockSpec((d, ft), lambda j: (0, j)), pl.BlockSpec((ft, d), lambda j: (j, 0))]
    return pl.pallas_call(
        functools.partial(expert_kernel, train, steps),
        grid=(steps,),
        in_specs=[whole((8, 128)), whole((n, d)), whole((n, d)), whole((d, 128)),
                  pl.BlockSpec((d, ft), lambda j: (0, j)), pl.BlockSpec((ft, d), lambda j: (j, 0))],
        out_specs=out_specs, out_shape=outs,
        scratch_shapes=[pltpu.VMEM((n, d), F32), pltpu.VMEM((n, d), F32), pltpu.VMEM((n, d), BF), pltpu.VMEM((n, 128), F32), pltpu.VMEM((n, 128), F32)],
        compiler_params=pltpu.CompilerParams(vmem_limit_bytes=limit),
        name="expert_new" if train else "expert_old",
    )(mine, rows, grads, router_pad, up, down)


def shards(
    block_input,
    cotangent,
    attn_in,
    attn_out,
    router,
    ln1_gain,
    ln1_bias,
    ln2_gain,
    ln2_bias,
    new_w1,
    new_w2,
    old_w1,
    old_w2,
    expert_ids,
    slots,
    drops,
):
    length, width = block_input.shape
    peers = lax.axis_size("expert")
    devices = lax.axis_size("dp") * peers
    experts = 2 * peers
    capacity = max(length * 7 // (2 * experts), 2)
    me = lax.axis_index("expert")
    ways = orders()
    third = width // 3
    in_share = attn_in.shape[1]
    share = width // devices
    router_size = router.size

    small = jnp.concatenate(
        [router.reshape(-1), ln1_gain, ln1_bias, ln2_gain, ln2_bias]
    )
    used = small.size
    lines = -(-used // width)
    small = jnp.pad(small, (0, lines * width - used)).reshape(lines, width)
    packed = jnp.concatenate([attn_in.T, attn_out.T, small], axis=0)
    packed = jnp.pad(packed, ((0, -packed.shape[0] % 8), (0, 0)))
    parts = [
        gather_blocks(packed[:, p * third : (p + 1) * third], ways[p]).reshape(
            devices, packed.shape[0], third
        )
        for p in range(3)
    ]
    full = jnp.concatenate(parts, axis=2)
    in_full = full[:, :in_share].reshape(3 * width, width)
    out_full = full[:, in_share : in_share + share].reshape(width, width)
    small_full = full[:, in_share + share : in_share + share + lines].reshape(devices, -1)
    router_full = small_full[:, :router_size].reshape(width, experts)
    router_pad = jnp.pad(router_full, ((0, 0), (0, 128 - experts)))
    vectors = small_full[:, router_size:used].reshape(devices, 4, share).transpose(1, 0, 2)
    vectors = jnp.pad(vectors.reshape(4, width).astype(F32), ((0, 4), (0, 0)))

    (old_w1, old_w2, new_w1, new_w2), parts = lax.optimization_barrier(
        ((old_w1, old_w2, new_w1, new_w2), parts)
    )
    old_up = gather_dp(old_w1[0])
    old_down = gather_dp(old_w2[0])
    new_up = gather_dp(new_w1[0])
    new_down = gather_dp(new_w2[0])

    target = ((expert_ids % 2) * peers + expert_ids // 2) * capacity + slots
    target = jnp.where(drops == 0, target, -1)
    target_rows = jnp.pad(target.T, ((0, 6), (0, 0)), constant_values=-1)
    count = peers * capacity

    def send(block):
        block = block.reshape(peers, capacity, width)
        moved = lax.all_to_all(block, "expert", split_axis=0, concat_axis=0, tiled=True)
        return moved.reshape(count, width)

    slot_outs = [((count, width), BF)] * 2
    gold, gnew = plain_call(place_kernel, slot_outs, [], "place_grads", target_rows, cotangent)
    gold = send(gold)
    gnew = send(gnew)

    normed, proj, context, middle, rold, rnew = plain_call(
        forward_kernel,
        [
            ((length, width), BF),
            ((length, 3 * width), BF),
            ((length, width), BF),
            ((length, width), F32),
        ]
        + slot_outs,
        [],
        "attention_forward",
        block_input,
        in_full,
        out_full,
        vectors,
        target_rows,
    )
    rold = send(rold)
    rnew = send(rnew)

    lane = lax.broadcasted_iota(jnp.int32, (8, 128), 1)
    line = lax.broadcasted_iota(jnp.int32, (8, 128), 0)

    def chosen(expert):
        return jnp.where(line == 0, (lane == expert).astype(F32), F32(experts))

    old_gated, old_in, old_router = expert_call(
        chosen(2 * me), rold, gold, router_pad, old_up, old_down, False
    )
    old_in = send(old_in)
    new_gated, new_in, new_router, grad_up, grad_down = expert_call(
        chosen(2 * me + 1), rnew, gnew, router_pad, new_up, new_down, True
    )
    new_in = send(new_in)
    old_gated = send(old_gated)
    new_gated = send(new_gated)
    new_w1_grad = scatter_dp(grad_up)[None]
    new_w2_grad = scatter_dp(grad_down)[None]
    router_part = (old_router + new_router)[:experts].T

    gmid, gctx, og0, og1, og2, sums_two = plain_call(
        branch_kernel,
        [((length, width), F32), ((length, width), BF)]
        + [((width, third), BF)] * 3
        + [((8, width), F32)],
        [],
        "branch_backward",
        old_in,
        new_in,
        target,
        cotangent,
        middle,
        context,
        out_full,
        vectors,
    )
    attn_out_grad = jnp.concatenate(
        [scatter_blocks(og, way) for og, way in zip((og0, og1, og2), ways)], axis=1
    ).T
    gproj, ig0, ig1, ig2 = plain_call(
        attention_back_kernel,
        [((length, 3 * width), BF)] + [((3 * width, third), BF)] * 3,
        [pltpu.VMEM((length, 2 * HEAD_DIM), F32)] * 2,
        "attention_backward",
        proj,
        gctx,
        normed,
    )
    attn_in_grad = jnp.concatenate(
        [scatter_blocks(ig, way) for ig, way in zip((ig0, ig1, ig2), ways)], axis=1
    ).T
    input_grad, sums_one = plain_call(
        input_kernel,
        [((length, width), F32), ((8, width), F32)],
        [],
        "input_backward",
        gproj,
        in_full,
        block_input,
        vectors,
        gmid,
    )
    (mixed,) = plain_call(
        mixed_kernel,
        [((length, width), BF)],
        [],
        "mixed_output",
        old_gated,
        new_gated,
        target,
        middle,
    )
    vector_grads = jnp.concatenate([sums_one[:2], sums_two[:2]], axis=0)
    vector_grads = vector_grads.reshape(4, devices, share).transpose(1, 0, 2)
    small_grads = jnp.concatenate(
        [router_part.reshape(devices, -1), vector_grads.reshape(devices, -1)], axis=1
    )
    small_grads = scatter_blocks(small_grads, ways[1]).reshape(-1)
    router_grad = small_grads[:router_size].reshape(share, experts)
    vector_grads = small_grads[router_size:].reshape(4, share)
    return (
        mixed,
        input_grad,
        attn_in_grad,
        attn_out_grad,
        router_grad,
        vector_grads[0],
        vector_grads[1],
        vector_grads[2],
        vector_grads[3],
        new_w1_grad,
        new_w2_grad,
    )


def solution(mesh):
    both = ("dp", "expert")
    rows = P(both, None)
    columns = P(None, both)
    vector = P(both)
    weight = P("expert", "dp", None)
    in_specs = (
        [rows, rows, columns, columns, rows] + [vector] * 4 + [weight] * 4 + [rows] * 3
    )
    out_specs = [rows, rows, columns, columns, rows] + [vector] * 4 + [weight] * 2
    return jax.shard_map(
        shards, mesh=mesh, in_specs=tuple(in_specs), out_specs=tuple(out_specs), check_vma=False
    )
```

```python
import functools

import jax
import jax.numpy as jnp
from jax import lax
from jax.experimental import pallas as pl
from jax.experimental.pallas import tpu as pltpu
from jax.sharding import PartitionSpec as P

HEADS = 12
HEAD_DIM = 64
BF = jnp.bfloat16
F32 = jnp.float32


def mm(a, b, dims, out=F32):
    return lax.dot_general(a, b, (dims, ((), ())), preferred_element_type=F32).astype(out)


def powers(count):
    found = []
    bit = 1
    while bit < count:
        found.append(bit)
        bit *= 2
    return found


def swap(values, axis, bit):
    count = lax.axis_size(axis)
    return lax.ppermute(values, axis, [(i, i ^ bit) for i in range(count)])


def my_bit(axis, bit):
    return (lax.axis_index(axis) // bit) % 2


def canonical():
    return [("dp", b) for b in reversed(powers(lax.axis_size("dp")))] + [
        ("expert", b) for b in reversed(powers(lax.axis_size("expert")))
    ]


def orders():
    dp_bits = powers(lax.axis_size("dp"))
    expert_bits = powers(lax.axis_size("expert"))
    core = [("dp", dp_bits[0])]
    xs = [("dp", b) for b in reversed(dp_bits[1:])]
    ys = [("expert", expert_bits[0])]
    zs = [("expert", b) for b in reversed(expert_bits[1:])]
    gathering = (zs + ys + xs + core, xs + zs + ys + core, ys + xs + zs + core)
    near = zs[::-1]
    summing = (xs + ys + near, ys + near + xs, near + xs + ys, near + ys + xs)
    return gathering, summing


def gather_steps(state, order):
    current, lead = state
    lead = list(lead)
    for axis, bit in order:
        other = swap(current, axis, bit)
        low = my_bit(axis, bit) == 0
        current = jnp.stack([jnp.where(low, current, other), jnp.where(low, other, current)])
        lead.insert(0, (axis, bit))
    return current, lead


def gather_finish(state):
    current, lead = state
    tail = current.shape[len(lead) :]
    perm = [lead.index(w) for w in canonical()]
    current = current.transpose(perm + list(range(len(lead), current.ndim)))
    return current.reshape((-1,) + tail)


def after(values, *earlier):
    if not earlier:
        return values
    return lax.optimization_barrier((values, earlier))[0]


def scatter_steps(state, order):
    current, lead = state
    lead = list(lead)
    for axis, bit in order:
        at = lead.index((axis, bit))
        mine = my_bit(axis, bit)
        keep = lax.dynamic_index_in_dim(current, mine, at, keepdims=False)
        send = lax.dynamic_index_in_dim(current, 1 - mine, at, keepdims=False)
        got = swap(send.astype(BF), axis, bit)
        current = keep.astype(F32) + got.astype(F32)
        lead.pop(at)
    return current, lead


def dp_pieces(shard, first, second):
    bits = powers(lax.axis_size("dp"))
    found = {0: shard, bits[0]: swap(after(shard, *first), "dp", bits[0])}
    far = {}
    for bit in bits[1:]:
        for away, piece in [(0, after(shard, *first)), *far.items()]:
            far[away ^ bit] = swap(piece, "dp", bit)
    for away, piece in far.items():
        found[away] = piece
        found[away ^ bits[0]] = swap(after(piece, *second), "dp", bits[0])
    return [found[away] for away in range(len(found))], far


def scatter_dp(keep, send):
    bits = powers(lax.axis_size("dp"))
    total = keep.astype(F32) + swap(send, "dp", bits[0]).astype(F32)
    order = [("dp", b) for b in bits[1:]]
    total = total.reshape([2] * len(order) + list(total.shape[1:]))
    return scatter_steps((total, order[::-1]), order)[0]


LIMIT = 56 * 1024 * 1024
QUERY_BLOCK = 128
SCALE = HEAD_DIM ** (-0.5)


def dot(a, b, over_a, over_b):
    return lax.dot_general(
        a, b, (((over_a,), (over_b,)), ((), ())), preferred_element_type=F32
    )


def dot_parts(values, parts):
    width = parts[0].shape[1]
    total = None
    for at, part in enumerate(parts):
        term = dot(values[:, at * width : (at + 1) * width], part, 1, 1)
        total = term if total is None else total + term
    return total


def whole(array):
    return jax.ShapeDtypeStruct(array[0], array[1])


def cost(micros):
    return pl.CostEstimate(flops=int(micros * 0.25e9), bytes_accessed=0, transcendentals=0)


def plain_call(body, outs, scratch, name, micros, *args):
    space = pl.BlockSpec(memory_space=pltpu.VMEM)
    return pl.pallas_call(
        body,
        out_shape=[whole(o) for o in outs],
        in_specs=[space] * len(args),
        out_specs=[space] * len(outs),
        scratch_shapes=scratch,
        compiler_params=pltpu.CompilerParams(vmem_limit_bytes=LIMIT),
        cost_estimate=cost(micros),
        name=name,
    )(*args)


def norm_parts(values):
    centre = values - jnp.mean(values, axis=-1, keepdims=True)
    spread = jnp.mean(centre * centre, axis=-1, keepdims=True)
    scale = lax.rsqrt(spread + 1e-05)
    return centre * scale, scale


def norm_back(values, gain, grad):
    normal, scale = norm_parts(values)
    scaled = grad * gain
    back = scale * (
        scaled
        - jnp.mean(scaled, axis=-1, keepdims=True)
        - normal * jnp.mean(scaled * normal, axis=-1, keepdims=True)
    )
    return back, jnp.sum(grad * normal, axis=0, keepdims=True), jnp.sum(grad, axis=0, keepdims=True)


def place_rows(target_ref, values, first, count):
    tokens = values.shape[0]
    at = lax.broadcasted_iota(jnp.int32, (count, tokens), 0) + first
    hit = (at == target_ref[0:1, :]) | (at == target_ref[1:2, :])
    return dot(hit.astype(F32).astype(BF), values, 1, 0).astype(BF)


def place_kernel(target_ref, values_ref, slots_ref):
    values = values_ref[...]
    part = slots_ref.shape[0] // 4
    for at in range(4):
        slots_ref[at * part : (at + 1) * part, :] = place_rows(
            target_ref, values, at * part, part
        )


def take_rows(target_ref, slots_refs, tokens):
    total = None
    first = 0
    for ref in slots_refs:
        count = ref.shape[0]
        at = lax.broadcasted_iota(jnp.int32, (tokens, count), 1) + first
        hit = (at == target_ref[:, 0:1]) | (at == target_ref[:, 1:2])
        part = dot(hit.astype(F32).astype(BF), ref[...], 1, 0)
        total = part if total is None else total + part
        first += count
    return total


def causal(size):
    rowpos = lax.broadcasted_iota(jnp.int32, (size, size), 0)
    colpos = lax.broadcasted_iota(jnp.int32, (size, size), 1)
    return rowpos >= colpos


def head_lanes(block, which):
    lane = lax.broadcasted_iota(jnp.int32, block.shape, 1)
    keep = (lane < HEAD_DIM) if which == 0 else (lane >= HEAD_DIM)
    return jnp.where(keep, block, jnp.zeros_like(block))


def block_softmax(query, keys, seen):
    size = query.shape[0]
    before = keys.shape[0] - size
    own = dot(query, keys[before:], 1, 1)
    own = jnp.where(seen, own, -1e30)
    top = jnp.max(own, axis=-1, keepdims=True)
    if before:
        past = dot(query, keys[:before], 1, 1)
        top = jnp.maximum(top, jnp.max(past, axis=-1, keepdims=True))
        past = jnp.exp(past - top)
    own = jnp.exp(own - top)
    total = jnp.sum(own, axis=-1, keepdims=True)
    if before:
        total = total + jnp.sum(past, axis=-1, keepdims=True)
    inverse = 1.0 / total
    own = own * inverse
    return (past * inverse, own) if before else (own,)


def pair_columns(pair, part, width):
    return pl.ds(pl.multiple_of(part * width + pair * 2 * HEAD_DIM, 2 * HEAD_DIM), 2 * HEAD_DIM)


def forward_kernel(
    x_ref,
    in0_ref,
    in1_ref,
    in2_ref,
    out0_ref,
    out1_ref,
    out2_ref,
    vec_ref,
    target_ref,
    normed_ref,
    proj_ref,
    context_ref,
    middle_ref,
    old_ref,
    new_ref,
):
    length, width = x_ref.shape
    x = x_ref[...].astype(F32)
    normal, _ = norm_parts(x)
    normed = (normal * vec_ref[0:1, :] + vec_ref[1:2, :]).astype(BF)
    normed_ref[...] = normed
    for part in range(3):
        cols = slice(part * width, (part + 1) * width)
        proj_ref[:, cols] = dot_parts(
            normed, [ref[cols, :] for ref in (in0_ref, in1_ref, in2_ref)]
        ).astype(BF)
    size = min(QUERY_BLOCK, length)
    seen = causal(size)

    def one_pair(pair, carry):
        q_at, k_at, v_at = (pair_columns(pair, part, width) for part in range(3))
        for block in range(length // size):
            rows = slice(block * size, (block + 1) * size)
            upto = (block + 1) * size
            query = proj_ref[rows, q_at] * BF(SCALE)
            keys = proj_ref[0:upto, k_at]
            values = proj_ref[0:upto, v_at]
            outs = []
            for which in range(2):
                probs = block_softmax(head_lanes(query, which), keys, seen)
                probs = [p.astype(BF) for p in probs]
                out = dot(probs[-1], values[upto - size :], 1, 0)
                if len(probs) > 1:
                    out = out + dot(probs[0], values[: upto - size], 1, 0)
                outs.append(out)
            lane = lax.broadcasted_iota(jnp.int32, outs[0].shape, 1)
            context_ref[rows, pair_columns(pair, 0, width)] = jnp.where(
                lane < HEAD_DIM, outs[0], outs[1]
            ).astype(BF)
        return carry

    lax.fori_loop(0, HEADS // 2, one_pair, 0)
    middle = x + dot_parts(context_ref[...], [ref[...] for ref in (out0_ref, out1_ref, out2_ref)])
    middle_ref[...] = middle
    normal, _ = norm_parts(middle)
    normed_two = (normal * vec_ref[2:3, :] + vec_ref[3:4, :]).astype(BF)
    count = old_ref.shape[0]
    half = count // 2
    for at, ref in ((0, old_ref), (count, new_ref)):
        for part in range(2):
            ref[part * half : (part + 1) * half, :] = place_rows(
                target_ref, normed_two, at + part * half, half
            )


def branch_kernel(
    old_ref,
    new_ref,
    target_ref,
    cot_ref,
    middle_ref,
    context_ref,
    out0_ref,
    out1_ref,
    out2_ref,
    vec_ref,
    gmid_ref,
    gctx_ref,
    outgrad_ref,
    sums_ref,
):
    length, width = cot_ref.shape
    grad = take_rows(target_ref, (old_ref, new_ref), length)
    back, gain_sum, bias_sum = norm_back(middle_ref[...], vec_ref[2:3, :], grad)
    gmid = back + cot_ref[...].astype(F32)
    gmid_ref[...] = gmid
    sums_ref[...] = jnp.concatenate([gain_sum, bias_sum, jnp.zeros((6, width), F32)], axis=0)
    branch = gmid.astype(BF)
    third = width // 3
    for part, ref in enumerate((out0_ref, out1_ref, out2_ref)):
        gctx_ref[:, part * third : (part + 1) * third] = dot(branch, ref[...], 1, 0).astype(BF)
    outgrad_ref[...] = dot(branch, context_ref[...], 0, 0).astype(BF)


def attention_back_kernel(
    place_ref,
    proj_ref,
    gctx_ref,
    normed_ref,
    gproj_ref,
    keep0_ref,
    keep1_ref,
    keep2_ref,
    send0_ref,
    send1_ref,
    send2_ref,
    gk_acc,
    gv_acc,
):
    length, width = gctx_ref.shape
    size = min(QUERY_BLOCK, length)
    seen = causal(size)

    def one_pair(pair, carry):
        q_at, k_at, v_at = (pair_columns(pair, part, width) for part in range(3))
        gk_acc[...] = jnp.zeros_like(gk_acc)
        gv_acc[...] = jnp.zeros_like(gv_acc)
        for block in range(length // size):
            rows = slice(block * size, (block + 1) * size)
            upto = (block + 1) * size
            query = proj_ref[rows, q_at] * BF(SCALE)
            keys = proj_ref[0:upto, k_at]
            values = proj_ref[0:upto, v_at]
            gout = gctx_ref[rows, pair_columns(pair, 0, width)]
            grads = []
            for which in range(2):
                mine = head_lanes(query, which)
                gmine = head_lanes(gout, which)
                probs = block_softmax(mine, keys, seen)
                spans = [slice(upto - size, upto)]
                if len(probs) > 1:
                    spans = [slice(0, upto - size)] + spans
                gprobs = [dot(gmine, values[s], 1, 1) for s in spans]
                row = sum(jnp.sum(p * g, axis=-1, keepdims=True) for p, g in zip(probs, gprobs))
                gquery = None
                for p, g, s in zip(probs, gprobs, spans):
                    gscore = (p * (g - row)).astype(BF)
                    part = dot(gscore, keys[s], 1, 0)
                    gquery = part if gquery is None else gquery + part
                    gk_acc[s, :] += dot(gscore, mine, 0, 0)
                    gv_acc[s, :] += dot(p.astype(BF), gmine, 0, 0)
                grads.append(gquery * SCALE)
            lane = lax.broadcasted_iota(jnp.int32, grads[0].shape, 1)
            gproj_ref[rows, q_at] = jnp.where(lane < HEAD_DIM, grads[0], grads[1]).astype(BF)
        gproj_ref[:, k_at] = gk_acc[...].astype(BF)
        gproj_ref[:, v_at] = gv_acc[...].astype(BF)
        return carry

    lax.fori_loop(0, HEADS // 2, one_pair, 0)
    third = width // 3
    core = place_ref[0] % 2
    halves, rows, _ = keep0_ref.shape
    refs = ((keep0_ref, send0_ref), (keep1_ref, send1_ref), (keep2_ref, send2_ref))
    for part, (keep_ref, send_ref) in enumerate(refs):
        grad = dot(gproj_ref[...], normed_ref[:, part * third : (part + 1) * third], 0, 0)
        grad = grad.astype(BF)
        for at in range(halves):
            first = grad[2 * at * rows : (2 * at + 1) * rows]
            second = grad[(2 * at + 1) * rows : (2 * at + 2) * rows]
            keep_ref[at] = jnp.where(core == 0, first, second)
            send_ref[at] = jnp.where(core == 0, second, first)


def input_kernel(
    gproj_ref, in0_ref, in1_ref, in2_ref, x_ref, vec_ref, gmid_ref, grad_ref, sums_ref
):
    grad = jnp.concatenate(
        [dot(gproj_ref[...], ref[...], 1, 0) for ref in (in0_ref, in1_ref, in2_ref)], axis=1
    )
    back, gain_sum, bias_sum = norm_back(x_ref[...].astype(F32), vec_ref[0:1, :], grad)
    grad_ref[...] = gmid_ref[...] + back
    width = x_ref.shape[1]
    sums_ref[...] = jnp.concatenate([gain_sum, bias_sum, jnp.zeros((6, width), F32)], axis=0)


def mixed_kernel(old_ref, new_ref, target_ref, middle_ref, mixed_ref):
    total = take_rows(target_ref, (old_ref, new_ref), middle_ref.shape[0])
    mixed_ref[...] = (middle_ref[...] + total).astype(BF)


def gelu_pair(x):
    c = 0.7978845608028654
    sq = x * x
    t = jnp.tanh(c * x * (1.0 + 0.044715 * sq))
    half = 0.5 * (1.0 + t)
    slope = half + 0.5 * x * (1.0 - t * t) * (c * (1.0 + 3 * 0.044715 * sq))
    return x * half, slope

def expert_kernel(train, steps, pieces, place_ref, mine_ref, rows_ref, grads4_ref, router_ref, *rest):
    ups, downs, rest = rest[:pieces], rest[pieces : 2 * pieces], rest[2 * pieces :]
    if train:
        gated_ref, gin_ref, rgrad_ref, upkeep_ref, upsend_ref, downkeep_ref, downsend_ref = rest[:7]
        rest = rest[7:]
    else:
        gated_ref, gin_ref, rgrad_ref = rest[:3]
        rest = rest[3:]
    up_s, down_s, out_acc, gin_acc, scaled, gate_s, probs_s, sems = rest
    j = pl.program_id(0)
    mine = mine_ref[0:1, :]
    up_rows = up_s.shape[0] // pieces
    down_rows = down_s.shape[0] // pieces
    tile = up_s.shape[1] // steps

    def grads():
        return grads4_ref[...].reshape(rows_ref.shape).astype(F32)

    def fetches():
        found = []
        for at in range(pieces):
            owner = place_ref[at]
            to = pl.ds(pl.multiple_of(owner * up_rows, up_rows), up_rows)
            found.append(pltpu.make_async_copy(ups[at], up_s.at[to], sems.at[0, at]))
            to = pl.ds(pl.multiple_of(owner * down_rows, down_rows), down_rows)
            found.append(pltpu.make_async_copy(downs[at], down_s.at[to], sems.at[1, at]))
        return found

    @pl.when(j == 0)
    def _():
        for fetch in fetches():
            fetch.start()
        logits = dot(rows_ref[...], router_ref[...], 1, 1)
        live = lax.broadcasted_iota(jnp.int32, logits.shape, 1) < mine_ref[1, 0].astype(jnp.int32)
        logits = jnp.where(live, logits, -1e30)
        e = jnp.exp(logits - jnp.max(logits, axis=1, keepdims=True))
        probs = e / jnp.sum(e, axis=1, keepdims=True)
        probs_s[...] = probs
        gate = jnp.sum(probs * mine, axis=1, keepdims=True)
        gate_s[...] = jnp.broadcast_to(gate, gate_s.shape)
        scaled[...] = (grads() * gate).astype(BF)
        out_acc[...] = jnp.zeros_like(out_acc)
        gin_acc[...] = jnp.zeros_like(gin_acc)
        for fetch in fetches():
            fetch.wait()

    rows = rows_ref[...]
    here = pl.ds(pl.multiple_of(j * tile, tile), tile)
    up = up_s[:, here]
    down = down_s[here, :]
    hid, slope = gelu_pair(dot(rows, up, 1, 0))
    hid = hid.astype(BF)
    gpre = (dot(scaled[...], down, 1, 1) * slope).astype(BF)
    out_acc[...] += dot(hid, down, 1, 0)
    gin_acc[...] += dot(gpre, up, 1, 1)

    if train:
        core = place_ref[0] % 2
        grad_up = dot(rows, gpre, 0, 0).astype(BF)
        for pair in range(pieces // 2):
            first = grad_up[2 * pair * up_rows : (2 * pair + 1) * up_rows]
            second = grad_up[(2 * pair + 1) * up_rows : (2 * pair + 2) * up_rows]
            upkeep_ref[pair] = jnp.where(core == 0, first, second)
            upsend_ref[pair] = jnp.where(core == 0, second, first)
        grad_down = dot(hid, scaled[...], 0, 0).astype(BF)
        inside = tile // down_rows
        for at in range(inside):
            block = grad_down[at * down_rows : (at + 1) * down_rows]
            owner = j * inside + at

            @pl.when(owner % 2 == core)
            def _():
                downkeep_ref[owner // 2] = block

            @pl.when(owner % 2 != core)
            def _():
                downsend_ref[owner // 2] = block

    @pl.when(j == steps - 1)
    def _():
        produced = out_acc[...].astype(BF).astype(F32)
        gate = gate_s[:, 0:1]
        gated_ref[...] = (produced * gate).astype(BF)
        grad_gate = jnp.sum(produced * grads(), axis=1, keepdims=True)
        gl = (grad_gate * gate * (mine - probs_s[...])).astype(BF)
        gin_ref[...] = (gin_acc[...] + dot(gl, router_ref[...], 1, 0)).astype(BF)
        rgrad_ref[...] = dot(gl, rows_ref[...], 0, 0)


def expert_call(owners, mine, rows, grads, router_pad, ups, downs, train):
    n, d = rows.shape
    pieces = len(ups)
    f = ups[0].shape[1]
    tile = max(d, f // pieces)
    steps = f // tile
    peers, _, capacity, _ = grads.shape
    member = 1 if train else 0
    one = pl.Buffered(buffer_count=1)

    def all_of(shape):
        return pl.BlockSpec(shape, lambda j: (0,) * len(shape), pipeline_mode=one)

    slot_spec = pl.BlockSpec(
        (peers, 1, capacity, d), lambda j: (0, member, 0, 0), pipeline_mode=one
    )
    anywhere = pl.BlockSpec(memory_space=pl.ANY)
    outs = [((n, d), BF), ((n, d), BF), ((128, d), F32)]
    out_specs = [all_of((n, d)), all_of((n, d)), all_of((128, d))]
    if train:
        half = pieces // 2
        up_shape = (half, d // pieces, f)
        down_shape = (half, f // pieces, d)
        outs += [(up_shape, BF)] * 2 + [(down_shape, BF)] * 2
        out_specs += [pl.BlockSpec((half, d // pieces, tile), lambda j: (0, 0, j))] * 2
        out_specs += [all_of(down_shape)] * 2
    args = [owners, mine, rows, grads, router_pad, *ups, *downs]
    return pl.pallas_call(
        functools.partial(expert_kernel, train, steps, pieces),
        grid=(steps,),
        in_specs=[
            pl.BlockSpec(memory_space=pltpu.SMEM),
            all_of((8, 128)),
            all_of((n, d)),
            slot_spec,
            all_of((128, d)),
        ]
        + [anywhere] * (2 * pieces),
        out_specs=out_specs,
        out_shape=[whole(o) for o in outs],
        scratch_shapes=[
            pltpu.VMEM((d, f), BF),
            pltpu.VMEM((f, d), BF),
            pltpu.VMEM((n, d), F32),
            pltpu.VMEM((n, d), F32),
            pltpu.VMEM((n, d), BF),
            pltpu.VMEM((n, 128), F32),
            pltpu.VMEM((n, 128), F32),
            pltpu.SemaphoreType.DMA((2, pieces)),
        ],
        compiler_params=pltpu.CompilerParams(vmem_limit_bytes=LIMIT),
        cost_estimate=cost(40 if train else 27),
        name="expert_new" if train else "expert_old",
    )(*args)


def shards(
    block_input,
    cotangent,
    attn_in,
    attn_out,
    router,
    ln1_gain,
    ln1_bias,
    ln2_gain,
    ln2_bias,
    new_w1,
    new_w2,
    old_w1,
    old_w2,
    expert_ids,
    slots,
    drops,
):
    length, width = block_input.shape
    peers = lax.axis_size("expert")
    devices = lax.axis_size("dp") * peers
    experts = 2 * peers
    capacity = max(length * 7 // (2 * experts), 2)
    me = lax.axis_index("expert")
    ways, scatter_ways = orders()
    third = width // 3
    in_share = attn_in.shape[1]
    share = width // devices

    small = jnp.concatenate(
        [v[None] for v in (ln1_gain, ln1_bias, ln2_gain, ln2_bias)] + [router.T], axis=0
    )
    lines = small.shape[0]
    small = jnp.pad(small, ((0, -lines % 8), (0, third - share)))
    in_t, out_t = attn_in.T, attn_out.T
    states = []
    for p in range(3):
        cols = slice(p * third, (p + 1) * third)
        rows = [in_t[:, cols], out_t[:, cols]] + ([small] if p == 0 else [])
        states.append((jnp.concatenate(rows, axis=0), []))
    states = [gather_steps(states[p], ways[p][:2]) for p in range(3)]
    early = [state[0] for state in states]
    states = [gather_steps(states[p], ways[p][2:-1]) for p in range(3)]
    between = [state[0] for state in states]
    parts = [gather_finish(gather_steps(states[p], ways[p][-1:])) for p in range(3)]
    parts = [part.reshape(devices, -1, third) for part in parts]
    in_parts = [part[:, :in_share].reshape(3 * width, third) for part in parts]
    out_parts = [part[:, in_share : in_share + share].reshape(width, third) for part in parts]
    small_full = parts[0][:, in_share + share : in_share + share + lines, :share]
    small_full = small_full.transpose(1, 0, 2).reshape(lines, width)
    vectors = jnp.pad(small_full[:4].astype(F32), ((0, 4), (0, 0)))
    router_pad = jnp.pad(small_full[4:], ((0, 128 - experts), (0, 0)))

    target = jnp.where(drops == 0, expert_ids * capacity + slots, -1)
    by_member = ((expert_ids % 2) * peers + expert_ids // 2) * capacity + slots
    by_member = jnp.where(drops == 0, by_member, -1)
    target_rows = jnp.pad(target.T, ((0, 6), (0, 0)), constant_values=-1)
    member_rows = jnp.pad(by_member.T, ((0, 6), (0, 0)), constant_values=-1)
    count = peers * capacity
    both_shape = (peers, 2, capacity, width)

    def move(block):
        return lax.all_to_all(block, "expert", split_axis=0, concat_axis=0, tiled=True)

    def send(block, *earlier):
        block = after(block, *earlier).reshape(peers, capacity, width)
        return move(block).reshape(count, width)

    (grad_slots,) = plain_call(
        place_kernel, [((2 * count, width), BF)], [], "place_grads", 4, target_rows, after(cotangent, early)
    )
    grads = move(after(grad_slots, between).reshape(both_shape))
    slot_outs = [((count, width), BF)] * 2

    normed, proj, context, middle, rold, rnew = plain_call(
        forward_kernel,
        [
            ((length, width), BF),
            ((length, 3 * width), BF),
            ((length, width), BF),
            ((length, width), F32),
        ]
        + slot_outs,
        [],
        "attention_forward", 27,
        block_input,
        *in_parts,
        *out_parts,
        vectors,
        member_rows,
    )
    owners = lax.axis_index("dp") ^ jnp.arange(lax.axis_size("dp"), dtype=jnp.int32)
    new_ups, far_up = dp_pieces(new_w1[0], (between,), ())
    new_downs, far_down = dp_pieces(new_w2[0], (between,), ())
    old_ups, _ = dp_pieces(old_w1[0], (between, far_up), ())
    old_downs, _ = dp_pieces(old_w2[0], (between, far_up), ())
    rold = send(rold, grads, far_up, far_down)
    rnew = send(rnew, rold)

    lane = lax.broadcasted_iota(jnp.int32, (8, 128), 1)
    line = lax.broadcasted_iota(jnp.int32, (8, 128), 0)

    def chosen(expert):
        return jnp.where(line == 0, (lane == expert).astype(F32), F32(experts))

    old_gated, old_in, old_router = expert_call(
        owners, chosen(2 * me), rold, grads, router_pad, old_ups, old_downs, False
    )
    rnew, old_in = lax.optimization_barrier((rnew, old_in))
    old_in = send(old_in, rnew)
    new_gated, new_in, new_router, up_keep, up_send, down_keep, down_send = expert_call(
        owners, chosen(2 * me + 1), rnew, grads, router_pad, new_ups, new_downs, True
    )
    new_in = send(new_in, old_in)
    old_gated = send(old_gated, new_in)
    new_gated = send(new_gated, old_gated)
    up_send, down_send = after((up_send, down_send), old_in)
    new_w1_grad = scatter_dp(up_keep, up_send)[None]
    new_w2_grad = scatter_dp(down_keep, down_send)[None]
    router_part = (old_router + new_router)[:experts]

    gmid, gctx, out_grad, sums_two = plain_call(
        branch_kernel,
        [
            ((length, width), F32),
            ((length, width), BF),
            ((width, width), BF),
            ((8, width), F32),
        ],
        [],
        "branch_backward",
        0,
        old_in,
        new_in,
        by_member,
        cotangent,
        middle,
        context,
        *out_parts,
        vectors,
    )
    half = lax.axis_size("dp") // 2
    gproj, *split = plain_call(
        attention_back_kernel,
        [((length, 3 * width), BF)] + [((half, 3 * width // (2 * half), third), BF)] * 6,
        [pltpu.VMEM((length, 2 * HEAD_DIM), F32)] * 2,
        "attention_backward",
        0,
        owners,
        proj,
        gctx,
        normed,
    )
    input_grad, sums_one = plain_call(
        input_kernel,
        [((length, width), F32), ((8, width), F32)],
        [],
        "input_backward", 0,
        gproj,
        *in_parts,
        block_input,
        vectors,
        gmid,
    )
    (mixed,) = plain_call(
        mixed_kernel,
        [((length, width), BF)],
        [],
        "mixed_output", 0,
        old_gated,
        new_gated,
        by_member,
        middle,
    )
    lead = canonical()
    core = [("dp", powers(lax.axis_size("dp"))[0])]
    states = []
    for keep, away in zip(split[:3], split[3:]):
        total = keep.astype(F32) + swap(away, *core[0]).astype(F32)
        left = [step for step in lead if step != core[0]]
        states.append((total.reshape([2] * len(left) + [in_share, third]), left))
    small_grads = jnp.concatenate([sums_one[:2], sums_two[:2], router_part], axis=0)
    small_grads = small_grads.reshape(lines, devices, share).transpose(1, 0, 2)
    small_grads = small_grads.reshape(devices, 1, lines * share).astype(BF)
    small_rows = -(-lines * share // width)
    small_grads = jnp.pad(small_grads, ((0, 0), (0, 0), (0, small_rows * width - lines * share)))
    rest = jnp.concatenate(
        [out_grad.reshape(devices, share, width), small_grads.reshape(devices, small_rows, width)],
        axis=1,
    )
    rest = rest.reshape([2] * len(lead) + list(rest.shape[1:]))
    states.append(scatter_steps((rest, lead), core))
    held = after([values for values, _ in states], old_gated, new_gated)
    sums = [
        scatter_steps((held[p], states[p][1]), scatter_ways[p])[0] for p in range(len(states))
    ]
    attn_in_grad = jnp.concatenate(sums[:3], axis=1).T
    attn_out_grad = sums[3][:share].T
    small_grads = sums[3][share:].reshape(-1)[: lines * share].reshape(lines, share)
    vector_grads = small_grads[:4]
    router_grad = small_grads[4:].T
    return (
        mixed,
        input_grad,
        attn_in_grad,
        attn_out_grad,
        router_grad,
        vector_grads[0],
        vector_grads[1],
        vector_grads[2],
        vector_grads[3],
        new_w1_grad,
        new_w2_grad,
    )


def solution(mesh):
    both = ("dp", "expert")
    rows = P(both, None)
    columns = P(None, both)
    vector = P(both)
    weight = P("expert", "dp", None)
    in_specs = (
        [rows, rows, columns, columns, rows] + [vector] * 4 + [weight] * 4 + [rows] * 3
    )
    out_specs = [rows, rows, columns, columns, rows] + [vector] * 4 + [weight] * 2
    return jax.shard_map(
        shards, mesh=mesh, in_specs=tuple(in_specs), out_specs=tuple(out_specs), check_vma=False
    )
```

```python
import functools

import jax
import jax.numpy as jnp
from jax import lax
from jax.experimental import pallas as pl
from jax.experimental.pallas import tpu as pltpu
from jax.sharding import PartitionSpec as P

HEADS = 12
HEAD_DIM = 64
BF = jnp.bfloat16
F32 = jnp.float32


def mm(a, b, dims, out=F32):
    return lax.dot_general(a, b, (dims, ((), ())), preferred_element_type=F32).astype(out)


def powers(count):
    found = []
    bit = 1
    while bit < count:
        found.append(bit)
        bit *= 2
    return found


def swap(values, axis, bit):
    count = lax.axis_size(axis)
    return lax.ppermute(values, axis, [(i, i ^ bit) for i in range(count)])


def my_bit(axis, bit):
    return (lax.axis_index(axis) // bit) % 2


def canonical():
    return [("dp", b) for b in reversed(powers(lax.axis_size("dp")))] + [
        ("expert", b) for b in reversed(powers(lax.axis_size("expert")))
    ]


def orders():
    dp_bits = powers(lax.axis_size("dp"))
    expert_bits = powers(lax.axis_size("expert"))
    core = [("dp", dp_bits[0])]
    xs = [("dp", b) for b in reversed(dp_bits[1:])]
    ys = [("expert", expert_bits[0])]
    zs = [("expert", b) for b in reversed(expert_bits[1:])]
    gathering = (zs + ys + xs + core, xs + zs + ys + core, ys + xs + zs + core)
    near = zs[::-1]
    summing = (xs + ys + near, ys + near + xs, near + xs + ys, near + ys + xs)
    return gathering, summing


def gather_steps(state, order):
    current, lead = state
    lead = list(lead)
    for axis, bit in order:
        other = swap(current, axis, bit)
        low = my_bit(axis, bit) == 0
        current = jnp.stack([jnp.where(low, current, other), jnp.where(low, other, current)])
        lead.insert(0, (axis, bit))
    return current, lead


def gather_finish(state):
    current, lead = state
    tail = current.shape[len(lead) :]
    perm = [lead.index(w) for w in canonical()]
    current = current.transpose(perm + list(range(len(lead), current.ndim)))
    return current.reshape((-1,) + tail)


def after(values, *earlier):
    if not earlier:
        return values
    return lax.optimization_barrier((values, earlier))[0]


def total(addends):
    found = addends[0].astype(F32)
    for addend in addends[1:]:
        found = found + addend.astype(F32)
    return found


def away_part(addends, lead, step):
    at = lead.index(step)
    mine = my_bit(*step)
    send = total([lax.dynamic_index_in_dim(a, 1 - mine, at, keepdims=False) for a in addends])
    return send.astype(BF)


def scatter_step(addends, lead, step):
    return swap(away_part(addends, lead, step), *step)


def scatter_rest(addends, lead, step, got):
    at = lead.index(step)
    addends = [lax.dynamic_index_in_dim(a, my_bit(*step), at, keepdims=False) for a in addends]
    return addends + [got], lead[:at] + lead[at + 1 :]


def core_swap(piece):
    return swap(piece, "dp", powers(lax.axis_size("dp"))[0])


def dp_far(shard):
    far = {}
    for bit in powers(lax.axis_size("dp"))[1:]:
        for away, piece in [(0, shard), *far.items()]:
            far[away ^ bit] = swap(piece, "dp", bit)
    return far


def dp_pieces(shard, own, far, near):
    core = powers(lax.axis_size("dp"))[0]
    found = {0: shard, core: own, **far}
    found.update({away ^ core: piece for away, piece in near.items()})
    return [found[away] for away in range(len(found))]


def x_steps():
    return [("dp", b) for b in powers(lax.axis_size("dp"))[1:]]


def scatter_dp_first(addends):
    order = x_steps()
    addends = [a.reshape([2] * len(order) + list(a.shape[1:])) for a in addends]
    return away_part(addends, order[::-1], order[0])


def scatter_dp(addends, first):
    order = x_steps()
    lead = order[::-1]
    addends = [a.reshape([2] * len(order) + list(a.shape[1:])) for a in addends]
    arrived = [swap(first, *order[0])]
    for at, step in enumerate(order[1:]):
        addends, lead = scatter_rest(addends, lead, order[at], arrived[-1])
        arrived.append(scatter_step(addends, lead, step))
    return arrived


def scatter_dp_total(addends, arrived):
    order = x_steps()
    lead = order[::-1]
    addends = [a.reshape([2] * len(order) + list(a.shape[1:])) for a in addends]
    for step, got in zip(order, arrived):
        addends, lead = scatter_rest(addends, lead, step, got)
    return total(addends)


LIMIT = 56 * 1024 * 1024
QUERY_BLOCK = 128
SCALE = HEAD_DIM ** (-0.5)


def dot(a, b, over_a, over_b):
    return lax.dot_general(
        a, b, (((over_a,), (over_b,)), ((), ())), preferred_element_type=F32
    )


def dot_parts(values, parts):
    width = parts[0].shape[1]
    total = None
    for at, part in enumerate(parts):
        term = dot(values[:, at * width : (at + 1) * width], part, 1, 1)
        total = term if total is None else total + term
    return total


def whole(array):
    return jax.ShapeDtypeStruct(array[0], array[1])


def cost(micros):
    return pl.CostEstimate(flops=int(micros * 0.25e9), bytes_accessed=0, transcendentals=0)


def plain_call(body, outs, scratch, name, micros, *args):
    space = pl.BlockSpec(memory_space=pltpu.VMEM)
    return pl.pallas_call(
        body,
        out_shape=[whole(o) for o in outs],
        in_specs=[space] * len(args),
        out_specs=[space] * len(outs),
        scratch_shapes=scratch,
        compiler_params=pltpu.CompilerParams(vmem_limit_bytes=LIMIT),
        cost_estimate=cost(micros),
        name=name,
    )(*args)


def norm_parts(values):
    centre = values - jnp.mean(values, axis=-1, keepdims=True)
    spread = jnp.mean(centre * centre, axis=-1, keepdims=True)
    scale = lax.rsqrt(spread + 1e-05)
    return centre * scale, scale


def norm_back(values, gain, grad):
    normal, scale = norm_parts(values)
    scaled = grad * gain
    back = scale * (
        scaled
        - jnp.mean(scaled, axis=-1, keepdims=True)
        - normal * jnp.mean(scaled * normal, axis=-1, keepdims=True)
    )
    return back, jnp.sum(grad * normal, axis=0, keepdims=True), jnp.sum(grad, axis=0, keepdims=True)


def place_rows(target_ref, values, first, count):
    tokens = values.shape[0]
    at = lax.broadcasted_iota(jnp.int32, (count, tokens), 0) + first
    hit = (at == target_ref[0:1, :]) | (at == target_ref[1:2, :])
    return dot(hit.astype(F32).astype(BF), values, 1, 0).astype(BF)


def place_kernel(target_ref, values_ref, slots_ref):
    values = values_ref[...]
    part = slots_ref.shape[0] // 4
    for at in range(4):
        slots_ref[at * part : (at + 1) * part, :] = place_rows(
            target_ref, values, at * part, part
        )


def take_rows(target_ref, slots_refs, tokens):
    total = None
    first = 0
    for ref in slots_refs:
        count = ref.shape[0]
        at = lax.broadcasted_iota(jnp.int32, (tokens, count), 1) + first
        hit = (at == target_ref[:, 0:1]) | (at == target_ref[:, 1:2])
        part = dot(hit.astype(F32).astype(BF), ref[...], 1, 0)
        total = part if total is None else total + part
        first += count
    return total


def causal(size):
    rowpos = lax.broadcasted_iota(jnp.int32, (size, size), 0)
    colpos = lax.broadcasted_iota(jnp.int32, (size, size), 1)
    return rowpos >= colpos


def head_lanes(block, which):
    lane = lax.broadcasted_iota(jnp.int32, block.shape, 1)
    keep = (lane < HEAD_DIM) if which == 0 else (lane >= HEAD_DIM)
    return jnp.where(keep, block, jnp.zeros_like(block))


def block_softmax(query, keys, seen):
    size = query.shape[0]
    before = keys.shape[0] - size
    own = dot(query, keys[before:], 1, 1)
    own = jnp.where(seen, own, -1e30)
    top = jnp.max(own, axis=-1, keepdims=True)
    if before:
        past = dot(query, keys[:before], 1, 1)
        top = jnp.maximum(top, jnp.max(past, axis=-1, keepdims=True))
        past = jnp.exp(past - top)
    own = jnp.exp(own - top)
    total = jnp.sum(own, axis=-1, keepdims=True)
    if before:
        total = total + jnp.sum(past, axis=-1, keepdims=True)
    inverse = 1.0 / total
    own = own * inverse
    return (past * inverse, own) if before else (own,)


def pair_columns(pair, part, width):
    return pl.ds(pl.multiple_of(part * width + pair * 2 * HEAD_DIM, 2 * HEAD_DIM), 2 * HEAD_DIM)


def forward_kernel(
    x_ref,
    in0_ref,
    in1_ref,
    in2_ref,
    out0_ref,
    out1_ref,
    out2_ref,
    vec_ref,
    target_ref,
    normed_ref,
    proj_ref,
    context_ref,
    middle_ref,
    old_ref,
    new_ref,
):
    length, width = x_ref.shape
    x = x_ref[...].astype(F32)
    normal, _ = norm_parts(x)
    normed = (normal * vec_ref[0:1, :] + vec_ref[1:2, :]).astype(BF)
    normed_ref[...] = normed
    for part in range(3):
        cols = slice(part * width, (part + 1) * width)
        proj_ref[:, cols] = dot_parts(
            normed, [ref[cols, :] for ref in (in0_ref, in1_ref, in2_ref)]
        ).astype(BF)
    size = min(QUERY_BLOCK, length)
    seen = causal(size)

    def one_pair(pair, carry):
        q_at, k_at, v_at = (pair_columns(pair, part, width) for part in range(3))
        for block in range(length // size):
            rows = slice(block * size, (block + 1) * size)
            upto = (block + 1) * size
            query = proj_ref[rows, q_at] * BF(SCALE)
            keys = proj_ref[0:upto, k_at]
            values = proj_ref[0:upto, v_at]
            outs = []
            for which in range(2):
                probs = block_softmax(head_lanes(query, which), keys, seen)
                probs = [p.astype(BF) for p in probs]
                out = dot(probs[-1], values[upto - size :], 1, 0)
                if len(probs) > 1:
                    out = out + dot(probs[0], values[: upto - size], 1, 0)
                outs.append(out)
            lane = lax.broadcasted_iota(jnp.int32, outs[0].shape, 1)
            context_ref[rows, pair_columns(pair, 0, width)] = jnp.where(
                lane < HEAD_DIM, outs[0], outs[1]
            ).astype(BF)
        return carry

    lax.fori_loop(0, HEADS // 2, one_pair, 0)
    middle = x + dot_parts(context_ref[...], [ref[...] for ref in (out0_ref, out1_ref, out2_ref)])
    middle_ref[...] = middle
    normal, _ = norm_parts(middle)
    normed_two = (normal * vec_ref[2:3, :] + vec_ref[3:4, :]).astype(BF)
    count = old_ref.shape[0]
    half = count // 2
    for at, ref in ((0, old_ref), (count, new_ref)):
        for part in range(2):
            ref[part * half : (part + 1) * half, :] = place_rows(
                target_ref, normed_two, at + part * half, half
            )


def branch_kernel(
    old_ref,
    new_ref,
    target_ref,
    cot_ref,
    middle_ref,
    context_ref,
    out0_ref,
    out1_ref,
    out2_ref,
    vec_ref,
    gmid_ref,
    gctx_ref,
    outgrad_ref,
    sums_ref,
):
    length, width = cot_ref.shape
    grad = take_rows(target_ref, (old_ref, new_ref), length)
    back, gain_sum, bias_sum = norm_back(middle_ref[...], vec_ref[2:3, :], grad)
    gmid = back + cot_ref[...].astype(F32)
    gmid_ref[...] = gmid
    sums_ref[...] = jnp.concatenate([gain_sum, bias_sum, jnp.zeros((6, width), F32)], axis=0)
    branch = gmid.astype(BF)
    third = width // 3
    for part, ref in enumerate((out0_ref, out1_ref, out2_ref)):
        gctx_ref[:, part * third : (part + 1) * third] = dot(branch, ref[...], 1, 0).astype(BF)
    outgrad_ref[...] = dot(branch, context_ref[...], 0, 0).astype(BF)


def pairs_back(proj_ref, gctx_ref, gproj_ref, gk_acc, gv_acc, first, last, shift, spread):
    length, width = gctx_ref.shape
    size = min(QUERY_BLOCK, length)
    seen = causal(size)

    def one_pair(pair, carry):
        q_at, k_at, v_at = (pair_columns(pair, part, width) for part in range(3))
        q_to, k_to, v_to = (pair_columns(pair - shift, part, spread) for part in range(3))
        gk_acc[...] = jnp.zeros_like(gk_acc)
        gv_acc[...] = jnp.zeros_like(gv_acc)
        for block in range(length // size):
            rows = slice(block * size, (block + 1) * size)
            upto = (block + 1) * size
            query = proj_ref[rows, q_at] * BF(SCALE)
            keys = proj_ref[0:upto, k_at]
            values = proj_ref[0:upto, v_at]
            gout = gctx_ref[rows, pair_columns(pair, 0, width)]
            grads = []
            for which in range(2):
                mine = head_lanes(query, which)
                gmine = head_lanes(gout, which)
                probs = block_softmax(mine, keys, seen)
                spans = [slice(upto - size, upto)]
                if len(probs) > 1:
                    spans = [slice(0, upto - size)] + spans
                gprobs = [dot(gmine, values[s], 1, 1) for s in spans]
                row = sum(jnp.sum(p * g, axis=-1, keepdims=True) for p, g in zip(probs, gprobs))
                gquery = None
                for p, g, s in zip(probs, gprobs, spans):
                    gscore = (p * (g - row)).astype(BF)
                    part = dot(gscore, keys[s], 1, 0)
                    gquery = part if gquery is None else gquery + part
                    gk_acc[s, :] += dot(gscore, mine, 0, 0)
                    gv_acc[s, :] += dot(p.astype(BF), gmine, 0, 0)
                grads.append(gquery * SCALE)
            lane = lax.broadcasted_iota(jnp.int32, grads[0].shape, 1)
            gproj_ref[rows, q_to] = jnp.where(lane < HEAD_DIM, grads[0], grads[1]).astype(BF)
        gproj_ref[:, k_to] = gk_acc[...].astype(BF)
        gproj_ref[:, v_to] = gv_acc[...].astype(BF)
        return carry

    lax.fori_loop(first, last, one_pair, 0)

def attention_first_kernel(proj_ref, gctx_ref, gproj_ref, gk_acc, gv_acc):
    spread = gproj_ref.shape[1] // 3
    last = spread // (2 * HEAD_DIM)
    pairs_back(proj_ref, gctx_ref, gproj_ref, gk_acc, gv_acc, 0, last, 0, spread)


def attention_back_kernel(
    place_ref,
    proj_ref,
    gctx_ref,
    normed_ref,
    before_ref,
    gproj_ref,
    keep0_ref,
    keep1_ref,
    keep2_ref,
    send0_ref,
    send1_ref,
    send2_ref,
    gk_acc,
    gv_acc,
):
    width = gctx_ref.shape[1]
    done = before_ref.shape[1] // 3
    for part in range(3):
        gproj_ref[:, part * width : part * width + done] = before_ref[
            :, part * done : (part + 1) * done
        ]
    first = done // (2 * HEAD_DIM)
    pairs_back(proj_ref, gctx_ref, gproj_ref, gk_acc, gv_acc, first, HEADS // 2, 0, width)
    length, width = gctx_ref.shape
    size = min(QUERY_BLOCK, length)
    seen = causal(size)

    def one_pair(pair, carry):
        q_at, k_at, v_at = (pair_columns(pair, part, width) for part in range(3))
        gk
    third = width // 3
    core = place_ref[0] % 2
    halves, rows, _ = keep0_ref.shape
    refs = ((keep0_ref, send0_ref), (keep1_ref, send1_ref), (keep2_ref, send2_ref))
    for part, (keep_ref, send_ref) in enumerate(refs):
        grad = dot(gproj_ref[...], normed_ref[:, part * third : (part + 1) * third], 0, 0)
        grad = grad.astype(BF)
        for at in range(halves):
            first = grad[2 * at * rows : (2 * at + 1) * rows]
            second = grad[(2 * at + 1) * rows : (2 * at + 2) * rows]
            keep_ref[at] = jnp.where(core == 0, first, second)
            send_ref[at] = jnp.where(core == 0, second, first)


def input_kernel(
    gproj_ref, in0_ref, in1_ref, in2_ref, x_ref, vec_ref, gmid_ref, grad_ref, sums_ref
):
    grad = jnp.concatenate(
        [dot(gproj_ref[...], ref[...], 1, 0) for ref in (in0_ref, in1_ref, in2_ref)], axis=1
    )
    back, gain_sum, bias_sum = norm_back(x_ref[...].astype(F32), vec_ref[0:1, :], grad)
    grad_ref[...] = gmid_ref[...] + back
    width = x_ref.shape[1]
    sums_ref[...] = jnp.concatenate([gain_sum, bias_sum, jnp.zeros((6, width), F32)], axis=0)


def mixed_kernel(old_ref, new_ref, target_ref, middle_ref, mixed_ref):
    total = take_rows(target_ref, (old_ref, new_ref), middle_ref.shape[0])
    mixed_ref[...] = (middle_ref[...] + total).astype(BF)


def gelu_pair(x):
    c = 0.7978845608028654
    sq = x * x
    t = jnp.tanh(c * x * (1.0 + 0.044715 * sq))
    half = 0.5 * (1.0 + t)
    slope = half + 0.5 * x * (1.0 - t * t) * (c * (1.0 + 3 * 0.044715 * sq))
    return x * half, slope

def expert_kernel(train, steps, pieces, place_ref, mine_ref, rows_ref, grads4_ref, router_ref, *rest):
    ups, downs, rest = rest[:pieces], rest[pieces : 2 * pieces], rest[2 * pieces :]
    if train:
        gated_ref, gin_ref, rgrad_ref, hid_ref, gpre_ref, scaled_ref = rest[:6]
        rest = rest[6:]
    else:
        gated_ref, gin_ref, rgrad_ref = rest[:3]
        rest = rest[3:]
    up_s, down_s, out_acc, gin_acc, scaled, gate_s, probs_s, sems = rest
    j = pl.program_id(0)
    mine = mine_ref[0:1, :]
    up_rows = up_s.shape[0] // pieces
    down_rows = down_s.shape[0] // pieces
    tile = up_s.shape[1] // steps

    def grads():
        return grads4_ref[...].reshape(rows_ref.shape).astype(F32)

    def fetches():
        found = []
        for at in range(pieces):
            owner = place_ref[at]
            to = pl.ds(pl.multiple_of(owner * up_rows, up_rows), up_rows)
            found.append(pltpu.make_async_copy(ups[at], up_s.at[to], sems.at[0, at]))
            to = pl.ds(pl.multiple_of(owner * down_rows, down_rows), down_rows)
            found.append(pltpu.make_async_copy(downs[at], down_s.at[to], sems.at[1, at]))
        return found

    @pl.when(j == 0)
    def _():
        for fetch in fetches():
            fetch.start()
        logits = dot(rows_ref[...], router_ref[...], 1, 1)
        live = lax.broadcasted_iota(jnp.int32, logits.shape, 1) < mine_ref[1, 0].astype(jnp.int32)
        logits = jnp.where(live, logits, -1e30)
        e = jnp.exp(logits - jnp.max(logits, axis=1, keepdims=True))
        probs = e / jnp.sum(e, axis=1, keepdims=True)
        probs_s[...] = probs
        gate = jnp.sum(probs * mine, axis=1, keepdims=True)
        gate_s[...] = jnp.broadcast_to(gate, gate_s.shape)
        scaled[...] = (grads() * gate).astype(BF)
        out_acc[...] = jnp.zeros_like(out_acc)
        gin_acc[...] = jnp.zeros_like(gin_acc)
        for fetch in fetches():
            fetch.wait()

    rows = rows_ref[...]
    here = pl.ds(pl.multiple_of(j * tile, tile), tile)
    up = up_s[:, here]
    down = down_s[here, :]
    hid, slope = gelu_pair(dot(rows, up, 1, 0))
    hid = hid.astype(BF)
    gpre = (dot(scaled[...], down, 1, 1) * slope).astype(BF)
    out_acc[...] += dot(hid, down, 1, 0)
    gin_acc[...] += dot(gpre, up, 1, 1)

    if train:
        hid_ref[...] = hid
        gpre_ref[...] = gpre

        @pl.when(j == 0)
        def _():
            scaled_ref[...] = scaled[...]

    @pl.when(j == steps - 1)
    def _():
        produced = out_acc[...].astype(BF).astype(F32)
        gate = gate_s[:, 0:1]
        gated_ref[...] = (produced * gate).astype(BF)
        grad_gate = jnp.sum(produced * grads(), axis=1, keepdims=True)
        gl = (grad_gate * gate * (mine - probs_s[...])).astype(BF)
        gin_ref[...] = (gin_acc[...] + dot(gl, router_ref[...], 1, 0)).astype(BF)
        rgrad_ref[...] = dot(gl, rows_ref[...], 0, 0)


def expert_call(owners, mine, rows, grads, router_pad, ups, downs, train):
    n, d = rows.shape
    pieces = len(ups)
    f = ups[0].shape[1]
    tile = max(d, f // pieces)
    steps = f // tile
    peers, _, capacity, _ = grads.shape
    member = 1 if train else 0
    one = pl.Buffered(buffer_count=1)

    def all_of(shape):
        return pl.BlockSpec(shape, lambda j: (0,) * len(shape), pipeline_mode=one)

    slot_spec = pl.BlockSpec(
        (peers, 1, capacity, d), lambda j: (0, member, 0, 0), pipeline_mode=one
    )
    anywhere = pl.BlockSpec(memory_space=pl.ANY)
    outs = [((n, d), BF), ((n, d), BF), ((128, d), F32)]
    out_specs = [all_of((n, d)), all_of((n, d)), all_of((128, d))]
    if train:
        outs += [((n, f), BF)] * 2 + [((n, d), BF)]
        out_specs += [pl.BlockSpec((n, tile), lambda j: (0, j))] * 2 + [all_of((n, d))]
    args = [owners, mine, rows, grads, router_pad, *ups, *downs]
    return pl.pallas_call(
        functools.partial(expert_kernel, train, steps, pieces),
        grid=(steps,),
        in_specs=[
            pl.BlockSpec(memory_space=pltpu.SMEM),
            all_of((8, 128)),
            all_of((n, d)),
            slot_spec,
            all_of((128, d)),
        ]
        + [anywhere] * (2 * pieces),
        out_specs=out_specs,
        out_shape=[whole(o) for o in outs],
        scratch_shapes=[
            pltpu.VMEM((d, f), BF),
            pltpu.VMEM((f, d), BF),
            pltpu.VMEM((n, d), F32),
            pltpu.VMEM((n, d), F32),
            pltpu.VMEM((n, d), BF),
            pltpu.VMEM((n, 128), F32),
            pltpu.VMEM((n, 128), F32),
            pltpu.SemaphoreType.DMA((2, pieces)),
        ],
        compiler_params=pltpu.CompilerParams(vmem_limit_bytes=LIMIT),
        cost_estimate=cost(29),
        name="expert_new" if train else "expert_old",
    )(*args)


def weight_grads_kernel(
    pieces,
    place_ref,
    rows_ref,
    scaled_ref,
    hid_ref,
    gpre_ref,
    upkeep_ref,
    upsend_ref,
    downkeep_ref,
    downsend_ref,
):
    j = pl.program_id(0)
    core = place_ref[0] % 2
    half, up_rows, tile = upkeep_ref.shape
    down_rows = downkeep_ref.shape[1]
    grad_up = dot(rows_ref[...], gpre_ref[...], 0, 0).astype(BF)
    for pair in range(half):
        first = grad_up[2 * pair * up_rows : (2 * pair + 1) * up_rows]
        second = grad_up[(2 * pair + 1) * up_rows : (2 * pair + 2) * up_rows]
        upkeep_ref[pair] = jnp.where(core == 0, first, second)
        upsend_ref[pair] = jnp.where(core == 0, second, first)
    grad_down = dot(hid_ref[...], scaled_ref[...], 0, 0).astype(BF)
    inside = tile // down_rows
    for at in range(inside):
        block = grad_down[at * down_rows : (at + 1) * down_rows]
        owner = j * inside + at

        @pl.when(owner % 2 == core)
        def _():
            downkeep_ref[owner // 2] = block

        @pl.when(owner % 2 != core)
        def _():
            downsend_ref[owner // 2] = block


def weight_grads_call(owners, rows, scaled, hidden, grad_pre):
    n, d = rows.shape
    f = hidden.shape[1]
    pieces = owners.shape[0]
    half = pieces // 2
    tile = max(d, f // pieces)
    one = pl.Buffered(buffer_count=1)
    up_shape = (half, d // pieces, f)
    down_shape = (half, f // pieces, d)
    flat = pl.BlockSpec((n, d), lambda j: (0, 0), pipeline_mode=one)
    tiled = pl.BlockSpec((n, tile), lambda j: (0, j))
    return pl.pallas_call(
        functools.partial(weight_grads_kernel, pieces),
        grid=(f // tile,),
        in_specs=[pl.BlockSpec(memory_space=pltpu.SMEM), flat, flat, tiled, tiled],
        out_specs=[pl.BlockSpec((half, d // pieces, tile), lambda j: (0, 0, j))] * 2
        + [pl.BlockSpec(down_shape, lambda j: (0, 0, 0), pipeline_mode=one)] * 2,
        out_shape=[whole((up_shape, BF))] * 2 + [whole((down_shape, BF))] * 2,
        compiler_params=pltpu.CompilerParams(vmem_limit_bytes=LIMIT),
        cost_estimate=cost(14),
        name="weight_grads",
    )(owners, rows, scaled, hidden, grad_pre)


def shards(
    block_input,
    cotangent,
    attn_in,
    attn_out,
    router,
    ln1_gain,
    ln1_bias,
    ln2_gain,
    ln2_bias,
    new_w1,
    new_w2,
    old_w1,
    old_w2,
    expert_ids,
    slots,
    drops,
):
    length, width = block_input.shape
    peers = lax.axis_size("expert")
    devices = lax.axis_size("dp") * peers
    experts = 2 * peers
    capacity = max(length * 7 // (2 * experts), 2)
    me = lax.axis_index("expert")
    ways, scatter_ways = orders()
    third = width // 3
    in_share = attn_in.shape[1]
    share = width // devices

    small = jnp.concatenate(
        [v[None] for v in (ln1_gain, ln1_bias, ln2_gain, ln2_bias)] + [router.T], axis=0
    )
    lines = small.shape[0]
    small = jnp.pad(small, ((0, -lines % 8), (0, third - share)))
    in_t, out_t = attn_in.T, attn_out.T
    states = []
    for p in range(3):
        cols = slice(p * third, (p + 1) * third)
        rows = [in_t[:, cols], out_t[:, cols]] + ([small] if p == 0 else [])
        states.append((jnp.concatenate(rows, axis=0), []))
    states = [gather_steps(states[p], ways[p][:2]) for p in range(3)]
    shards_dp = [old_w1[0], old_w2[0], new_w1[0], new_w2[0]]
    early = [state[0] for state in states]
    states = [gather_steps(states[p], ways[p][2:-1]) for p in range(3)]
    between = [state[0] for state in states]
    parts = [gather_finish(gather_steps(states[p], ways[p][-1:])) for p in range(3)]
    parts = [part.reshape(devices, -1, third) for part in parts]
    in_parts = [part[:, :in_share].reshape(3 * width, third) for part in parts]
    out_parts = [part[:, in_share : in_share + share].reshape(width, third) for part in parts]
    small_full = parts[0][:, in_share + share : in_share + share + lines, :share]
    small_full = small_full.transpose(1, 0, 2).reshape(lines, width)
    vectors = jnp.pad(small_full[:4].astype(F32), ((0, 4), (0, 0)))
    router_pad = jnp.pad(small_full[4:], ((0, 128 - experts), (0, 0)))

    target = jnp.where(drops == 0, expert_ids * capacity + slots, -1)
    by_member = ((expert_ids % 2) * peers + expert_ids // 2) * capacity + slots
    by_member = jnp.where(drops == 0, by_member, -1)
    target_rows = jnp.pad(target.T, ((0, 6), (0, 0)), constant_values=-1)
    member_rows = jnp.pad(by_member.T, ((0, 6), (0, 0)), constant_values=-1)
    count = peers * capacity
    both_shape = (peers, 2, capacity, width)

    def move(block):
        return lax.all_to_all(block, "expert", split_axis=0, concat_axis=0, tiled=True)

    def send(block, *earlier):
        block = after(block, *earlier).reshape(peers, capacity, width)
        return move(block).reshape(count, width)

    (grad_slots,) = plain_call(
        place_kernel, [((2 * count, width), BF)], [], "place_grads", 4, target_rows, after(cotangent, early)
    )
    grads = move(after(grad_slots, between).reshape(both_shape))
    slot_outs = [((count, width), BF)] * 2

    normed, proj, context, middle, rold, rnew = plain_call(
        forward_kernel,
        [
            ((length, width), BF),
            ((length, 3 * width), BF),
            ((length, width), BF),
            ((length, width), F32),
        ]
        + slot_outs,
        [],
        "attention_forward", 27,
        block_input,
        *in_parts,
        *out_parts,
        vectors,
        member_rows,
    )
    owners = lax.axis_index("dp") ^ jnp.arange(lax.axis_size("dp"), dtype=jnp.int32)
    far = [dp_far(after(shard, between)) for shard in shards_dp[:2]]
    far.append(dp_far(after(shards_dp[2], between, far)))
    far.append(dp_far(after(shards_dp[3], between, far)))
    near = [{away: core_swap(piece) for away, piece in f.items()} for f in far[:3]]
    rold = send(rold, grads, far[:2])
    own = [core_swap(after(shard, grads)) for shard in shards_dp]
    rnew = send(rnew, rold, near, own)

    lane = lax.broadcasted_iota(jnp.int32, (8, 128), 1)
    line = lax.broadcasted_iota(jnp.int32, (8, 128), 0)

    def chosen(expert):
        return jnp.where(line == 0, (lane == expert).astype(F32), F32(experts))

    pieces = [dp_pieces(shards_dp[i], own[i], far[i], near[i]) for i in range(2)]
    old_gated, old_in, old_router = expert_call(
        owners, chosen(2 * me), rold, grads, router_pad, *pieces, False
    )
    near.append({away: core_swap(after(piece, old_in)) for away, piece in far[3].items()})
    pieces = [dp_pieces(shards_dp[i], own[i], far[i], near[i]) for i in range(2, 4)]
    rnew, old_in = lax.optimization_barrier((rnew, old_in))
    old_in = send(old_in, rnew)
    new_gated, new_in, new_router, hidden, grad_pre, scaled = expert_call(
        owners, chosen(2 * me + 1), rnew, grads, router_pad, *pieces, True
    )
    up_keep, up_send, down_keep, down_send = weight_grads_call(
        owners, rnew, scaled, hidden, grad_pre
    )
    new_in = send(new_in, old_in)
    ups = [up_keep, core_swap(after(up_send, old_in))]
    downs = [down_keep, core_swap(after(down_send, old_in))]
    old_gated = send(old_gated, new_in)
    router_part = (old_router + new_router)[:experts]

    gmid, gctx, out_grad, sums_two = plain_call(
        branch_kernel,
        [
            ((length, width), F32),
            ((length, width), BF),
            ((width, width), BF),
            ((8, width), F32),
        ],
        [],
        "branch_backward",
        8,
        old_in,
        new_in,
        by_member,
        cotangent,
        middle,
        context,
        *out_parts,
        vectors,
    )
    accumulators = [pltpu.VMEM((length, 2 * HEAD_DIM), F32)] * 2
    (gfirst,) = plain_call(
        attention_first_kernel,
        [((length, 3 * width // 2), BF)],
        accumulators,
        "attention_backward_first",
        40,
        proj,
        gctx,
    )
    new_gated = send(new_gated, old_gated, gfirst)
    ups_first, downs_first = [scatter_dp_first(after(sums, gctx)) for sums in (ups, downs)]
    ups_x = scatter_dp(ups, ups_first)
    downs_x = scatter_dp(downs, downs_first)
    gfirst = after(gfirst, ups_x)
    half = lax.axis_size("dp") // 2
    gproj, *split = plain_call(
        attention_back_kernel,
        [((length, 3 * width), BF)] + [((half, 3 * width // (2 * half), third), BF)] * 6,
        accumulators,
        "attention_backward",
        40,
        owners,
        proj,
        gctx,
        normed,
        gfirst,
    )
    input_grad, sums_one = plain_call(
        input_kernel,
        [((length, width), F32), ((8, width), F32)],
        [],
        "input_backward", 20,
        gproj,
        *in_parts,
        block_input,
        vectors,
        gmid,
    )
    lead = canonical()
    core = [("dp", powers(lax.axis_size("dp"))[0])]
    states = []
    left = [step for step in lead if step != core[0]]
    for keep, away in zip(split[:3], split[3:]):
        addends = [keep, swap(away, *core[0])]
        states.append([a.reshape([2] * len(left) + [in_share, third]) for a in addends])
    small_grads = jnp.concatenate([sums_one[:2], sums_two[:2], router_part], axis=0)
    small_grads = small_grads.reshape(lines, devices, share).transpose(1, 0, 2)
    small_grads = small_grads.reshape(devices, 1, lines * share).astype(BF)
    small_rows = -(-lines * share // width)
    small_grads = jnp.pad(small_grads, ((0, 0), (0, 0), (0, small_rows * width - lines * share)))
    rest = jnp.concatenate(
        [out_grad.reshape(devices, share, width), small_grads.reshape(devices, small_rows, width)],
        axis=1,
    )
    rest = rest.reshape([2] * len(lead) + list(rest.shape[1:]))
    got = scatter_step([rest], lead, core[0])
    states.append(scatter_rest([rest], lead, core[0], got)[0])
    states = after(states, old_gated, new_gated, downs_x)
    lefts = [left] * len(states)
    for at in range(len(left)):
        arrived = [
            scatter_step(state, left, way[at])
            for state, left, way in zip(states, lefts, scatter_ways)
        ]
        if at == 0:
            (mixed,) = plain_call(
                mixed_kernel,
                [((length, width), BF)],
                [],
                "mixed_output", 5,
                *after((old_gated, new_gated), arrived),
                by_member,
                middle,
            )
        if at == 1:
            (ups, downs, ups_x, downs_x), _ = lax.optimization_barrier(
                ((ups, downs, ups_x, downs_x), arrived)
            )
            new_w1_grad = scatter_dp_total(ups, ups_x)[None]
            new_w2_grad = scatter_dp_total(downs, downs_x)[None]
        pairs = [
            scatter_rest(state, left, way[at], got)
            for state, left, way, got in zip(states, lefts, scatter_ways, arrived)
        ]
        states = [pair[0] for pair in pairs]
        lefts = [pair[1] for pair in pairs]
    sums = [total(state) for state in states]
    attn_in_grad = jnp.concatenate(sums[:3], axis=1).T
    attn_out_grad = sums[3][:share].T
    small_grads = sums[3][share:].reshape(-1)[: lines * share].reshape(lines, share)
    vector_grads = small_grads[:4]
    router_grad = small_grads[4:].T
    return (
        mixed,
        input_grad,
        attn_in_grad,
        attn_out_grad,
        router_grad,
        vector_grads[0],
        vector_grads[1],
        vector_grads[2],
        vector_grads[3],
        new_w1_grad,
        new_w2_grad,
    )


def solution(mesh):
    both = ("dp", "expert")
    rows = P(both, None)
    columns = P(None, both)
    vector = P(both)
    weight = P("expert", "dp", None)
    in_specs = (
        [rows, rows, columns, columns, rows] + [vector] * 4 + [weight] * 4 + [rows] * 3
    )
    out_specs = [rows, rows, columns, columns, rows] + [vector] * 4 + [weight] * 2
    return jax.shard_map(
        shards, mesh=mesh, in_specs=tuple(in_specs), out_specs=tuple(out_specs), check_vma=False
    )
```

```python
import functools

import jax
import jax.numpy as jnp
from jax import lax
from jax.experimental import pallas as pl
from jax.experimental.pallas import tpu as pltpu
from jax.sharding import PartitionSpec as P

HEADS = 12
HEAD_DIM = 64
BF = jnp.bfloat16
F32 = jnp.float32


def mm(a, b, dims, out=F32):
    return lax.dot_general(a, b, (dims, ((), ())), preferred_element_type=F32).astype(out)


def powers(count):
    found = []
    bit = 1
    while bit < count:
        found.append(bit)
        bit *= 2
    return found


def swap(values, axis, bit):
    count = lax.axis_size(axis)
    return lax.ppermute(values, axis, [(i, i ^ bit) for i in range(count)])


def my_bit(axis, bit):
    return (lax.axis_index(axis) // bit) % 2


def canonical():
    return [("dp", b) for b in reversed(powers(lax.axis_size("dp")))] + [
        ("expert", b) for b in reversed(powers(lax.axis_size("expert")))
    ]


def orders():
    dp_bits = powers(lax.axis_size("dp"))
    expert_bits = powers(lax.axis_size("expert"))
    core = [("dp", dp_bits[0])]
    xs = [("dp", b) for b in reversed(dp_bits[1:])]
    ys = [("expert", expert_bits[0])]
    zs = [("expert", b) for b in reversed(expert_bits[1:])]
    gathering = (zs + ys + xs + core, xs + zs + ys + core, ys + xs + zs + core)
    near = zs[::-1]
    summing = (xs + ys + near, ys + near + xs, near + xs + ys, near + ys + xs)
    return gathering, summing


def gather_steps(state, order):
    current, lead = state
    lead = list(lead)
    for axis, bit in order:
        other = swap(current, axis, bit)
        low = my_bit(axis, bit) == 0
        current = jnp.stack([jnp.where(low, current, other), jnp.where(low, other, current)])
        lead.insert(0, (axis, bit))
    return current, lead


def gather_finish(state):
    current, lead = state
    tail = current.shape[len(lead) :]
    perm = [lead.index(w) for w in canonical()]
    current = current.transpose(perm + list(range(len(lead), current.ndim)))
    return current.reshape((-1,) + tail)


def after(values, *earlier):
    if not earlier:
        return values
    return lax.optimization_barrier((values, earlier))[0]


def total(addends):
    found = addends[0].astype(F32)
    for addend in addends[1:]:
        found = found + addend.astype(F32)
    return found


def away_part(addends, lead, step):
    at = lead.index(step)
    mine = my_bit(*step)
    send = total([lax.dynamic_index_in_dim(a, 1 - mine, at, keepdims=False) for a in addends])
    return send.astype(BF)


def scatter_step(addends, lead, step):
    return swap(away_part(addends, lead, step), *step)


def scatter_rest(addends, lead, step, got):
    at = lead.index(step)
    addends = [lax.dynamic_index_in_dim(a, my_bit(*step), at, keepdims=False) for a in addends]
    return addends + [got], lead[:at] + lead[at + 1 :]


def core_swap(piece):
    return swap(piece, "dp", powers(lax.axis_size("dp"))[0])


def dp_far(shard):
    far = {}
    for bit in powers(lax.axis_size("dp"))[1:]:
        for away, piece in [(0, shard), *far.items()]:
            far[away ^ bit] = swap(piece, "dp", bit)
    return far


def dp_pieces(shard, own, far, near):
    core = powers(lax.axis_size("dp"))[0]
    found = {0: shard, core: own, **far}
    found.update({away ^ core: piece for away, piece in near.items()})
    return [found[away] for away in range(len(found))]


def x_steps():
    return [("dp", b) for b in powers(lax.axis_size("dp"))[1:]]


def scatter_dp_first(addends):
    order = x_steps()
    addends = [a.reshape([2] * len(order) + list(a.shape[1:])) for a in addends]
    return away_part(addends, order[::-1], order[0])


def scatter_dp(addends, first):
    order = x_steps()
    lead = order[::-1]
    addends = [a.reshape([2] * len(order) + list(a.shape[1:])) for a in addends]
    arrived = [swap(first, *order[0])]
    for at, step in enumerate(order[1:]):
        addends, lead = scatter_rest(addends, lead, order[at], arrived[-1])
        arrived.append(scatter_step(addends, lead, step))
    return arrived


def scatter_dp_total(addends, arrived):
    order = x_steps()
    lead = order[::-1]
    addends = [a.reshape([2] * len(order) + list(a.shape[1:])) for a in addends]
    for step, got in zip(order, arrived):
        addends, lead = scatter_rest(addends, lead, step, got)
    return total(addends)


LIMIT = 56 * 1024 * 1024
QUERY_BLOCK = 512
SCALE = HEAD_DIM ** (-0.5)


def dot(a, b, over_a, over_b):
    return lax.dot_general(
        a, b, (((over_a,), (over_b,)), ((), ())), preferred_element_type=F32
    )


def dot_parts(values, parts):
    width = parts[0].shape[1]
    total = None
    for at, part in enumerate(parts):
        term = dot(values[:, at * width : (at + 1) * width], part, 1, 1)
        total = term if total is None else total + term
    return total


def whole(array):
    return jax.ShapeDtypeStruct(array[0], array[1])


def cost(micros):
    return pl.CostEstimate(flops=int(micros * 0.25e9), bytes_accessed=0, transcendentals=0)


def plain_call(body, outs, scratch, name, micros, *args):
    space = pl.BlockSpec(memory_space=pltpu.VMEM)
    return pl.pallas_call(
        body,
        out_shape=[whole(o) for o in outs],
        in_specs=[space] * len(args),
        out_specs=[space] * len(outs),
        scratch_shapes=scratch,
        compiler_params=pltpu.CompilerParams(vmem_limit_bytes=LIMIT),
        cost_estimate=cost(micros),
        name=name,
    )(*args)


def norm_parts(values):
    centre = values - jnp.mean(values, axis=-1, keepdims=True)
    spread = jnp.mean(centre * centre, axis=-1, keepdims=True)
    scale = lax.rsqrt(spread + 1e-05)
    return centre * scale, scale


def norm_back(values, gain, grad):
    normal, scale = norm_parts(values)
    scaled = grad * gain
    back = scale * (
        scaled
        - jnp.mean(scaled, axis=-1, keepdims=True)
        - normal * jnp.mean(scaled * normal, axis=-1, keepdims=True)
    )
    return back, jnp.sum(grad * normal, axis=0, keepdims=True), jnp.sum(grad, axis=0, keepdims=True)


def place_rows(target_ref, values, first, count):
    tokens = values.shape[0]
    at = lax.broadcasted_iota(jnp.int32, (count, tokens), 0) + first
    hit = (at == target_ref[0:1, :]) | (at == target_ref[1:2, :])
    return dot(hit.astype(F32).astype(BF), values, 1, 0).astype(BF)


def place_kernel(target_ref, values_ref, slots_ref):
    values = values_ref[...]
    part = slots_ref.shape[0] // 4
    for at in range(4):
        slots_ref[at * part : (at + 1) * part, :] = place_rows(
            target_ref, values, at * part, part
        )


def take_rows(target_ref, slots_refs, tokens):
    total = None
    first = 0
    for ref in slots_refs:
        count = ref.shape[0]
        at = lax.broadcasted_iota(jnp.int32, (tokens, count), 1) + first
        hit = (at == target_ref[:, 0:1]) | (at == target_ref[:, 1:2])
        part = dot(hit.astype(F32).astype(BF), ref[...], 1, 0)
        total = part if total is None else total + part
        first += count
    return total


def causal(size):
    rowpos = lax.broadcasted_iota(jnp.int32, (size, size), 0)
    colpos = lax.broadcasted_iota(jnp.int32, (size, size), 1)
    return rowpos >= colpos


def head_lanes(block, which):
    lane = lax.broadcasted_iota(jnp.int32, block.shape, 1)
    keep = (lane < HEAD_DIM) if which == 0 else (lane >= HEAD_DIM)
    return jnp.where(keep, block, jnp.zeros_like(block))


def block_softmax(query, keys, seen):
    size = query.shape[0]
    before = keys.shape[0] - size
    own = dot(query, keys[before:], 1, 1)
    own = jnp.where(seen, own, -1e30)
    top = jnp.max(own, axis=-1, keepdims=True)
    if before:
        past = dot(query, keys[:before], 1, 1)
        top = jnp.maximum(top, jnp.max(past, axis=-1, keepdims=True))
        past = jnp.exp(past - top)
    own = jnp.exp(own - top)
    total = jnp.sum(own, axis=-1, keepdims=True)
    if before:
        total = total + jnp.sum(past, axis=-1, keepdims=True)
    inverse = 1.0 / total
    own = own * inverse
    return (past * inverse, own) if before else (own,)


def pair_columns(pair, part, width):
    return pl.ds(pl.multiple_of(part * width + pair * 2 * HEAD_DIM, 2 * HEAD_DIM), 2 * HEAD_DIM)


def forward_kernel(
    x_ref,
    in0_ref,
    in1_ref,
    in2_ref,
    out0_ref,
    out1_ref,
    out2_ref,
    vec_ref,
    target_ref,
    normed_ref,
    proj_ref,
    context_ref,
    middle_ref,
    old_ref,
    new_ref,
):
    length, width = x_ref.shape
    x = x_ref[...].astype(F32)
    normal, _ = norm_parts(x)
    normed = (normal * vec_ref[0:1, :] + vec_ref[1:2, :]).astype(BF)
    normed_ref[...] = normed
    for part in range(3):
        cols = slice(part * width, (part + 1) * width)
        proj_ref[:, cols] = dot_parts(
            normed, [ref[cols, :] for ref in (in0_ref, in1_ref, in2_ref)]
        ).astype(BF)
    size = min(QUERY_BLOCK, length)
    seen = causal(size)

    def one_pair(pair, carry):
        q_at, k_at, v_at = (pair_columns(pair, part, width) for part in range(3))
        for block in range(length // size):
            rows = slice(block * size, (block + 1) * size)
            upto = (block + 1) * size
            query = proj_ref[rows, q_at] * BF(SCALE)
            keys = proj_ref[0:upto, k_at]
            values = proj_ref[0:upto, v_at]
            outs = []
            for which in range(2):
                probs = block_softmax(head_lanes(query, which), keys, seen)
                probs = [p.astype(BF) for p in probs]
                out = dot(probs[-1], values[upto - size :], 1, 0)
                if len(probs) > 1:
                    out = out + dot(probs[0], values[: upto - size], 1, 0)
                outs.append(out)
            lane = lax.broadcasted_iota(jnp.int32, outs[0].shape, 1)
            context_ref[rows, pair_columns(pair, 0, width)] = jnp.where(
                lane < HEAD_DIM, outs[0], outs[1]
            ).astype(BF)
        return carry

    lax.fori_loop(0, HEADS // 2, one_pair, 0)
    middle = x + dot_parts(context_ref[...], [ref[...] for ref in (out0_ref, out1_ref, out2_ref)])
    middle_ref[...] = middle
    normal, _ = norm_parts(middle)
    normed_two = (normal * vec_ref[2:3, :] + vec_ref[3:4, :]).astype(BF)
    count = old_ref.shape[0]
    half = count // 2
    for at, ref in ((0, old_ref), (count, new_ref)):
        for part in range(2):
            ref[part * half : (part + 1) * half, :] = place_rows(
                target_ref, normed_two, at + part * half, half
            )


def branch_kernel(
    old_ref,
    new_ref,
    target_ref,
    cot_ref,
    middle_ref,
    context_ref,
    out0_ref,
    out1_ref,
    out2_ref,
    vec_ref,
    gmid_ref,
    gctx_ref,
    outgrad_ref,
    sums_ref,
):
    length, width = cot_ref.shape
    grad = take_rows(target_ref, (old_ref, new_ref), length)
    back, gain_sum, bias_sum = norm_back(middle_ref[...], vec_ref[2:3, :], grad)
    gmid = back + cot_ref[...].astype(F32)
    gmid_ref[...] = gmid
    sums_ref[...] = jnp.concatenate([gain_sum, bias_sum, jnp.zeros((6, width), F32)], axis=0)
    branch = gmid.astype(BF)
    third = width // 3
    for part, ref in enumerate((out0_ref, out1_ref, out2_ref)):
        gctx_ref[:, part * third : (part + 1) * third] = dot(branch, ref[...], 1, 0).astype(BF)
    outgrad_ref[...] = dot(branch, context_ref[...], 0, 0).astype(BF)


def pairs_back(proj_ref, gctx_ref, gproj_ref, gk_acc, gv_acc):
    length, width = gctx_ref.shape
    size = min(QUERY_BLOCK, length)
    seen = causal(size)

    def one_pair(pair, carry):
        q_at, k_at, v_at = (pair_columns(pair, part, width) for part in range(3))
        gk_acc[...] = jnp.zeros_like(gk_acc)
        gv_acc[...] = jnp.zeros_like(gv_acc)
        for block in range(length // size):
            rows = slice(block * size, (block + 1) * size)
            upto = (block + 1) * size
            query = proj_ref[rows, q_at] * BF(SCALE)
            keys = proj_ref[0:upto, k_at]
            values = proj_ref[0:upto, v_at]
            gout = gctx_ref[rows, pair_columns(pair, 0, width)]
            grads = []
            for which in range(2):
                mine = head_lanes(query, which)
                gmine = head_lanes(gout, which)
                probs = block_softmax(mine, keys, seen)
                spans = [slice(upto - size, upto)]
                if len(probs) > 1:
                    spans = [slice(0, upto - size)] + spans
                gprobs = [dot(gmine, values[s], 1, 1) for s in spans]
                row = sum(jnp.sum(p * g, axis=-1, keepdims=True) for p, g in zip(probs, gprobs))
                gquery = None
                for p, g, s in zip(probs, gprobs, spans):
                    gscore = (p * (g - row)).astype(BF)
                    part = dot(gscore, keys[s], 1, 0)
                    gquery = part if gquery is None else gquery + part
                    gk_acc[s, :] += dot(gscore, mine, 0, 0)
                    gv_acc[s, :] += dot(p.astype(BF), gmine, 0, 0)
                grads.append(gquery * SCALE)
            lane = lax.broadcasted_iota(jnp.int32, grads[0].shape, 1)
            gproj_ref[rows, q_at] = jnp.where(lane < HEAD_DIM, grads[0], grads[1]).astype(BF)
        gproj_ref[:, k_at] = gk_acc[...].astype(BF)
        gproj_ref[:, v_at] = gv_acc[...].astype(BF)
        return carry

    lax.fori_loop(0, HEADS // 2, one_pair, 0)

def attention_back_kernel(
    place_ref,
    proj_ref,
    gctx_ref,
    normed_ref,
    gproj_ref,
    keep0_ref,
    keep1_ref,
    keep2_ref,
    send0_ref,
    send1_ref,
    send2_ref,
    gk_acc,
    gv_acc,
):
    width = gctx_ref.shape[1]
    pairs_back(proj_ref, gctx_ref, gproj_ref, gk_acc, gv_acc)
    third = width // 3
    core = place_ref[0] % 2
    halves, rows, _ = keep0_ref.shape
    refs = ((keep0_ref, send0_ref), (keep1_ref, send1_ref), (keep2_ref, send2_ref))
    for part, (keep_ref, send_ref) in enumerate(refs):
        grad = dot(gproj_ref[...], normed_ref[:, part * third : (part + 1) * third], 0, 0)
        grad = grad.astype(BF)
        for at in range(halves):
            first = grad[2 * at * rows : (2 * at + 1) * rows]
            second = grad[(2 * at + 1) * rows : (2 * at + 2) * rows]
            keep_ref[at] = jnp.where(core == 0, first, second)
            send_ref[at] = jnp.where(core == 0, second, first)


def input_kernel(
    gproj_ref, in0_ref, in1_ref, in2_ref, x_ref, vec_ref, gmid_ref, grad_ref, sums_ref
):
    grad = jnp.concatenate(
        [dot(gproj_ref[...], ref[...], 1, 0) for ref in (in0_ref, in1_ref, in2_ref)], axis=1
    )
    back, gain_sum, bias_sum = norm_back(x_ref[...].astype(F32), vec_ref[0:1, :], grad)
    grad_ref[...] = gmid_ref[...] + back
    width = x_ref.shape[1]
    sums_ref[...] = jnp.concatenate([gain_sum, bias_sum, jnp.zeros((6, width), F32)], axis=0)


def mixed_kernel(slots_ref, target_ref, middle_ref, mixed_ref):
    total = take_rows(target_ref, (slots_ref,), middle_ref.shape[0])
    mixed_ref[...] = (middle_ref[...] + total).astype(BF)


def gelu_pair(x):
    c = 0.7978845608028654
    sq = x * x
    t = jnp.tanh(c * x * (1.0 + 0.044715 * sq))
    half = 0.5 * (1.0 + t)
    slope = half + 0.5 * x * (1.0 - t * t) * (c * (1.0 + 3 * 0.044715 * sq))
    return x * half, slope

def expert_kernel(train, steps, pieces, place_ref, mine_ref, rows_ref, grads4_ref, router_ref, *rest):
    ups, downs, rest = rest[:pieces], rest[pieces : 2 * pieces], rest[2 * pieces :]
    if train:
        _, gated_ref, gin_ref, rgrad_ref, hid_ref, gpre_ref, scaled_ref = rest[:7]
        rest = rest[7:]
    else:
        gated_ref, gin_ref, rgrad_ref = rest[:3]
        rest = rest[3:]
    up_s, down_s, out_acc, gin_acc, scaled, gate_s, probs_s, sems = rest
    j = pl.program_id(0)
    mine = mine_ref[0:1, :]
    up_rows = up_s.shape[0] // pieces
    down_rows = down_s.shape[0] // pieces
    tile = up_s.shape[1] // steps

    def grads():
        return grads4_ref[...].reshape(rows_ref.shape).astype(F32)

    def fetches():
        found = []
        for at in range(pieces):
            owner = place_ref[at]
            to = pl.ds(pl.multiple_of(owner * up_rows, up_rows), up_rows)
            found.append(pltpu.make_async_copy(ups[at], up_s.at[to], sems.at[0, at]))
            to = pl.ds(pl.multiple_of(owner * down_rows, down_rows), down_rows)
            found.append(pltpu.make_async_copy(downs[at], down_s.at[to], sems.at[1, at]))
        return found

    @pl.when(j == 0)
    def _():
        for fetch in fetches():
            fetch.start()
        logits = dot(rows_ref[...], router_ref[...], 1, 1)
        live = lax.broadcasted_iota(jnp.int32, logits.shape, 1) < mine_ref[1, 0].astype(jnp.int32)
        logits = jnp.where(live, logits, -1e30)
        e = jnp.exp(logits - jnp.max(logits, axis=1, keepdims=True))
        probs = e / jnp.sum(e, axis=1, keepdims=True)
        probs_s[...] = probs
        gate = jnp.sum(probs * mine, axis=1, keepdims=True)
        gate_s[...] = jnp.broadcast_to(gate, gate_s.shape)
        scaled[...] = (grads() * gate).astype(BF)
        out_acc[...] = jnp.zeros_like(out_acc)
        gin_acc[...] = jnp.zeros_like(gin_acc)
        for fetch in fetches():
            fetch.wait()

    rows = rows_ref[...]
    here = pl.ds(pl.multiple_of(j * tile, tile), tile)
    up = up_s[:, here]
    down = down_s[here, :]
    hid, slope = gelu_pair(dot(rows, up, 1, 0))
    hid = hid.astype(BF)
    gpre = (dot(scaled[...], down, 1, 1) * slope).astype(BF)
    out_acc[...] += dot(hid, down, 1, 0)
    gin_acc[...] += dot(gpre, up, 1, 1)

    if train:
        hid_ref[...] = hid
        gpre_ref[...] = gpre

        @pl.when(j == 0)
        def _():
            scaled_ref[...] = scaled[...]

    @pl.when(j == steps - 1)
    def _():
        produced = out_acc[...].astype(BF).astype(F32)
        gate = gate_s[:, 0:1]
        gated_ref[...] = (produced * gate).astype(BF).reshape(gated_ref.shape)
        grad_gate = jnp.sum(produced * grads(), axis=1, keepdims=True)
        gl = (grad_gate * gate * (mine - probs_s[...])).astype(BF)
        gin_ref[...] = (gin_acc[...] + dot(gl, router_ref[...], 1, 0)).astype(BF)
        rgrad_ref[...] = dot(gl, rows_ref[...], 0, 0)


def expert_call(owners, mine, rows, grads, router_pad, ups, downs, gated=None):
    train = gated is not None
    n, d = rows.shape
    pieces = len(ups)
    f = ups[0].shape[1]
    tile = max(d, f // pieces)
    steps = f // tile
    peers, _, capacity, _ = grads.shape
    member = 1 if train else 0
    one = pl.Buffered(buffer_count=1)

    def all_of(shape):
        return pl.BlockSpec(shape, lambda j: (0,) * len(shape), pipeline_mode=one)

    slot_spec = pl.BlockSpec(
        (peers, 1, capacity, d), lambda j: (0, member, 0, 0), pipeline_mode=one
    )
    anywhere = pl.BlockSpec(memory_space=pl.ANY)
    outs = [(grads.shape, BF), ((n, d), BF), ((128, d), F32)]
    out_specs = [slot_spec, all_of((n, d)), all_of((128, d))]
    if train:
        outs += [((n, f), BF)] * 2 + [((n, d), BF)]
        out_specs += [pl.BlockSpec((n, tile), lambda j: (0, j))] * 2 + [all_of((n, d))]
    args = [owners, mine, rows, grads, router_pad, *ups, *downs] + ([gated] if train else [])
    return pl.pallas_call(
        functools.partial(expert_kernel, train, steps, pieces),
        grid=(steps,),
        in_specs=[
            pl.BlockSpec(memory_space=pltpu.SMEM),
            all_of((8, 128)),
            all_of((n, d)),
            slot_spec,
            all_of((128, d)),
        ]
        + [anywhere] * (2 * pieces + train),
        out_specs=out_specs,
        out_shape=[whole(o) for o in outs],
        scratch_shapes=[
            pltpu.VMEM((d, f), BF),
            pltpu.VMEM((f, d), BF),
            pltpu.VMEM((n, d), F32),
            pltpu.VMEM((n, d), F32),
            pltpu.VMEM((n, d), BF),
            pltpu.VMEM((n, 128), F32),
            pltpu.VMEM((n, 128), F32),
            pltpu.SemaphoreType.DMA((2, pieces)),
        ],
        input_output_aliases={len(args) - 1: 0} if train else {},
        compiler_params=pltpu.CompilerParams(vmem_limit_bytes=LIMIT),
        cost_estimate=cost(29),
        name="expert_new" if train else "expert_old",
    )(*args)


def weight_grads_kernel(
    pieces,
    place_ref,
    rows_ref,
    scaled_ref,
    hid_ref,
    gpre_ref,
    upkeep_ref,
    upsend_ref,
    downkeep_ref,
    downsend_ref,
):
    j = pl.program_id(0)
    core = place_ref[0] % 2
    half, up_rows, tile = upkeep_ref.shape
    down_rows = downkeep_ref.shape[1]
    grad_up = dot(rows_ref[...], gpre_ref[...], 0, 0).astype(BF)
    for pair in range(half):
        first = grad_up[2 * pair * up_rows : (2 * pair + 1) * up_rows]
        second = grad_up[(2 * pair + 1) * up_rows : (2 * pair + 2) * up_rows]
        upkeep_ref[pair] = jnp.where(core == 0, first, second)
        upsend_ref[pair] = jnp.where(core == 0, second, first)
    grad_down = dot(hid_ref[...], scaled_ref[...], 0, 0).astype(BF)
    inside = tile // down_rows
    for at in range(inside):
        block = grad_down[at * down_rows : (at + 1) * down_rows]
        owner = j * inside + at

        @pl.when(owner % 2 == core)
        def _():
            downkeep_ref[owner // 2] = block

        @pl.when(owner % 2 != core)
        def _():
            downsend_ref[owner // 2] = block


def weight_grads_call(owners, rows, scaled, hidden, grad_pre):
    n, d = rows.shape
    f = hidden.shape[1]
    pieces = owners.shape[0]
    half = pieces // 2
    tile = max(d, f // pieces)
    one = pl.Buffered(buffer_count=1)
    up_shape = (half, d // pieces, f)
    down_shape = (half, f // pieces, d)
    flat = pl.BlockSpec((n, d), lambda j: (0, 0), pipeline_mode=one)
    tiled = pl.BlockSpec((n, tile), lambda j: (0, j))
    return pl.pallas_call(
        functools.partial(weight_grads_kernel, pieces),
        grid=(f // tile,),
        in_specs=[pl.BlockSpec(memory_space=pltpu.SMEM), flat, flat, tiled, tiled],
        out_specs=[pl.BlockSpec((half, d // pieces, tile), lambda j: (0, 0, j))] * 2
        + [pl.BlockSpec(down_shape, lambda j: (0, 0, 0), pipeline_mode=one)] * 2,
        out_shape=[whole((up_shape, BF))] * 2 + [whole((down_shape, BF))] * 2,
        compiler_params=pltpu.CompilerParams(vmem_limit_bytes=LIMIT),
        cost_estimate=cost(14),
        name="weight_grads",
    )(owners, rows, scaled, hidden, grad_pre)


def shards(
    block_input,
    cotangent,
    attn_in,
    attn_out,
    router,
    ln1_gain,
    ln1_bias,
    ln2_gain,
    ln2_bias,
    new_w1,
    new_w2,
    old_w1,
    old_w2,
    expert_ids,
    slots,
    drops,
):
    length, width = block_input.shape
    peers = lax.axis_size("expert")
    devices = lax.axis_size("dp") * peers
    experts = 2 * peers
    capacity = max(length * 7 // (2 * experts), 2)
    me = lax.axis_index("expert")
    ways, scatter_ways = orders()
    third = width // 3
    in_share = attn_in.shape[1]
    share = width // devices

    small = jnp.concatenate(
        [v[None] for v in (ln1_gain, ln1_bias, ln2_gain, ln2_bias)] + [router.T], axis=0
    )
    lines = small.shape[0]
    small = jnp.pad(small, ((0, -lines % 8), (0, third - share)))
    in_t, out_t = attn_in.T, attn_out.T
    states = []
    for p in range(3):
        cols = slice(p * third, (p + 1) * third)
        rows = [in_t[:, cols], out_t[:, cols]] + ([small] if p == 0 else [])
        states.append((jnp.concatenate(rows, axis=0), []))
    states = [gather_steps(states[p], ways[p][:2]) for p in range(3)]
    shards_dp = [old_w1[0], old_w2[0], new_w1[0], new_w2[0]]
    early = [state[0] for state in states]
    states = [gather_steps(states[p], ways[p][2:-1]) for p in range(3)]
    between = [state[0] for state in states]
    parts = [gather_finish(gather_steps(states[p], ways[p][-1:])) for p in range(3)]
    parts = [part.reshape(devices, -1, third) for part in parts]
    in_parts = [part[:, :in_share].reshape(3 * width, third) for part in parts]
    out_parts = [part[:, in_share : in_share + share].reshape(width, third) for part in parts]
    small_full = parts[0][:, in_share + share : in_share + share + lines, :share]
    small_full = small_full.transpose(1, 0, 2).reshape(lines, width)
    vectors = jnp.pad(small_full[:4].astype(F32), ((0, 4), (0, 0)))
    router_pad = jnp.pad(small_full[4:], ((0, 128 - experts), (0, 0)))

    target = jnp.where(drops == 0, expert_ids * capacity + slots, -1)
    by_member = ((expert_ids % 2) * peers + expert_ids // 2) * capacity + slots
    by_member = jnp.where(drops == 0, by_member, -1)
    target_rows = jnp.pad(target.T, ((0, 6), (0, 0)), constant_values=-1)
    member_rows = jnp.pad(by_member.T, ((0, 6), (0, 0)), constant_values=-1)
    count = peers * capacity
    both_shape = (peers, 2, capacity, width)

    def move(block):
        return lax.all_to_all(block, "expert", split_axis=0, concat_axis=0, tiled=True)

    def send(block, *earlier):
        block = after(block, *earlier).reshape(peers, capacity, width)
        return move(block).reshape(count, width)

    (grad_slots,) = plain_call(
        place_kernel, [((2 * count, width), BF)], [], "place_grads", 4, target_rows, after(cotangent, early)
    )
    grads = move(after(grad_slots, between).reshape(both_shape))
    slot_outs = [((count, width), BF)] * 2

    normed, proj, context, middle, rold, rnew = plain_call(
        forward_kernel,
        [
            ((length, width), BF),
            ((length, 3 * width), BF),
            ((length, width), BF),
            ((length, width), F32),
        ]
        + slot_outs,
        [],
        "attention_forward", 27,
        block_input,
        *in_parts,
        *out_parts,
        vectors,
        member_rows,
    )
    owners = lax.axis_index("dp") ^ jnp.arange(lax.axis_size("dp"), dtype=jnp.int32)
    far = [dp_far(after(shard, between)) for shard in shards_dp[:2]]
    far.append(dp_far(after(shards_dp[2], between, far)))
    far.append(dp_far(after(shards_dp[3], between, far)))
    near = [{away: core_swap(piece) for away, piece in f.items()} for f in far[:3]]
    own = [core_swap(after(shard, normed)) for shard in shards_dp]
    rold = send(rold, grads, far[:2], own)
    rnew = send(rnew, rold, near)

    lane = lax.broadcasted_iota(jnp.int32, (8, 128), 1)
    line = lax.broadcasted_iota(jnp.int32, (8, 128), 0)

    def chosen(expert):
        return jnp.where(line == 0, (lane == expert).astype(F32), F32(experts))

    pieces = [dp_pieces(shards_dp[i], own[i], far[i], near[i]) for i in range(2)]
    gated, old_in, old_router = expert_call(
        owners, chosen(2 * me), rold, grads, router_pad, *pieces
    )
    near.append({away: core_swap(after(piece, old_in)) for away, piece in far[3].items()})
    pieces = [dp_pieces(shards_dp[i], own[i], far[i], near[i]) for i in range(2, 4)]
    rnew, old_in = lax.optimization_barrier((rnew, old_in))
    old_in = send(old_in, rnew)
    gated, new_in, new_router, hidden, grad_pre, scaled = expert_call(
        owners, chosen(2 * me + 1), rnew, grads, router_pad, *pieces, gated
    )
    up_keep, up_send, down_keep, down_send = weight_grads_call(
        owners, rnew, scaled, hidden, grad_pre
    )
    new_in = send(new_in, old_in)
    ups = [up_keep, core_swap(after(up_send, old_in))]
    downs = [down_keep, core_swap(after(down_send, old_in))]
    gated = move(after(gated, new_in, ups, downs)).reshape(2 * count, width)
    router_part = (old_router + new_router)[:experts]

    gmid, gctx, out_grad, sums_two = plain_call(
        branch_kernel,
        [
            ((length, width), F32),
            ((length, width), BF),
            ((width, width), BF),
            ((8, width), F32),
        ],
        [],
        "branch_backward",
        0,
        old_in,
        new_in,
        by_member,
        cotangent,
        middle,
        context,
        *out_parts,
        vectors,
    )
    accumulators = [pltpu.VMEM((length, 2 * HEAD_DIM), F32)] * 2
    ups_first, downs_first = [scatter_dp_first(after(sums, gctx)) for sums in (ups, downs)]
    ups_x = scatter_dp(ups, ups_first)
    downs_x = scatter_dp(downs, downs_first)
    half = lax.axis_size("dp") // 2
    gproj, *split = plain_call(
        attention_back_kernel,
        [((length, 3 * width), BF)] + [((half, 3 * width // (2 * half), third), BF)] * 6,
        accumulators,
        "attention_backward",
        0,
        owners,
        proj,
        after(gctx, ups_first, downs_first),
        normed,
    )
    input_grad, sums_one = plain_call(
        input_kernel,
        [((length, width), F32), ((8, width), F32)],
        [],
        "input_backward", 0,
        gproj,
        *in_parts,
        block_input,
        vectors,
        gmid,
    )
    lead = canonical()
    core = [("dp", powers(lax.axis_size("dp"))[0])]
    states = []
    left = [step for step in lead if step != core[0]]
    for keep, away in zip(split[:3], split[3:]):
        addends = [keep, swap(away, *core[0])]
        states.append([a.reshape([2] * len(left) + [in_share, third]) for a in addends])
    small_grads = jnp.concatenate([sums_one[:2], sums_two[:2], router_part], axis=0)
    small_grads = small_grads.reshape(lines, devices, share).transpose(1, 0, 2)
    small_grads = small_grads.reshape(devices, 1, lines * share).astype(BF)
    small_rows = -(-lines * share // width)
    small_rows += -(share + small_rows) % 8
    small_grads = jnp.pad(small_grads, ((0, 0), (0, 0), (0, small_rows * width - lines * share)))
    rest = jnp.concatenate(
        [out_grad.reshape(devices, share, width), small_grads.reshape(devices, small_rows, width)],
        axis=1,
    )
    rest = rest.reshape([2] * len(lead) + list(rest.shape[1:]))
    got = scatter_step([rest], lead, core[0])
    states.append(scatter_rest([rest], lead, core[0], got)[0])
    states = after(states, gated, ups_x, downs_x)
    lefts = [left] * len(states)
    for at in range(len(left)):
        arrived = [
            scatter_step(state, left, way[at])
            for state, left, way in zip(states, lefts, scatter_ways)
        ]
        if at == 0:
            (mixed,) = plain_call(
                mixed_kernel,
                [((length, width), BF)],
                [],
                "mixed_output", 5,
                after(gated, arrived),
                target,
                middle,
            )
        if at == 1:
            (ups, downs, ups_x, downs_x), _ = lax.optimization_barrier(
                ((ups, downs, ups_x, downs_x), arrived)
            )
            new_w1_grad = scatter_dp_total(ups, ups_x)[None]
            new_w2_grad = scatter_dp_total(downs, downs_x)[None]
        pairs = [
            scatter_rest(state, left, way[at], got)
            for state, left, way, got in zip(states, lefts, scatter_ways, arrived)
        ]
        states = [pair[0] for pair in pairs]
        lefts = [pair[1] for pair in pairs]
    sums = [total(state) for state in states]
    attn_in_grad = jnp.concatenate(sums[:3], axis=1).T
    attn_out_grad = sums[3][:share].T
    small_grads = sums[3][share:].reshape(-1)[: lines * share].reshape(lines, share)
    vector_grads = small_grads[:4]
    router_grad = small_grads[4:].T
    return (
        mixed,
        input_grad,
        attn_in_grad,
        attn_out_grad,
        router_grad,
        vector_grads[0],
        vector_grads[1],
        vector_grads[2],
        vector_grads[3],
        new_w1_grad,
        new_w2_grad,
    )


def solution(mesh):
    both = ("dp", "expert")
    rows = P(both, None)
    columns = P(None, both)
    vector = P(both)
    weight = P("expert", "dp", None)
    in_specs = (
        [rows, rows, columns, columns, rows] + [vector] * 4 + [weight] * 4 + [rows] * 3
    )
    out_specs = [rows, rows, columns, columns, rows] + [vector] * 4 + [weight] * 2
    return jax.shard_map(
        shards, mesh=mesh, in_specs=tuple(in_specs), out_specs=tuple(out_specs), check_vma=False
    )
```

```python
import functools

import jax
import jax.numpy as jnp
from jax import lax
from jax.experimental import pallas as pl
from jax.experimental.pallas import tpu as pltpu
from jax.sharding import PartitionSpec as P

HEADS = 12
HEAD_DIM = 64
BF = jnp.bfloat16
F32 = jnp.float32


def mm(a, b, dims, out=F32):
    return lax.dot_general(a, b, (dims, ((), ())), preferred_element_type=F32).astype(out)


def powers(count):
    found = []
    bit = 1
    while bit < count:
        found.append(bit)
        bit *= 2
    return found


def swap(values, axis, bit):
    count = lax.axis_size(axis)
    return lax.ppermute(values, axis, [(i, i ^ bit) for i in range(count)])


def my_bit(axis, bit):
    return (lax.axis_index(axis) // bit) % 2


def canonical():
    return [("dp", b) for b in reversed(powers(lax.axis_size("dp")))] + [
        ("expert", b) for b in reversed(powers(lax.axis_size("expert")))
    ]


def orders():
    dp_bits = powers(lax.axis_size("dp"))
    expert_bits = powers(lax.axis_size("expert"))
    core = [("dp", dp_bits[0])]
    xs = [("dp", b) for b in reversed(dp_bits[1:])]
    ys = [("expert", expert_bits[0])]
    zs = [("expert", b) for b in reversed(expert_bits[1:])]
    gathering = (zs + ys + xs + core, xs + zs + ys + core, ys + xs + zs + core)
    near = zs[::-1]
    summing = (xs + ys + near, ys + near + xs, near + xs + ys, xs + ys + near)
    return gathering, summing


def gather_steps(state, order):
    current, lead = state
    lead = list(lead)
    for axis, bit in order:
        other = swap(current, axis, bit)
        low = my_bit(axis, bit) == 0
        current = jnp.stack([jnp.where(low, current, other), jnp.where(low, other, current)])
        lead.insert(0, (axis, bit))
    return current, lead


def gather_finish(state):
    current, lead = state
    tail = current.shape[len(lead) :]
    perm = [lead.index(w) for w in canonical()]
    current = current.transpose(perm + list(range(len(lead), current.ndim)))
    return current.reshape((-1,) + tail)


def after(values, *earlier):
    if not earlier:
        return values
    return lax.optimization_barrier((values, earlier))[0]


def total(addends):
    found = addends[0].astype(F32)
    for addend in addends[1:]:
        found = found + addend.astype(F32)
    return found


def away_part(addends, lead, step):
    at = lead.index(step)
    mine = my_bit(*step)
    send = total([lax.dynamic_index_in_dim(a, 1 - mine, at, keepdims=False) for a in addends])
    return send.astype(BF)


def scatter_step(addends, lead, step):
    return swap(away_part(addends, lead, step), *step)


def scatter_rest(addends, lead, step, got):
    at = lead.index(step)
    addends = [lax.dynamic_index_in_dim(a, my_bit(*step), at, keepdims=False) for a in addends]
    return addends + [got], lead[:at] + lead[at + 1 :]


def core_swap(piece):
    return swap(piece, "dp", powers(lax.axis_size("dp"))[0])


def dp_far(shard):
    far = {}
    for bit in powers(lax.axis_size("dp"))[1:]:
        for away, piece in [(0, shard), *far.items()]:
            far[away ^ bit] = swap(piece, "dp", bit)
    return far


def dp_pieces(shard, own, far, near):
    core = powers(lax.axis_size("dp"))[0]
    found = {0: shard, core: own, **far}
    found.update({away ^ core: piece for away, piece in near.items()})
    return [found[away] for away in range(len(found))]


def x_steps():
    return [("dp", b) for b in powers(lax.axis_size("dp"))[1:]]


def scatter_dp(own, first):
    order = x_steps()
    lead = order[::-1]
    addends = [own.reshape([2] * (len(order) - 1) + list(own.shape[1:]))]
    first = first.reshape(addends[0].shape)
    addends.append(swap(first, *order[0]))
    lead.remove(order[0])
    for step in order[1:]:
        got = scatter_step(addends, lead, step)
        addends, lead = scatter_rest(addends, lead, step, got)
    return total(addends)


LIMIT = 56 * 1024 * 1024
QUERY_BLOCK = 512
SCALE = HEAD_DIM ** (-0.5)


def dot(a, b, over_a, over_b):
    return lax.dot_general(
        a, b, (((over_a,), (over_b,)), ((), ())), preferred_element_type=F32
    )


def dot_parts(values, parts):
    width = parts[0].shape[1]
    total = None
    for at, part in enumerate(parts):
        term = dot(values[:, at * width : (at + 1) * width], part, 1, 1)
        total = term if total is None else total + term
    return total


def whole(array):
    return jax.ShapeDtypeStruct(array[0], array[1])


def cost(micros):
    return pl.CostEstimate(flops=int(micros * 0.25e9), bytes_accessed=0, transcendentals=0)


def plain_call(body, outs, scratch, name, micros, *args):
    space = pl.BlockSpec(memory_space=pltpu.VMEM)
    return pl.pallas_call(
        body,
        out_shape=[whole(o) for o in outs],
        in_specs=[space] * len(args),
        out_specs=[space] * len(outs),
        scratch_shapes=scratch,
        compiler_params=pltpu.CompilerParams(vmem_limit_bytes=LIMIT),
        cost_estimate=cost(micros),
        name=name,
    )(*args)


def norm_parts(values):
    centre = values - jnp.mean(values, axis=-1, keepdims=True)
    spread = jnp.mean(centre * centre, axis=-1, keepdims=True)
    scale = lax.rsqrt(spread + 1e-05)
    return centre * scale, scale


def norm_back(values, gain, grad):
    normal, scale = norm_parts(values)
    scaled = grad * gain
    back = scale * (
        scaled
        - jnp.mean(scaled, axis=-1, keepdims=True)
        - normal * jnp.mean(scaled * normal, axis=-1, keepdims=True)
    )
    return back, jnp.sum(grad * normal, axis=0, keepdims=True), jnp.sum(grad, axis=0, keepdims=True)


def place_rows(target_ref, values, first, count):
    tokens = values.shape[0]
    at = lax.broadcasted_iota(jnp.int32, (count, tokens), 0) + first
    hit = (at == target_ref[0:1, :]) | (at == target_ref[1:2, :])
    return dot(hit.astype(F32).astype(BF), values, 1, 0).astype(BF)


def place_kernel(target_ref, values_ref, slots_ref):
    values = values_ref[...]
    part = slots_ref.shape[0] // 4
    for at in range(4):
        slots_ref[at * part : (at + 1) * part, :] = place_rows(
            target_ref, values, at * part, part
        )


def take_rows(target_ref, slots_refs, tokens):
    total = None
    first = 0
    for ref in slots_refs:
        count = ref.shape[0]
        at = lax.broadcasted_iota(jnp.int32, (tokens, count), 1) + first
        hit = (at == target_ref[:, 0:1]) | (at == target_ref[:, 1:2])
        part = dot(hit.astype(F32).astype(BF), ref[...], 1, 0)
        total = part if total is None else total + part
        first += count
    return total


def causal(size):
    rowpos = lax.broadcasted_iota(jnp.int32, (size, size), 0)
    colpos = lax.broadcasted_iota(jnp.int32, (size, size), 1)
    return rowpos >= colpos


def head_lanes(block, which):
    lane = lax.broadcasted_iota(jnp.int32, block.shape, 1)
    keep = (lane < HEAD_DIM) if which == 0 else (lane >= HEAD_DIM)
    return jnp.where(keep, block, jnp.zeros_like(block))


def block_softmax(query, keys, seen):
    size = query.shape[0]
    before = keys.shape[0] - size
    own = dot(query, keys[before:], 1, 1)
    own = jnp.where(seen, own, -1e30)
    top = jnp.max(own, axis=-1, keepdims=True)
    if before:
        past = dot(query, keys[:before], 1, 1)
        top = jnp.maximum(top, jnp.max(past, axis=-1, keepdims=True))
        past = jnp.exp(past - top)
    own = jnp.exp(own - top)
    total = jnp.sum(own, axis=-1, keepdims=True)
    if before:
        total = total + jnp.sum(past, axis=-1, keepdims=True)
    inverse = 1.0 / total
    own = own * inverse
    return (past * inverse, own) if before else (own,)


def pair_columns(pair, part, width):
    return pl.ds(pl.multiple_of(part * width + pair * 2 * HEAD_DIM, 2 * HEAD_DIM), 2 * HEAD_DIM)


def forward_kernel(
    x_ref,
    in0_ref,
    in1_ref,
    in2_ref,
    out0_ref,
    out1_ref,
    out2_ref,
    vec_ref,
    target_ref,
    normed_ref,
    proj_ref,
    context_ref,
    middle_ref,
    old_ref,
    new_ref,
):
    length, width = x_ref.shape
    x = x_ref[...].astype(F32)
    normal, _ = norm_parts(x)
    normed = (normal * vec_ref[0:1, :] + vec_ref[1:2, :]).astype(BF)
    normed_ref[...] = normed
    for part in range(3):
        cols = slice(part * width, (part + 1) * width)
        proj_ref[:, cols] = dot_parts(
            normed, [ref[cols, :] for ref in (in0_ref, in1_ref, in2_ref)]
        ).astype(BF)
    size = min(QUERY_BLOCK, length)
    seen = causal(size)

    def one_pair(pair, carry):
        q_at, k_at, v_at = (pair_columns(pair, part, width) for part in range(3))
        for block in range(length // size):
            rows = slice(block * size, (block + 1) * size)
            upto = (block + 1) * size
            query = proj_ref[rows, q_at] * BF(SCALE)
            keys = proj_ref[0:upto, k_at]
            values = proj_ref[0:upto, v_at]
            outs = []
            for which in range(2):
                probs = block_softmax(head_lanes(query, which), keys, seen)
                probs = [p.astype(BF) for p in probs]
                out = dot(probs[-1], values[upto - size :], 1, 0)
                if len(probs) > 1:
                    out = out + dot(probs[0], values[: upto - size], 1, 0)
                outs.append(out)
            lane = lax.broadcasted_iota(jnp.int32, outs[0].shape, 1)
            context_ref[rows, pair_columns(pair, 0, width)] = jnp.where(
                lane < HEAD_DIM, outs[0], outs[1]
            ).astype(BF)
        return carry

    lax.fori_loop(0, HEADS // 2, one_pair, 0)
    middle = x + dot_parts(context_ref[...], [ref[...] for ref in (out0_ref, out1_ref, out2_ref)])
    middle_ref[...] = middle
    normal, _ = norm_parts(middle)
    normed_two = (normal * vec_ref[2:3, :] + vec_ref[3:4, :]).astype(BF)
    count = old_ref.shape[0]
    half = count // 2
    for at, ref in ((0, old_ref), (count, new_ref)):
        for part in range(2):
            ref[part * half : (part + 1) * half, :] = place_rows(
                target_ref, normed_two, at + part * half, half
            )


def branch_kernel(
    old_ref,
    new_ref,
    target_ref,
    cot_ref,
    middle_ref,
    context_ref,
    out0_ref,
    out1_ref,
    out2_ref,
    vec_ref,
    gmid_ref,
    gctx_ref,
    outgrad_ref,
    sums_ref,
):
    length, width = cot_ref.shape
    grad = take_rows(target_ref, (old_ref, new_ref), length)
    back, gain_sum, bias_sum = norm_back(middle_ref[...], vec_ref[2:3, :], grad)
    gmid = back + cot_ref[...].astype(F32)
    gmid_ref[...] = gmid
    sums_ref[...] = jnp.concatenate([gain_sum, bias_sum, jnp.zeros((6, width), F32)], axis=0)
    branch = gmid.astype(BF)
    third = width // 3
    for part, ref in enumerate((out0_ref, out1_ref, out2_ref)):
        gctx_ref[:, part * third : (part + 1) * third] = dot(branch, ref[...], 1, 0).astype(BF)
    outgrad_ref[...] = dot(branch, context_ref[...], 0, 0).astype(BF)


def pairs_back(proj_ref, gctx_ref, gproj_ref, gk_acc, gv_acc):
    length, width = gctx_ref.shape
    size = min(QUERY_BLOCK, length)
    seen = causal(size)

    def one_pair(pair, carry):
        q_at, k_at, v_at = (pair_columns(pair, part, width) for part in range(3))
        gk_acc[...] = jnp.zeros_like(gk_acc)
        gv_acc[...] = jnp.zeros_like(gv_acc)
        for block in range(length // size):
            rows = slice(block * size, (block + 1) * size)
            upto = (block + 1) * size
            query = proj_ref[rows, q_at] * BF(SCALE)
            keys = proj_ref[0:upto, k_at]
            values = proj_ref[0:upto, v_at]
            gout = gctx_ref[rows, pair_columns(pair, 0, width)]
            grads = []
            for which in range(2):
                mine = head_lanes(query, which)
                gmine = head_lanes(gout, which)
                probs = block_softmax(mine, keys, seen)
                spans = [slice(upto - size, upto)]
                if len(probs) > 1:
                    spans = [slice(0, upto - size)] + spans
                gprobs = [dot(gmine, values[s], 1, 1) for s in spans]
                row = sum(jnp.sum(p * g, axis=-1, keepdims=True) for p, g in zip(probs, gprobs))
                gquery = None
                for p, g, s in zip(probs, gprobs, spans):
                    gscore = (p * (g - row)).astype(BF)
                    part = dot(gscore, keys[s], 1, 0)
                    gquery = part if gquery is None else gquery + part
                    gk_acc[s, :] += dot(gscore, mine, 0, 0)
                    gv_acc[s, :] += dot(p.astype(BF), gmine, 0, 0)
                grads.append(gquery * SCALE)
            lane = lax.broadcasted_iota(jnp.int32, grads[0].shape, 1)
            gproj_ref[rows, q_at] = jnp.where(lane < HEAD_DIM, grads[0], grads[1]).astype(BF)
        gproj_ref[:, k_at] = gk_acc[...].astype(BF)
        gproj_ref[:, v_at] = gv_acc[...].astype(BF)
        return carry

    lax.fori_loop(0, HEADS // 2, one_pair, 0)

def attention_back_kernel(
    place_ref,
    proj_ref,
    gctx_ref,
    normed_ref,
    gproj_ref,
    keep0_ref,
    keep1_ref,
    keep2_ref,
    send0_ref,
    send1_ref,
    send2_ref,
    gk_acc,
    gv_acc,
):
    width = gctx_ref.shape[1]
    pairs_back(proj_ref, gctx_ref, gproj_ref, gk_acc, gv_acc)
    third = width // 3
    core = place_ref[0] % 2
    halves, rows, _ = keep0_ref.shape
    refs = ((keep0_ref, send0_ref), (keep1_ref, send1_ref), (keep2_ref, send2_ref))
    for part, (keep_ref, send_ref) in enumerate(refs):
        grad = dot(gproj_ref[...], normed_ref[:, part * third : (part + 1) * third], 0, 0)
        grad = grad.astype(BF)
        for at in range(halves):
            first = grad[2 * at * rows : (2 * at + 1) * rows]
            second = grad[(2 * at + 1) * rows : (2 * at + 2) * rows]
            keep_ref[at] = jnp.where(core == 0, first, second)
            send_ref[at] = jnp.where(core == 0, second, first)


def input_kernel(
    gproj_ref, in0_ref, in1_ref, in2_ref, x_ref, vec_ref, gmid_ref, grad_ref, sums_ref
):
    grad = jnp.concatenate(
        [dot(gproj_ref[...], ref[...], 1, 0) for ref in (in0_ref, in1_ref, in2_ref)], axis=1
    )
    back, gain_sum, bias_sum = norm_back(x_ref[...].astype(F32), vec_ref[0:1, :], grad)
    grad_ref[...] = gmid_ref[...] + back
    width = x_ref.shape[1]
    sums_ref[...] = jnp.concatenate([gain_sum, bias_sum, jnp.zeros((6, width), F32)], axis=0)


def mixed_kernel(slots_ref, target_ref, middle_ref, mixed_ref):
    total = take_rows(target_ref, (slots_ref,), middle_ref.shape[0])
    mixed_ref[...] = (middle_ref[...] + total).astype(BF)


def gelu_pair(x):
    c = 0.7978845608028654
    sq = x * x
    t = jnp.tanh(c * x * (1.0 + 0.044715 * sq))
    half = 0.5 * (1.0 + t)
    slope = half + 0.5 * x * (1.0 - t * t) * (c * (1.0 + 3 * 0.044715 * sq))
    return x * half, slope

def expert_kernel(train, steps, pieces, place_ref, mine_ref, rows_ref, grads4_ref, router_ref, *rest):
    ups, downs, rest = rest[:pieces], rest[pieces : 2 * pieces], rest[2 * pieces :]
    if train:
        _, gated_ref, gin_ref, rgrad_ref, hid_ref, gpre_ref, scaled_ref = rest[:7]
        rest = rest[7:]
    else:
        gated_ref, gin_ref, rgrad_ref = rest[:3]
        rest = rest[3:]
    up_s, down_s, out_acc, gin_acc, scaled, gate_s, probs_s, sems = rest
    j = pl.program_id(0)
    mine = mine_ref[0:1, :]
    up_rows = up_s.shape[0] // pieces
    down_rows = down_s.shape[0] // pieces
    tile = up_s.shape[1] // steps

    def grads():
        return grads4_ref[...].reshape(rows_ref.shape).astype(F32)

    def fetches():
        found = []
        for at in range(pieces):
            owner = place_ref[at]
            to = pl.ds(pl.multiple_of(owner * up_rows, up_rows), up_rows)
            found.append(pltpu.make_async_copy(ups[at], up_s.at[to], sems.at[0, at]))
            to = pl.ds(pl.multiple_of(owner * down_rows, down_rows), down_rows)
            found.append(pltpu.make_async_copy(downs[at], down_s.at[to], sems.at[1, at]))
        return found

    @pl.when(j == 0)
    def _():
        for fetch in fetches():
            fetch.start()
        logits = dot(rows_ref[...], router_ref[...], 1, 1)
        live = lax.broadcasted_iota(jnp.int32, logits.shape, 1) < mine_ref[1, 0].astype(jnp.int32)
        logits = jnp.where(live, logits, -1e30)
        e = jnp.exp(logits - jnp.max(logits, axis=1, keepdims=True))
        probs = e / jnp.sum(e, axis=1, keepdims=True)
        probs_s[...] = probs
        gate = jnp.sum(probs * mine, axis=1, keepdims=True)
        gate_s[...] = jnp.broadcast_to(gate, gate_s.shape)
        scaled[...] = (grads() * gate).astype(BF)
        out_acc[...] = jnp.zeros_like(out_acc)
        gin_acc[...] = jnp.zeros_like(gin_acc)
        for fetch in fetches():
            fetch.wait()

    rows = rows_ref[...]
    here = pl.ds(pl.multiple_of(j * tile, tile), tile)
    up = up_s[:, here]
    down = down_s[here, :]
    hid, slope = gelu_pair(dot(rows, up, 1, 0))
    hid = hid.astype(BF)
    gpre = (dot(scaled[...], down, 1, 1) * slope).astype(BF)
    out_acc[...] += dot(hid, down, 1, 0)
    gin_acc[...] += dot(gpre, up, 1, 1)

    if train:
        hid_ref[...] = hid
        gpre_ref[...] = gpre

        @pl.when(j == 0)
        def _():
            scaled_ref[...] = scaled[...]

    @pl.when(j == steps - 1)
    def _():
        produced = out_acc[...].astype(BF).astype(F32)
        gate = gate_s[:, 0:1]
        gated_ref[...] = (produced * gate).astype(BF).reshape(gated_ref.shape)
        grad_gate = jnp.sum(produced * grads(), axis=1, keepdims=True)
        gl = (grad_gate * gate * (mine - probs_s[...])).astype(BF)
        gin_ref[...] = (gin_acc[...] + dot(gl, router_ref[...], 1, 0)).astype(BF)
        rgrad_ref[...] = dot(gl, rows_ref[...], 0, 0)


def expert_call(owners, mine, rows, grads, router_pad, ups, downs, gated=None):
    train = gated is not None
    n, d = rows.shape
    pieces = len(ups)
    f = ups[0].shape[1]
    tile = max(d, f // pieces)
    steps = f // tile
    peers, _, capacity, _ = grads.shape
    member = 1 if train else 0
    one = pl.Buffered(buffer_count=1)

    def all_of(shape):
        return pl.BlockSpec(shape, lambda j: (0,) * len(shape), pipeline_mode=one)

    slot_spec = pl.BlockSpec(
        (peers, 1, capacity, d), lambda j: (0, member, 0, 0), pipeline_mode=one
    )
    anywhere = pl.BlockSpec(memory_space=pl.ANY)
    outs = [(grads.shape, BF), ((n, d), BF), ((128, d), F32)]
    out_specs = [slot_spec, all_of((n, d)), all_of((128, d))]
    if train:
        outs += [((n, f), BF)] * 2 + [((n, d), BF)]
        out_specs += [pl.BlockSpec((n, tile), lambda j: (0, j))] * 2 + [all_of((n, d))]
    args = [owners, mine, rows, grads, router_pad, *ups, *downs] + ([gated] if train else [])
    return pl.pallas_call(
        functools.partial(expert_kernel, train, steps, pieces),
        grid=(steps,),
        in_specs=[
            pl.BlockSpec(memory_space=pltpu.SMEM),
            all_of((8, 128)),
            all_of((n, d)),
            slot_spec,
            all_of((128, d)),
        ]
        + [anywhere] * (2 * pieces + train),
        out_specs=out_specs,
        out_shape=[whole(o) for o in outs],
        scratch_shapes=[
            pltpu.VMEM((d, f), BF),
            pltpu.VMEM((f, d), BF),
            pltpu.VMEM((n, d), F32),
            pltpu.VMEM((n, d), F32),
            pltpu.VMEM((n, d), BF),
            pltpu.VMEM((n, 128), F32),
            pltpu.VMEM((n, 128), F32),
            pltpu.SemaphoreType.DMA((2, pieces)),
        ],
        input_output_aliases={len(args) - 1: 0} if train else {},
        compiler_params=pltpu.CompilerParams(vmem_limit_bytes=LIMIT),
        cost_estimate=cost(29),
        name="expert_new" if train else "expert_old",
    )(*args)


def weight_grads_kernel(
    pieces,
    place_ref,
    rows_ref,
    scaled_ref,
    hid_ref,
    gpre_ref,
    upkeep_ref,
    upsend_ref,
    downkeep_ref,
    downsend_ref,
):
    j = pl.program_id(0)
    core = place_ref[0] % 2
    half, up_rows, tile = upkeep_ref.shape
    down_rows = downkeep_ref.shape[1]
    grad_up = dot(rows_ref[...], gpre_ref[...], 0, 0).astype(BF)
    for pair in range(half):
        first = grad_up[2 * pair * up_rows : (2 * pair + 1) * up_rows]
        second = grad_up[(2 * pair + 1) * up_rows : (2 * pair + 2) * up_rows]
        upkeep_ref[pair] = jnp.where(core == 0, first, second)
        upsend_ref[pair] = jnp.where(core == 0, second, first)
    grad_down = dot(hid_ref[...], scaled_ref[...], 0, 0).astype(BF)
    inside = tile // down_rows
    for at in range(inside):
        block = grad_down[at * down_rows : (at + 1) * down_rows]
        owner = j * inside + at

        @pl.when(owner % 2 == core)
        def _():
            downkeep_ref[owner // 2] = block

        @pl.when(owner % 2 != core)
        def _():
            downsend_ref[owner // 2] = block


def weight_grads_call(owners, rows, scaled, hidden, grad_pre):
    n, d = rows.shape
    f = hidden.shape[1]
    pieces = owners.shape[0]
    half = pieces // 2
    tile = max(d, f // pieces)
    one = pl.Buffered(buffer_count=1)
    up_shape = (half, d // pieces, f)
    down_shape = (half, f // pieces, d)
    flat = pl.BlockSpec((n, d), lambda j: (0, 0), pipeline_mode=one)
    tiled = pl.BlockSpec((n, tile), lambda j: (0, j))
    return pl.pallas_call(
        functools.partial(weight_grads_kernel, pieces),
        grid=(f // tile,),
        in_specs=[pl.BlockSpec(memory_space=pltpu.SMEM), flat, flat, tiled, tiled],
        out_specs=[pl.BlockSpec((half, d // pieces, tile), lambda j: (0, 0, j))] * 2
        + [pl.BlockSpec(down_shape, lambda j: (0, 0, 0), pipeline_mode=one)] * 2,
        out_shape=[whole((up_shape, BF))] * 2 + [whole((down_shape, BF))] * 2,
        compiler_params=pltpu.CompilerParams(vmem_limit_bytes=LIMIT),
        cost_estimate=cost(1),
        name="weight_grads",
    )(owners, rows, scaled, hidden, grad_pre)


def x_parts_kernel(place_ref, keep_ref, got_ref, own_ref, away_ref):
    mine = (place_ref[0] // 2) % 2
    for at in range(own_ref.shape[0]):
        first = keep_ref[2 * at].astype(F32) + got_ref[2 * at].astype(F32)
        second = keep_ref[2 * at + 1].astype(F32) + got_ref[2 * at + 1].astype(F32)
        own_ref[at] = jnp.where(mine == 0, first, second)
        away_ref[at] = jnp.where(mine == 0, second, first).astype(BF)


def x_parts_call(owners, keep, got):
    half, rows, width = keep.shape
    tile = min(width, 768)
    grid = width // tile

    def block(count):
        return pl.BlockSpec((count, rows, tile), lambda j: (0, 0, j))

    own = (half // 2, rows, width)
    return pl.pallas_call(
        x_parts_kernel,
        grid=(grid,),
        in_specs=[pl.BlockSpec(memory_space=pltpu.SMEM), block(half), block(half)],
        out_specs=[block(half // 2)] * 2,
        out_shape=[whole((own, F32)), whole((own, BF))],
        compiler_params=pltpu.CompilerParams(vmem_limit_bytes=LIMIT),
        cost_estimate=cost(0),
        name="x_parts",
    )(owners, keep, got)


def shards(
    block_input,
    cotangent,
    attn_in,
    attn_out,
    router,
    ln1_gain,
    ln1_bias,
    ln2_gain,
    ln2_bias,
    new_w1,
    new_w2,
    old_w1,
    old_w2,
    expert_ids,
    slots,
    drops,
):
    length, width = block_input.shape
    peers = lax.axis_size("expert")
    devices = lax.axis_size("dp") * peers
    experts = 2 * peers
    capacity = max(length * 7 // (2 * experts), 2)
    me = lax.axis_index("expert")
    ways, scatter_ways = orders()
    third = width // 3
    in_share = attn_in.shape[1]
    share = width // devices

    small = jnp.concatenate(
        [v[None] for v in (ln1_gain, ln1_bias, ln2_gain, ln2_bias)] + [router.T], axis=0
    )
    lines = small.shape[0]
    small = jnp.pad(small, ((0, -lines % 8), (0, third - share)))
    in_t, out_t = attn_in.T, attn_out.T
    states = []
    for p in range(3):
        cols = slice(p * third, (p + 1) * third)
        rows = [in_t[:, cols], out_t[:, cols]] + ([small] if p == 0 else [])
        states.append((jnp.concatenate(rows, axis=0), []))
    states = [gather_steps(states[p], ways[p][:2]) for p in range(3)]
    shards_dp = [old_w1[0], old_w2[0], new_w1[0], new_w2[0]]
    early = [state[0] for state in states]
    states = [gather_steps(states[p], ways[p][2:-1]) for p in range(3)]
    between = [state[0] for state in states]
    parts = [gather_finish(gather_steps(states[p], ways[p][-1:])) for p in range(3)]
    parts = [part.reshape(devices, -1, third) for part in parts]
    in_parts = [part[:, :in_share].reshape(3 * width, third) for part in parts]
    out_parts = [part[:, in_share : in_share + share].reshape(width, third) for part in parts]
    small_full = parts[0][:, in_share + share : in_share + share + lines, :share]
    small_full = small_full.transpose(1, 0, 2).reshape(lines, width)
    vectors = jnp.pad(small_full[:4].astype(F32), ((0, 4), (0, 0)))
    router_pad = jnp.pad(small_full[4:], ((0, 128 - experts), (0, 0)))

    target = jnp.where(drops == 0, expert_ids * capacity + slots, -1)
    by_member = ((expert_ids % 2) * peers + expert_ids // 2) * capacity + slots
    by_member = jnp.where(drops == 0, by_member, -1)
    target_rows = jnp.pad(target.T, ((0, 6), (0, 0)), constant_values=-1)
    member_rows = jnp.pad(by_member.T, ((0, 6), (0, 0)), constant_values=-1)
    count = peers * capacity
    both_shape = (peers, 2, capacity, width)

    def move(block):
        return lax.all_to_all(block, "expert", split_axis=0, concat_axis=0, tiled=True)

    def send(block, *earlier):
        block = after(block, *earlier).reshape(peers, capacity, width)
        return move(block).reshape(count, width)

    (grad_slots,) = plain_call(
        place_kernel, [((2 * count, width), BF)], [], "place_grads", 4, target_rows, after(cotangent, early)
    )
    grads = move(after(grad_slots, between).reshape(both_shape))
    slot_outs = [((count, width), BF)] * 2

    normed, proj, context, middle, rold, rnew = plain_call(
        forward_kernel,
        [
            ((length, width), BF),
            ((length, 3 * width), BF),
            ((length, width), BF),
            ((length, width), F32),
        ]
        + slot_outs,
        [],
        "attention_forward", 27,
        block_input,
        *in_parts,
        *out_parts,
        vectors,
        member_rows,
    )
    owners = lax.axis_index("dp") ^ jnp.arange(lax.axis_size("dp"), dtype=jnp.int32)
    far = [dp_far(after(shard, between)) for shard in shards_dp[:2]]
    far.append(dp_far(after(shards_dp[2], between, far)))
    far.append(dp_far(after(shards_dp[3], between, far)))
    near = [{away: core_swap(piece) for away, piece in f.items()} for f in far[:3]]
    own = [core_swap(after(shard, normed)) for shard in shards_dp]
    rold = send(rold, grads, far[:2], own)
    rnew = send(rnew, rold, near)

    lane = lax.broadcasted_iota(jnp.int32, (8, 128), 1)
    line = lax.broadcasted_iota(jnp.int32, (8, 128), 0)

    def chosen(expert):
        return jnp.where(line == 0, (lane == expert).astype(F32), F32(experts))

    pieces = [dp_pieces(shards_dp[i], own[i], far[i], near[i]) for i in range(2)]
    gated, old_in, old_router = expert_call(
        owners, chosen(2 * me), rold, grads, router_pad, *pieces
    )
    near.append({away: core_swap(after(piece, old_in)) for away, piece in far[3].items()})
    pieces = [dp_pieces(shards_dp[i], own[i], far[i], near[i]) for i in range(2, 4)]
    rnew, old_in = lax.optimization_barrier((rnew, old_in))
    old_in = send(old_in, rnew)
    gated, new_in, new_router, hidden, grad_pre, scaled = expert_call(
        owners, chosen(2 * me + 1), rnew, grads, router_pad, *pieces, gated
    )
    up_keep, up_send, down_keep, down_send = weight_grads_call(
        owners, rnew, scaled, hidden, grad_pre
    )
    new_in = send(new_in, old_in)
    up_own, up_away = x_parts_call(owners, up_keep, core_swap(after(up_send, old_in)))
    down_own, down_away = x_parts_call(owners, down_keep, core_swap(after(down_send, old_in)))
    gated = move(after(gated, new_in, up_away, down_away)).reshape(2 * count, width)
    new_w1_grad = scatter_dp(up_own, up_away)[None]
    new_w2_grad = scatter_dp(down_own, down_away)[None]
    router_part = (old_router + new_router)[:experts]

    gmid, gctx, out_grad, sums_two = plain_call(
        branch_kernel,
        [
            ((length, width), F32),
            ((length, width), BF),
            ((width, width), BF),
            ((8, width), F32),
        ],
        [],
        "branch_backward",
        0,
        old_in,
        new_in,
        by_member,
        cotangent,
        middle,
        context,
        *out_parts,
        vectors,
    )
    accumulators = [pltpu.VMEM((length, 2 * HEAD_DIM), F32)] * 2
    half = lax.axis_size("dp") // 2
    gproj, *split = plain_call(
        attention_back_kernel,
        [((length, 3 * width), BF)] + [((half, 3 * width // (2 * half), third), BF)] * 6,
        accumulators,
        "attention_backward",
        0,
        owners,
        proj,
        gctx,
        normed,
    )
    input_grad, sums_one = plain_call(
        input_kernel,
        [((length, width), F32), ((8, width), F32)],
        [],
        "input_backward", 0,
        gproj,
        *in_parts,
        block_input,
        vectors,
        gmid,
    )
    lead = canonical()
    core = [("dp", powers(lax.axis_size("dp"))[0])]
    states = []
    left = [step for step in lead if step != core[0]]
    for keep, away in zip(split[:3], split[3:]):
        addends = [keep, swap(away, *core[0])]
        states.append([a.reshape([2] * len(left) + [in_share, third]) for a in addends])
    small_grads = jnp.concatenate([sums_one[:2], sums_two[:2], router_part], axis=0)
    small_grads = small_grads.reshape(lines, devices, share).transpose(1, 0, 2)
    small_grads = small_grads.reshape(devices, 1, lines * share).astype(BF)
    small_rows = -(-lines * share // width)
    small_rows += -(share + small_rows) % 8
    small_grads = jnp.pad(small_grads, ((0, 0), (0, 0), (0, small_rows * width - lines * share)))
    rest = jnp.concatenate(
        [out_grad.reshape(devices, share, width), small_grads.reshape(devices, small_rows, width)],
        axis=1,
    )
    rest = rest.reshape([2] * len(lead) + list(rest.shape[1:]))
    got = scatter_step([rest], lead, core[0])
    states.append(scatter_rest([rest], lead, core[0], got)[0])
    lefts = [left] * len(states)

    def advance(chains, step_of):
        found = {
            p: scatter_step(states[p], lefts[p], scatter_ways[p][step_of(p)]) for p in chains
        }
        for p in chains:
            step = scatter_ways[p][step_of(p)]
            states[p], lefts[p] = scatter_rest(states[p], lefts[p], step, found[p])
        return list(found.values())

    ahead = ()
    states = after(states, gated, new_w1_grad, new_w2_grad)
    for at in range(len(left)):
        chains = [p for p in range(4) if at + (p in ahead) < len(left)]
        arrived = advance(chains, lambda p: at + (p in ahead))
        if at == 0:
            (mixed,) = plain_call(
                mixed_kernel,
                [((length, width), BF)],
                [],
                "mixed_output", 5,
                after(gated, arrived),
                target,
                middle,
            )
    sums = [total(state) for state in states]
    attn_in_grad = jnp.concatenate(sums[:3], axis=1).T
    attn_out_grad = sums[3][:share].T
    small_grads = sums[3][share:].reshape(-1)[: lines * share].reshape(lines, share)
    vector_grads = small_grads[:4]
    router_grad = small_grads[4:].T
    return (
        mixed,
        input_grad,
        attn_in_grad,
        attn_out_grad,
        router_grad,
        vector_grads[0],
        vector_grads[1],
        vector_grads[2],
        vector_grads[3],
        new_w1_grad,
        new_w2_grad,
    )


def solution(mesh):
    both = ("dp", "expert")
    rows = P(both, None)
    columns = P(None, both)
    vector = P(both)
    weight = P("expert", "dp", None)
    in_specs = (
        [rows, rows, columns, columns, rows] + [vector] * 4 + [weight] * 4 + [rows] * 3
    )
    out_specs = [rows, rows, columns, columns, rows] + [vector] * 4 + [weight] * 2
    return jax.shard_map(
        shards, mesh=mesh, in_specs=tuple(in_specs), out_specs=tuple(out_specs), check_vma=False
    )
```

```python
import functools

import jax
import jax.numpy as jnp
from jax import lax
from jax.experimental import pallas as pl
from jax.experimental.pallas import tpu as pltpu
from jax.sharding import PartitionSpec as P

HEADS = 12
HEAD_DIM = 64
BF = jnp.bfloat16
F32 = jnp.float32


def mm(a, b, dims, out=F32):
    return lax.dot_general(a, b, (dims, ((), ())), preferred_element_type=F32).astype(out)


def powers(count):
    found = []
    bit = 1
    while bit < count:
        found.append(bit)
        bit *= 2
    return found


def swap(values, axis, bit):
    count = lax.axis_size(axis)
    return lax.ppermute(values, axis, [(i, i ^ bit) for i in range(count)])


def my_bit(axis, bit):
    return (lax.axis_index(axis) // bit) % 2


def canonical():
    return [("dp", b) for b in reversed(powers(lax.axis_size("dp")))] + [
        ("expert", b) for b in reversed(powers(lax.axis_size("expert")))
    ]


def orders():
    dp_bits = powers(lax.axis_size("dp"))
    expert_bits = powers(lax.axis_size("expert"))
    core = [("dp", dp_bits[0])]
    xs = [("dp", b) for b in reversed(dp_bits[1:])]
    ys = [("expert", expert_bits[0])]
    zs = [("expert", b) for b in reversed(expert_bits[1:])]
    gathering = (zs + ys + xs + core, xs + zs + ys + core, ys + xs + zs + core)
    near = zs[::-1]
    summing = (xs + ys + near, ys + near + xs, near + xs + ys, xs + ys + near)
    return gathering, summing


def gather_steps(state, order):
    current, lead = state
    lead = list(lead)
    for axis, bit in order:
        other = swap(current, axis, bit)
        low = my_bit(axis, bit) == 0
        current = jnp.stack([jnp.where(low, current, other), jnp.where(low, other, current)])
        lead.insert(0, (axis, bit))
    return current, lead


def gather_finish(state):
    current, lead = state
    tail = current.shape[len(lead) :]
    perm = [lead.index(w) for w in canonical()]
    current = current.transpose(perm + list(range(len(lead), current.ndim)))
    return current.reshape((-1,) + tail)


def after(values, *earlier):
    if not earlier:
        return values
    return lax.optimization_barrier((values, earlier))[0]


def total(addends):
    found = addends[0].astype(F32)
    for addend in addends[1:]:
        found = found + addend.astype(F32)
    return found


def away_part(addends, lead, step):
    at = lead.index(step)
    mine = my_bit(*step)
    send = total([lax.dynamic_index_in_dim(a, 1 - mine, at, keepdims=False) for a in addends])
    return send.astype(BF)


def scatter_step(addends, lead, step):
    return swap(away_part(addends, lead, step), *step)


def scatter_rest(addends, lead, step, got):
    at = lead.index(step)
    addends = [lax.dynamic_index_in_dim(a, my_bit(*step), at, keepdims=False) for a in addends]
    return addends + [got], lead[:at] + lead[at + 1 :]


def core_swap(piece):
    return swap(piece, "dp", powers(lax.axis_size("dp"))[0])


def dp_far(shard):
    far = {}
    for bit in powers(lax.axis_size("dp"))[1:]:
        for away, piece in [(0, shard), *far.items()]:
            far[away ^ bit] = swap(piece, "dp", bit)
    return far


def dp_pieces(shard, own, far, near):
    core = powers(lax.axis_size("dp"))[0]
    found = {0: shard, core: own, **far}
    found.update({away ^ core: piece for away, piece in near.items()})
    return [found[away] for away in range(len(found))]


def x_steps():
    return [("dp", b) for b in powers(lax.axis_size("dp"))[1:]]


def scatter_dp(own, first):
    order = x_steps()
    lead = order[::-1]
    addends = [own.reshape([2] * (len(order) - 1) + list(own.shape[1:]))]
    first = first.reshape(addends[0].shape)
    addends.append(swap(first, *order[0]))
    lead.remove(order[0])
    for step in order[1:]:
        got = scatter_step(addends, lead, step)
        addends, lead = scatter_rest(addends, lead, step, got)
    return total(addends)


LIMIT = 56 * 1024 * 1024
QUERY_BLOCK = 512
SCALE = HEAD_DIM ** (-0.5)


def dot(a, b, over_a, over_b):
    return lax.dot_general(
        a, b, (((over_a,), (over_b,)), ((), ())), preferred_element_type=F32
    )


def dot_parts(values, parts):
    width = parts[0].shape[1]
    total = None
    for at, part in enumerate(parts):
        term = dot(values[:, at * width : (at + 1) * width], part, 1, 1)
        total = term if total is None else total + term
    return total


def whole(array):
    return jax.ShapeDtypeStruct(array[0], array[1])


def cost(micros):
    return pl.CostEstimate(flops=int(micros * 0.25e9), bytes_accessed=0, transcendentals=0)


def plain_call(body, outs, scratch, name, micros, *args):
    space = pl.BlockSpec(memory_space=pltpu.VMEM)
    return pl.pallas_call(
        body,
        out_shape=[whole(o) for o in outs],
        in_specs=[space] * len(args),
        out_specs=[space] * len(outs),
        scratch_shapes=scratch,
        compiler_params=pltpu.CompilerParams(vmem_limit_bytes=LIMIT),
        cost_estimate=cost(micros),
        name=name,
    )(*args)


def norm_parts(values):
    centre = values - jnp.mean(values, axis=-1, keepdims=True)
    spread = jnp.mean(centre * centre, axis=-1, keepdims=True)
    scale = lax.rsqrt(spread + 1e-05)
    return centre * scale, scale


def norm_back(values, gain, grad):
    normal, scale = norm_parts(values)
    scaled = grad * gain
    back = scale * (
        scaled
        - jnp.mean(scaled, axis=-1, keepdims=True)
        - normal * jnp.mean(scaled * normal, axis=-1, keepdims=True)
    )
    return back, jnp.sum(grad * normal, axis=0, keepdims=True), jnp.sum(grad, axis=0, keepdims=True)


def place_rows(target_ref, values, first, count):
    tokens = values.shape[0]
    at = lax.broadcasted_iota(jnp.int32, (count, tokens), 0) + first
    hit = (at == target_ref[0:1, :]) | (at == target_ref[1:2, :])
    return dot(hit.astype(F32).astype(BF), values, 1, 0).astype(BF)


def place_kernel(target_ref, values_ref, slots_ref):
    values = values_ref[...]
    part = slots_ref.shape[0] // 4
    for at in range(4):
        slots_ref[at * part : (at + 1) * part, :] = place_rows(
            target_ref, values, at * part, part
        )


def take_rows(target_ref, slots_refs, tokens):
    total = None
    first = 0
    for ref in slots_refs:
        count = ref.shape[0]
        at = lax.broadcasted_iota(jnp.int32, (tokens, count), 1) + first
        hit = (at == target_ref[:, 0:1]) | (at == target_ref[:, 1:2])
        part = dot(hit.astype(F32).astype(BF), ref[...], 1, 0)
        total = part if total is None else total + part
        first += count
    return total


def causal(size):
    rowpos = lax.broadcasted_iota(jnp.int32, (size, size), 0)
    colpos = lax.broadcasted_iota(jnp.int32, (size, size), 1)
    return rowpos >= colpos


def head_lanes(block, which):
    lane = lax.broadcasted_iota(jnp.int32, block.shape, 1)
    keep = (lane < HEAD_DIM) if which == 0 else (lane >= HEAD_DIM)
    return jnp.where(keep, block, jnp.zeros_like(block))


def block_softmax(query, keys, seen):
    size = query.shape[0]
    before = keys.shape[0] - size
    own = dot(query, keys[before:], 1, 1)
    own = jnp.where(seen, own, -1e30)
    top = jnp.max(own, axis=-1, keepdims=True)
    if before:
        past = dot(query, keys[:before], 1, 1)
        top = jnp.maximum(top, jnp.max(past, axis=-1, keepdims=True))
        past = jnp.exp(past - top)
    own = jnp.exp(own - top)
    total = jnp.sum(own, axis=-1, keepdims=True)
    if before:
        total = total + jnp.sum(past, axis=-1, keepdims=True)
    inverse = 1.0 / total
    own = own * inverse
    return (past * inverse, own) if before else (own,)


def pair_columns(pair, part, width):
    return pl.ds(pl.multiple_of(part * width + pair * 2 * HEAD_DIM, 2 * HEAD_DIM), 2 * HEAD_DIM)


def forward_kernel(
    x_ref,
    in0_ref,
    in1_ref,
    in2_ref,
    out0_ref,
    out1_ref,
    out2_ref,
    vec_ref,
    target_ref,
    normed_ref,
    proj_ref,
    context_ref,
    middle_ref,
    old_ref,
    new_ref,
):
    length, width = x_ref.shape
    x = x_ref[...].astype(F32)
    normal, _ = norm_parts(x)
    normed = (normal * vec_ref[0:1, :] + vec_ref[1:2, :]).astype(BF)
    normed_ref[...] = normed
    for part in range(3):
        cols = slice(part * width, (part + 1) * width)
        proj_ref[:, cols] = dot_parts(
            normed, [ref[cols, :] for ref in (in0_ref, in1_ref, in2_ref)]
        ).astype(BF)
    size = min(QUERY_BLOCK, length)
    seen = causal(size)

    def one_pair(pair, carry):
        q_at, k_at, v_at = (pair_columns(pair, part, width) for part in range(3))
        for block in range(length // size):
            rows = slice(block * size, (block + 1) * size)
            upto = (block + 1) * size
            query = proj_ref[rows, q_at] * BF(SCALE)
            keys = proj_ref[0:upto, k_at]
            values = proj_ref[0:upto, v_at]
            outs = []
            for which in range(2):
                probs = block_softmax(head_lanes(query, which), keys, seen)
                probs = [p.astype(BF) for p in probs]
                out = dot(probs[-1], values[upto - size :], 1, 0)
                if len(probs) > 1:
                    out = out + dot(probs[0], values[: upto - size], 1, 0)
                outs.append(out)
            lane = lax.broadcasted_iota(jnp.int32, outs[0].shape, 1)
            context_ref[rows, pair_columns(pair, 0, width)] = jnp.where(
                lane < HEAD_DIM, outs[0], outs[1]
            ).astype(BF)
        return carry

    lax.fori_loop(0, HEADS // 2, one_pair, 0)
    middle = x + dot_parts(context_ref[...], [ref[...] for ref in (out0_ref, out1_ref, out2_ref)])
    middle_ref[...] = middle
    normal, _ = norm_parts(middle)
    normed_two = (normal * vec_ref[2:3, :] + vec_ref[3:4, :]).astype(BF)
    count = old_ref.shape[0]
    half = count // 2
    for at, ref in ((0, old_ref), (count, new_ref)):
        for part in range(2):
            ref[part * half : (part + 1) * half, :] = place_rows(
                target_ref, normed_two, at + part * half, half
            )


def branch_kernel(
    old_ref,
    new_ref,
    target_ref,
    cot_ref,
    middle_ref,
    context_ref,
    out0_ref,
    out1_ref,
    out2_ref,
    vec_ref,
    gmid_ref,
    gctx_ref,
    outgrad_ref,
    sums_ref,
):
    length, width = cot_ref.shape
    grad = take_rows(target_ref, (old_ref, new_ref), length)
    back, gain_sum, bias_sum = norm_back(middle_ref[...], vec_ref[2:3, :], grad)
    gmid = back + cot_ref[...].astype(F32)
    gmid_ref[...] = gmid
    sums_ref[...] = jnp.concatenate([gain_sum, bias_sum, jnp.zeros((6, width), F32)], axis=0)
    branch = gmid.astype(BF)
    third = width // 3
    for part, ref in enumerate((out0_ref, out1_ref, out2_ref)):
        gctx_ref[:, part * third : (part + 1) * third] = dot(branch, ref[...], 1, 0).astype(BF)
    outgrad_ref[...] = dot(branch, context_ref[...], 0, 0).astype(BF)


def pairs_back(proj_ref, gctx_ref, gproj_ref, gk_acc, gv_acc):
    length, width = gctx_ref.shape
    size = min(QUERY_BLOCK, length)
    seen = causal(size)

    def one_pair(pair, carry):
        q_at, k_at, v_at = (pair_columns(pair, part, width) for part in range(3))
        gk_acc[...] = jnp.zeros_like(gk_acc)
        gv_acc[...] = jnp.zeros_like(gv_acc)
        for block in range(length // size):
            rows = slice(block * size, (block + 1) * size)
            upto = (block + 1) * size
            query = proj_ref[rows, q_at] * BF(SCALE)
            keys = proj_ref[0:upto, k_at]
            values = proj_ref[0:upto, v_at]
            gout = gctx_ref[rows, pair_columns(pair, 0, width)]
            grads = []
            for which in range(2):
                mine = head_lanes(query, which)
                gmine = head_lanes(gout, which)
                probs = block_softmax(mine, keys, seen)
                spans = [slice(upto - size, upto)]
                if len(probs) > 1:
                    spans = [slice(0, upto - size)] + spans
                gprobs = [dot(gmine, values[s], 1, 1) for s in spans]
                row = sum(jnp.sum(p * g, axis=-1, keepdims=True) for p, g in zip(probs, gprobs))
                gquery = None
                for p, g, s in zip(probs, gprobs, spans):
                    gscore = (p * (g - row)).astype(BF)
                    part = dot(gscore, keys[s], 1, 0)
                    gquery = part if gquery is None else gquery + part
                    gk_acc[s, :] += dot(gscore, mine, 0, 0)
                    gv_acc[s, :] += dot(p.astype(BF), gmine, 0, 0)
                grads.append(gquery * SCALE)
            lane = lax.broadcasted_iota(jnp.int32, grads[0].shape, 1)
            gproj_ref[rows, q_at] = jnp.where(lane < HEAD_DIM, grads[0], grads[1]).astype(BF)
        gproj_ref[:, k_at] = gk_acc[...].astype(BF)
        gproj_ref[:, v_at] = gv_acc[...].astype(BF)
        return carry

    lax.fori_loop(0, HEADS // 2, one_pair, 0)

def attention_back_kernel(
    place_ref,
    proj_ref,
    gctx_ref,
    normed_ref,
    gproj_ref,
    keep0_ref,
    keep1_ref,
    keep2_ref,
    send0_ref,
    send1_ref,
    send2_ref,
    gk_acc,
    gv_acc,
):
    width = gctx_ref.shape[1]
    pairs_back(proj_ref, gctx_ref, gproj_ref, gk_acc, gv_acc)
    third = width // 3
    core = place_ref[0] % 2
    halves, rows, _ = keep0_ref.shape
    refs = ((keep0_ref, send0_ref), (keep1_ref, send1_ref), (keep2_ref, send2_ref))
    for part, (keep_ref, send_ref) in enumerate(refs):
        grad = dot(gproj_ref[...], normed_ref[:, part * third : (part + 1) * third], 0, 0)
        grad = grad.astype(BF)
        for at in range(halves):
            first = grad[2 * at * rows : (2 * at + 1) * rows]
            second = grad[(2 * at + 1) * rows : (2 * at + 2) * rows]
            keep_ref[at] = jnp.where(core == 0, first, second)
            send_ref[at] = jnp.where(core == 0, second, first)


def input_kernel(
    gproj_ref, in0_ref, in1_ref, in2_ref, x_ref, vec_ref, gmid_ref, grad_ref, sums_ref
):
    grad = jnp.concatenate(
        [dot(gproj_ref[...], ref[...], 1, 0) for ref in (in0_ref, in1_ref, in2_ref)], axis=1
    )
    back, gain_sum, bias_sum = norm_back(x_ref[...].astype(F32), vec_ref[0:1, :], grad)
    grad_ref[...] = gmid_ref[...] + back
    width = x_ref.shape[1]
    sums_ref[...] = jnp.concatenate([gain_sum, bias_sum, jnp.zeros((6, width), F32)], axis=0)


def mixed_kernel(slots_ref, target_ref, middle_ref, mixed_ref):
    total = take_rows(target_ref, (slots_ref,), middle_ref.shape[0])
    mixed_ref[...] = (middle_ref[...] + total).astype(BF)


def gelu_pair(x):
    c = 0.7978845608028654
    sq = x * x
    t = jnp.tanh(c * x * (1.0 + 0.044715 * sq))
    half = 0.5 * (1.0 + t)
    slope = half + 0.5 * x * (1.0 - t * t) * (c * (1.0 + 3 * 0.044715 * sq))
    return x * half, slope

def expert_kernel(train, steps, pieces, place_ref, mine_ref, rows_ref, grads4_ref, router_ref, *rest):
    ups, downs, rest = rest[:pieces], rest[pieces : 2 * pieces], rest[2 * pieces :]
    if train:
        _, gated_ref, gin_ref, rgrad_ref, hid_ref, gpre_ref, scaled_ref = rest[:7]
        rest = rest[7:]
    else:
        gated_ref, gin_ref, rgrad_ref = rest[:3]
        rest = rest[3:]
    up_s, down_s, out_acc, gin_acc, scaled, gate_s, probs_s, sems = rest
    j = pl.program_id(0)
    mine = mine_ref[0:1, :]
    up_rows = up_s.shape[0] // pieces
    down_rows = down_s.shape[0] // pieces
    tile = up_s.shape[1] // steps

    def grads():
        return grads4_ref[...].reshape(rows_ref.shape).astype(F32)

    def fetches():
        found = []
        for at in range(pieces):
            owner = place_ref[at]
            to = pl.ds(pl.multiple_of(owner * up_rows, up_rows), up_rows)
            found.append(pltpu.make_async_copy(ups[at], up_s.at[to], sems.at[0, at]))
            to = pl.ds(pl.multiple_of(owner * down_rows, down_rows), down_rows)
            found.append(pltpu.make_async_copy(downs[at], down_s.at[to], sems.at[1, at]))
        return found

    @pl.when(j == 0)
    def _():
        for fetch in fetches():
            fetch.start()
        logits = dot(rows_ref[...], router_ref[...], 1, 1)
        live = lax.broadcasted_iota(jnp.int32, logits.shape, 1) < mine_ref[1, 0].astype(jnp.int32)
        logits = jnp.where(live, logits, -1e30)
        e = jnp.exp(logits - jnp.max(logits, axis=1, keepdims=True))
        probs = e / jnp.sum(e, axis=1, keepdims=True)
        probs_s[...] = probs
        gate = jnp.sum(probs * mine, axis=1, keepdims=True)
        gate_s[...] = jnp.broadcast_to(gate, gate_s.shape)
        scaled[...] = (grads() * gate).astype(BF)
        out_acc[...] = jnp.zeros_like(out_acc)
        gin_acc[...] = jnp.zeros_like(gin_acc)
        for fetch in fetches():
            fetch.wait()

    rows = rows_ref[...]
    here = pl.ds(pl.multiple_of(j * tile, tile), tile)
    up = up_s[:, here]
    down = down_s[here, :]
    hid, slope = gelu_pair(dot(rows, up, 1, 0))
    hid = hid.astype(BF)
    gpre = (dot(scaled[...], down, 1, 1) * slope).astype(BF)
    out_acc[...] += dot(hid, down, 1, 0)
    gin_acc[...] += dot(gpre, up, 1, 1)

    if train:
        hid_ref[...] = hid
        gpre_ref[...] = gpre

        @pl.when(j == 0)
        def _():
            scaled_ref[...] = scaled[...]

    @pl.when(j == steps - 1)
    def _():
        produced = out_acc[...].astype(BF).astype(F32)
        gate = gate_s[:, 0:1]
        gated_ref[...] = (produced * gate).astype(BF).reshape(gated_ref.shape)
        grad_gate = jnp.sum(produced * grads(), axis=1, keepdims=True)
        gl = (grad_gate * gate * (mine - probs_s[...])).astype(BF)
        gin_ref[...] = (gin_acc[...] + dot(gl, router_ref[...], 1, 0)).astype(BF)
        rgrad_ref[...] = dot(gl, rows_ref[...], 0, 0)


def expert_call(owners, mine, rows, grads, router_pad, ups, downs, gated=None):
    train = gated is not None
    n, d = rows.shape
    pieces = len(ups)
    f = ups[0].shape[1]
    tile = max(d, f // pieces)
    steps = f // tile
    peers, _, capacity, _ = grads.shape
    member = 1 if train else 0
    one = pl.Buffered(buffer_count=1)

    def all_of(shape):
        return pl.BlockSpec(shape, lambda j: (0,) * len(shape), pipeline_mode=one)

    slot_spec = pl.BlockSpec(
        (peers, 1, capacity, d), lambda j: (0, member, 0, 0), pipeline_mode=one
    )
    anywhere = pl.BlockSpec(memory_space=pl.ANY)
    outs = [(grads.shape, BF), ((n, d), BF), ((128, d), F32)]
    out_specs = [slot_spec, all_of((n, d)), all_of((128, d))]
    if train:
        outs += [((n, f), BF)] * 2 + [((n, d), BF)]
        out_specs += [pl.BlockSpec((n, tile), lambda j: (0, j))] * 2 + [all_of((n, d))]
    args = [owners, mine, rows, grads, router_pad, *ups, *downs] + ([gated] if train else [])
    return pl.pallas_call(
        functools.partial(expert_kernel, train, steps, pieces),
        grid=(steps,),
        in_specs=[
            pl.BlockSpec(memory_space=pltpu.SMEM),
            all_of((8, 128)),
            all_of((n, d)),
            slot_spec,
            all_of((128, d)),
        ]
        + [anywhere] * (2 * pieces + train),
        out_specs=out_specs,
        out_shape=[whole(o) for o in outs],
        scratch_shapes=[
            pltpu.VMEM((d, f), BF),
            pltpu.VMEM((f, d), BF),
            pltpu.VMEM((n, d), F32),
            pltpu.VMEM((n, d), F32),
            pltpu.VMEM((n, d), BF),
            pltpu.VMEM((n, 128), F32),
            pltpu.VMEM((n, 128), F32),
            pltpu.SemaphoreType.DMA((2, pieces)),
        ],
        input_output_aliases={len(args) - 1: 0} if train else {},
        compiler_params=pltpu.CompilerParams(vmem_limit_bytes=LIMIT),
        cost_estimate=cost(29),
        name="expert_new" if train else "expert_old",
    )(*args)


def weight_grads_kernel(
    pieces,
    place_ref,
    rows_ref,
    scaled_ref,
    hid_ref,
    gpre_ref,
    upkeep_ref,
    upsend_ref,
    downkeep_ref,
    downsend_ref,
):
    j = pl.program_id(0)
    core = place_ref[0] % 2
    half, up_rows, tile = upkeep_ref.shape
    down_rows = downkeep_ref.shape[1]
    grad_up = dot(rows_ref[...], gpre_ref[...], 0, 0).astype(BF)
    for pair in range(half):
        first = grad_up[2 * pair * up_rows : (2 * pair + 1) * up_rows]
        second = grad_up[(2 * pair + 1) * up_rows : (2 * pair + 2) * up_rows]
        upkeep_ref[pair] = jnp.where(core == 0, first, second)
        upsend_ref[pair] = jnp.where(core == 0, second, first)
    grad_down = dot(hid_ref[...], scaled_ref[...], 0, 0).astype(BF)
    inside = tile // down_rows
    for at in range(inside):
        block = grad_down[at * down_rows : (at + 1) * down_rows]
        owner = j * inside + at

        @pl.when(owner % 2 == core)
        def _():
            downkeep_ref[owner // 2] = block

        @pl.when(owner % 2 != core)
        def _():
            downsend_ref[owner // 2] = block


def weight_grads_call(owners, rows, scaled, hidden, grad_pre):
    n, d = rows.shape
    f = hidden.shape[1]
    pieces = owners.shape[0]
    half = pieces // 2
    tile = max(d, f // pieces)
    one = pl.Buffered(buffer_count=1)
    up_shape = (half, d // pieces, f)
    down_shape = (half, f // pieces, d)
    flat = pl.BlockSpec((n, d), lambda j: (0, 0), pipeline_mode=one)
    tiled = pl.BlockSpec((n, tile), lambda j: (0, j))
    return pl.pallas_call(
        functools.partial(weight_grads_kernel, pieces),
        grid=(f // tile,),
        in_specs=[pl.BlockSpec(memory_space=pltpu.SMEM), flat, flat, tiled, tiled],
        out_specs=[pl.BlockSpec((half, d // pieces, tile), lambda j: (0, 0, j))] * 2
        + [pl.BlockSpec(down_shape, lambda j: (0, 0, 0), pipeline_mode=one)] * 2,
        out_shape=[whole((up_shape, BF))] * 2 + [whole((down_shape, BF))] * 2,
        compiler_params=pltpu.CompilerParams(vmem_limit_bytes=LIMIT),
        cost_estimate=cost(1),
        name="weight_grads",
    )(owners, rows, scaled, hidden, grad_pre)


def x_parts_kernel(place_ref, keep_ref, got_ref, own_ref, away_ref):
    mine = (place_ref[0] // 2) % 2
    for at in range(own_ref.shape[0]):
        first = keep_ref[2 * at].astype(F32) + got_ref[2 * at].astype(F32)
        second = keep_ref[2 * at + 1].astype(F32) + got_ref[2 * at + 1].astype(F32)
        own_ref[at] = jnp.where(mine == 0, first, second)
        away_ref[at] = jnp.where(mine == 0, second, first).astype(BF)


def x_parts_call(owners, keep, got):
    half, rows, width = keep.shape
    tile = min(width, 768)
    grid = width // tile

    def block(count):
        return pl.BlockSpec((count, rows, tile), lambda j: (0, 0, j))

    own = (half // 2, rows, width)
    return pl.pallas_call(
        x_parts_kernel,
        grid=(grid,),
        in_specs=[pl.BlockSpec(memory_space=pltpu.SMEM), block(half), block(half)],
        out_specs=[block(half // 2)] * 2,
        out_shape=[whole((own, F32)), whole((own, BF))],
        compiler_params=pltpu.CompilerParams(vmem_limit_bytes=LIMIT),
        cost_estimate=cost(0),
        name="x_parts",
    )(owners, keep, got)


def shards(
    block_input,
    cotangent,
    attn_in,
    attn_out,
    router,
    ln1_gain,
    ln1_bias,
    ln2_gain,
    ln2_bias,
    new_w1,
    new_w2,
    old_w1,
    old_w2,
    expert_ids,
    slots,
    drops,
):
    length, width = block_input.shape
    peers = lax.axis_size("expert")
    devices = lax.axis_size("dp") * peers
    experts = 2 * peers
    capacity = max(length * 7 // (2 * experts), 2)
    me = lax.axis_index("expert")
    ways, scatter_ways = orders()
    third = width // 3
    in_share = attn_in.shape[1]
    share = width // devices

    small = jnp.concatenate(
        [v[None] for v in (ln1_gain, ln1_bias, ln2_gain, ln2_bias)] + [router.T], axis=0
    )
    lines = small.shape[0]
    small = jnp.pad(small, ((0, -lines % 8), (0, third - share)))
    in_t, out_t = attn_in.T, attn_out.T
    states = []
    for p in range(3):
        cols = slice(p * third, (p + 1) * third)
        rows = [in_t[:, cols], out_t[:, cols]] + ([small] if p == 0 else [])
        states.append((jnp.concatenate(rows, axis=0), []))
    states = [gather_steps(states[p], ways[p][:3]) for p in range(3)]
    shards_dp = [old_w1[0], old_w2[0], new_w1[0], new_w2[0]]
    early = [state[0] for state in states]
    states = [gather_steps(states[p], ways[p][3:-1]) for p in range(3)]
    between = [state[0] for state in states]
    parts = [gather_finish(gather_steps(states[p], ways[p][-1:])) for p in range(3)]
    parts = [part.reshape(devices, -1, third) for part in parts]
    in_parts = [part[:, :in_share].reshape(3 * width, third) for part in parts]
    out_parts = [part[:, in_share : in_share + share].reshape(width, third) for part in parts]
    small_full = parts[0][:, in_share + share : in_share + share + lines, :share]
    small_full = small_full.transpose(1, 0, 2).reshape(lines, width)
    vectors = jnp.pad(small_full[:4].astype(F32), ((0, 4), (0, 0)))
    router_pad = jnp.pad(small_full[4:], ((0, 128 - experts), (0, 0)))

    target = jnp.where(drops == 0, expert_ids * capacity + slots, -1)
    by_member = ((expert_ids % 2) * peers + expert_ids // 2) * capacity + slots
    by_member = jnp.where(drops == 0, by_member, -1)
    target_rows = jnp.pad(target.T, ((0, 6), (0, 0)), constant_values=-1)
    member_rows = jnp.pad(by_member.T, ((0, 6), (0, 0)), constant_values=-1)
    count = peers * capacity
    both_shape = (peers, 2, capacity, width)

    def move(block):
        return lax.all_to_all(block, "expert", split_axis=0, concat_axis=0, tiled=True)

    def send(block, *earlier):
        block = after(block, *earlier).reshape(peers, capacity, width)
        return move(block).reshape(count, width)

    (grad_slots,) = plain_call(
        place_kernel, [((2 * count, width), BF)], [], "place_grads", 4, target_rows, after(cotangent, early)
    )
    grads = move(after(grad_slots, between).reshape(both_shape))
    slot_outs = [((count, width), BF)] * 2

    normed, proj, context, middle, rold, rnew = plain_call(
        forward_kernel,
        [
            ((length, width), BF),
            ((length, 3 * width), BF),
            ((length, width), BF),
            ((length, width), F32),
        ]
        + slot_outs,
        [],
        "attention_forward", 27,
        block_input,
        *in_parts,
        *out_parts,
        vectors,
        member_rows,
    )
    owners = lax.axis_index("dp") ^ jnp.arange(lax.axis_size("dp"), dtype=jnp.int32)
    far = [dp_far(after(shard, between)) for shard in shards_dp[:2]]
    far.append(dp_far(after(shards_dp[2], between, far)))
    far.append(dp_far(after(shards_dp[3], between, far)))
    near = [{away: core_swap(piece) for away, piece in f.items()} for f in far[:3]]
    own = [core_swap(after(shard, normed)) for shard in shards_dp]
    rold = send(rold, grads, far[:2], own)
    rnew = send(rnew, rold, near)

    lane = lax.broadcasted_iota(jnp.int32, (8, 128), 1)
    line = lax.broadcasted_iota(jnp.int32, (8, 128), 0)

    def chosen(expert):
        return jnp.where(line == 0, (lane == expert).astype(F32), F32(experts))

    pieces = [dp_pieces(shards_dp[i], own[i], far[i], near[i]) for i in range(2)]
    gated, old_in, old_router = expert_call(
        owners, chosen(2 * me), rold, grads, router_pad, *pieces
    )
    near.append({away: core_swap(after(piece, old_in)) for away, piece in far[3].items()})
    pieces = [dp_pieces(shards_dp[i], own[i], far[i], near[i]) for i in range(2, 4)]
    rnew, old_in = lax.optimization_barrier((rnew, old_in))
    old_in = send(old_in, rnew)
    gated, new_in, new_router, hidden, grad_pre, scaled = expert_call(
        owners, chosen(2 * me + 1), rnew, grads, router_pad, *pieces, gated
    )
    up_keep, up_send, down_keep, down_send = weight_grads_call(
        owners, rnew, scaled, hidden, grad_pre
    )
    new_in = send(new_in, old_in)
    up_own, up_away = x_parts_call(owners, up_keep, core_swap(after(up_send, old_in)))
    down_own, down_away = x_parts_call(owners, down_keep, core_swap(after(down_send, old_in)))
    gated = move(after(gated, new_in, up_away, down_away)).reshape(2 * count, width)
    new_w1_grad = scatter_dp(up_own, up_away)[None]
    new_w2_grad = scatter_dp(down_own, down_away)[None]
    router_part = (old_router + new_router)[:experts]

    gmid, gctx, out_grad, sums_two = plain_call(
        branch_kernel,
        [
            ((length, width), F32),
            ((length, width), BF),
            ((width, width), BF),
            ((8, width), F32),
        ],
        [],
        "branch_backward",
        0,
        old_in,
        new_in,
        by_member,
        cotangent,
        middle,
        context,
        *out_parts,
        vectors,
    )
    accumulators = [pltpu.VMEM((length, 2 * HEAD_DIM), F32)] * 2
    half = lax.axis_size("dp") // 2
    gproj, *split = plain_call(
        attention_back_kernel,
        [((length, 3 * width), BF)] + [((half, 3 * width // (2 * half), third), BF)] * 6,
        accumulators,
        "attention_backward",
        0,
        owners,
        proj,
        gctx,
        normed,
    )
    input_grad, sums_one = plain_call(
        input_kernel,
        [((length, width), F32), ((8, width), F32)],
        [],
        "input_backward", 0,
        gproj,
        *in_parts,
        block_input,
        vectors,
        gmid,
    )
    lead = canonical()
    core = [("dp", powers(lax.axis_size("dp"))[0])]
    states = []
    left = [step for step in lead if step != core[0]]
    for keep, away in zip(split[:3], split[3:]):
        addends = [keep, swap(away, *core[0])]
        states.append([a.reshape([2] * len(left) + [in_share, third]) for a in addends])
    small_grads = jnp.concatenate([sums_one[:2], sums_two[:2], router_part], axis=0)
    small_grads = small_grads.reshape(lines, devices, share).transpose(1, 0, 2)
    small_grads = small_grads.reshape(devices, 1, lines * share).astype(BF)
    small_rows = -(-lines * share // width)
    small_rows += -(share + small_rows) % 8
    small_grads = jnp.pad(small_grads, ((0, 0), (0, 0), (0, small_rows * width - lines * share)))
    rest = jnp.concatenate(
        [out_grad.reshape(devices, share, width), small_grads.reshape(devices, small_rows, width)],
        axis=1,
    )
    rest = rest.reshape([2] * len(lead) + list(rest.shape[1:]))
    got = scatter_step([rest], lead, core[0])
    states.append(scatter_rest([rest], lead, core[0], got)[0])
    lefts = [left] * len(states)

    def advance(chains, step_of):
        found = {
            p: scatter_step(states[p], lefts[p], scatter_ways[p][step_of(p)]) for p in chains
        }
        for p in chains:
            step = scatter_ways[p][step_of(p)]
            states[p], lefts[p] = scatter_rest(states[p], lefts[p], step, found[p])
        return list(found.values())

    ahead = ()
    states = after(states, gated, new_w1_grad, new_w2_grad)
    for at in range(len(left)):
        chains = [p for p in range(4) if at + (p in ahead) < len(left)]
        arrived = advance(chains, lambda p: at + (p in ahead))
        if at == 0:
            (mixed,) = plain_call(
                mixed_kernel,
                [((length, width), BF)],
                [],
                "mixed_output", 5,
                after(gated, arrived),
                target,
                middle,
            )
    sums = [total(state) for state in states]
    attn_in_grad = jnp.concatenate(sums[:3], axis=1).T
    attn_out_grad = sums[3][:share].T
    small_grads = sums[3][share:].reshape(-1)[: lines * share].reshape(lines, share)
    vector_grads = small_grads[:4]
    router_grad = small_grads[4:].T
    return (
        mixed,
        input_grad,
        attn_in_grad,
        attn_out_grad,
        router_grad,
        vector_grads[0],
        vector_grads[1],
        vector_grads[2],
        vector_grads[3],
        new_w1_grad,
        new_w2_grad,
    )


def solution(mesh):
    both = ("dp", "expert")
    rows = P(both, None)
    columns = P(None, both)
    vector = P(both)
    weight = P("expert", "dp", None)
    in_specs = (
        [rows, rows, columns, columns, rows] + [vector] * 4 + [weight] * 4 + [rows] * 3
    )
    out_specs = [rows, rows, columns, columns, rows] + [vector] * 4 + [weight] * 2
    return jax.shard_map(
        shards, mesh=mesh, in_specs=tuple(in_specs), out_specs=tuple(out_specs), check_vma=False
    )
```
